32 devices in a mesh: dp: 4 (over y, core), seq: 8 (over z, x).
Axes of the slice: x: 2, y: 2, z: 4, core: 2. Of those that a mesh axis runs over, the one named last changes fastest.
Arguments:
- features: bfloat16 [4, 6144, 512], P('dp', 'seq'), may hold values from -12 to 12, as said below
- slot_kind: int32 [4, 24], P('dp', 'seq'), may hold values from 0 to 2, as said below
- block_gain: float32 [512], replicated, may hold values from 0.1 to 1.9
- block_shift: float32 [512], replicated, may hold values from -2 to 2
- block_weight: bfloat16 [4608, 512], replicated, may hold values from -0.09375 to 0.09375
- block_bias: float32 [512], replicated, may hold values from -2 to 2
- final_gain: float32 [512], replicated, may hold values from 0.1 to 1.9
- final_shift: float32 [512], replicated, may hold values from -2 to 2
- latent_weight: bfloat16 [512, 144], replicated, may hold values from -0.09375 to 0.09375
- latent_bias: float32 [16], replicated, may hold values from -2 to 2
- embed_weight: bfloat16 [64, 1152], P(None, 'dp'), may hold values from -0.75 to 0.75
- embed_bias: bfloat16 [1152], P('dp'), may hold values from -2 to 2
Outputs:
- sequence: bfloat16 [4, 1024, 1152], P('dp', 'seq')
The draws below stay inside these ranges and needn't reach their ends.
Inputs may be any that keep to these rules, and one draw needn't show every extreme that they name: `slot_kind`: the live slots of a device (kind 1 or 2) come before its empty ones. In every dp group, the live slots of the devices with seq index below d number between 2 d and 2 d + 2, and 2 * 8 over the whole group; in every group some device has 3 live slots. `features`: finite values.
All inputs are finite; a program needn't handle non-finite values.
Results may differ from the reference program's by a relative error of at most 0.014.
Values may be sent and summed in bfloat16 or wider, within the bound.
No kernel may reach another device: no remote copies, remote signals or barrier semaphores. Data moves between devices by JAX's collectives and lax.ppermute only.
A program may use at most 64 MiB of HBM per device.

```python
import jax
import jax.numpy as jnp
from jax import lax

C = 512
GROUPS = 32
LAT = 16
HID = 1152
SLOT_ROWS = 32
SLOT_COLS = 8
SLOTS = 3
CELLS = 256
TOK_SLOT = 64
TOK_SEQ = 128
FEAT = 64
N_DP = 4
N_SEQ = 8


def draw_features(key, part):
    first_key, second_key, third_key = jax.random.split(key, 3)
    base_values = jax.random.normal(first_key, (N_DP, N_SEQ * SLOTS * CELLS, C), jnp.float32)
    channel_scale = jnp.exp(jax.random.uniform(second_key, (C,), jnp.float32, -1.15, 1.15))
    cell_scale = jnp.exp(jax.random.uniform(third_key, (N_DP, N_SEQ * SLOTS * CELLS, 1), jnp.float32, -0.7, 0.7))
    values = base_values * channel_scale * cell_scale
    return jnp.clip(values, -12.0, 12.0).astype(jnp.bfloat16)


def draw_slot_kind(key, part):
    first_key, second_key, third_key = jax.random.split(key, 3)
    raw_excess = jax.random.randint(first_key, (N_DP, N_SEQ), 0, 3).astype(jnp.int32)
    busiest = jax.random.randint(second_key, (N_DP, 1), 0, N_SEQ - 1).astype(jnp.int32)
    seat = jnp.arange(N_SEQ, dtype=jnp.int32)[None, :]
    raw_excess = jnp.where(seat == busiest, 1, raw_excess)
    raw_excess = jnp.where(seat == busiest - 1, 0, raw_excess)
    raw_excess = jnp.where(seat == N_SEQ - 1, 0, raw_excess)
    lowest = lax.cummin(raw_excess - seat, axis=1)
    excess = jnp.minimum(lowest + seat, seat + 1).astype(jnp.int32)
    before = jnp.concatenate([jnp.zeros((N_DP, 1), jnp.int32), excess[:, :-1]], axis=1)
    counts = 2 + excess - before
    buckets = jax.random.randint(third_key, (N_DP, N_SEQ, SLOTS), 1, 3).astype(jnp.int32)
    live_slots = jnp.arange(SLOTS, dtype=jnp.int32)[None, None, :] < counts[:, :, None]
    return jnp.where(live_slots, buckets, 0).reshape(N_DP, N_SEQ * SLOTS).astype(jnp.int32)


def shard_levels(key, shape, shards, smallest, largest):
    factor_of, own = 1.0, jax.random.fold_in(key, 6)
    for axis_at, parts in shards:
        heights = jnp.exp(jax.random.uniform(jax.random.fold_in(own, axis_at), (parts,), jnp.float32, smallest / len(shards), largest / len(shards)))
        factor_of = factor_of * jnp.repeat(heights, shape[axis_at] // parts).reshape([-1 if axis == axis_at else 1 for axis in range(len(shape))])
    return factor_of


def noise(rng, extent, scale, limit, cuts=(), kind=jnp.bfloat16):
    result = scale * jax.random.normal(rng, extent, jnp.float32)
    if cuts:
        result = result * shard_levels(rng, extent, cuts, -0.22, 0.18)
    return jnp.clip(result, -limit, limit).astype(kind)


def setup_inputs(seed: int = 0) -> dict:
    keys = jax.random.split(jax.random.key(seed), 13)
    features = draw_features(jax.random.fold_in(keys[12], 71), 0)
    slot_kind = draw_slot_kind(jax.random.fold_in(keys[12], 71), 0)
    block_gain = jnp.clip(1.0 + 0.18 * jax.random.normal(keys[2], (C,), jnp.float32), 0.1, 1.9)
    block_shift = noise(keys[3], (C,), 0.3, 2.0, (), jnp.float32)
    block_weight = noise(keys[4], (9 * C, C), (9 * C) ** -0.5, 0.09375)
    block_bias = noise(keys[5], (C,), 0.3, 2.0, (), jnp.float32)
    final_gain = jnp.clip(1.0 + 0.18 * jax.random.normal(keys[6], (C,), jnp.float32), 0.1, 1.9)
    final_shift = noise(keys[7], (C,), 0.3, 2.0, (), jnp.float32)
    latent_weight = noise(keys[8], (C, 9 * LAT), (9 * C) ** -0.5, 0.09375)
    latent_bias = noise(keys[9], (LAT,), 0.3, 2.0, (), jnp.float32)
    embed_weight = noise(keys[10], (FEAT, HID), FEAT ** -0.5, 0.75, ((1, 4),))
    embed_bias = noise(keys[11], (HID,), 0.3, 2.0, ((0, 4),))
    return dict(features=features, slot_kind=slot_kind, block_gain=block_gain, block_shift=block_shift, block_weight=block_weight, block_bias=block_bias, final_gain=final_gain, final_shift=final_shift, latent_weight=latent_weight, latent_bias=latent_bias, embed_weight=embed_weight, embed_bias=embed_bias)


LATENT_SHIFT = 0.0609
LATENT_SCALE = 1.5305
NORM_EPSILON = 1e-06
OFFSETS = [(-1, -1), (-1, 0), (-1, 1), (0, -1), (0, 0), (0, 1), (1, -1), (1, 0), (1, 1)]

def group_norm(values, slot_types, norm_gain, norm_shift):
    slot_count, height, across, channels = values.shape
    grouped = values.reshape(slot_count, 2, height // 2, across, GROUPS, channels // GROUPS)
    joined = (slot_types == 2)[:, None, None, None, None, None]
    half_centre = lax.optimization_barrier(jnp.mean(grouped, axis=(2, 3, 5), keepdims=True))
    centre = jnp.where(joined, lax.optimization_barrier(jnp.mean(half_centre, axis=1, keepdims=True)), half_centre)
    centred = grouped - centre
    half_spread = lax.optimization_barrier(jnp.mean(centred * centred, axis=(2, 3, 5), keepdims=True))
    spread = jnp.where(joined, lax.optimization_barrier(jnp.mean(half_spread, axis=1, keepdims=True)), half_spread)
    normed = (centred * lax.rsqrt(spread + NORM_EPSILON)).reshape(values.shape)
    return normed * norm_gain.astype(jnp.float32) + norm_shift.astype(jnp.float32)

def boundary_mask(slot_types, height, row_step, out_type):
    row_index = jnp.arange(height)
    edge_row = height // 2 if row_step < 0 else height // 2 - 1
    crossing = (slot_types == 1)[:, None] & (row_index == edge_row)[None, :]
    return jnp.where(crossing, 0.0, 1.0).astype(out_type)[:, :, None, None]

def neighbour(padded, slot_types, row_step, col_step):
    height = padded.shape[1] - 2
    across = padded.shape[2] - 2
    window = padded[:, 1 + row_step:1 + row_step + height, 1 + col_step:1 + col_step + across, :]
    if row_step != 0:
        window = window * boundary_mask(slot_types, height, row_step, window.dtype)
    return window

def encode(slots, slot_types, block_gain, block_shift, block_weight, block_bias, final_gain, final_shift, latent_weight, latent_bias):
    slot_count, height, across, channels = slots.shape
    lat_width = latent_weight.shape[1] // 9
    first_act = jax.nn.silu(group_norm(slots.astype(jnp.float32), slot_types, block_gain, block_shift)).astype(jnp.bfloat16)
    padded = jnp.pad(first_act, ((0, 0), (1, 1), (1, 1), (0, 0)))
    columns = jnp.concatenate([neighbour(padded, slot_types, row_step, col_step) for row_step, col_step in OFFSETS], axis=-1)
    conv_out = jnp.dot(columns.reshape(-1, 9 * channels), block_weight, preferred_element_type=jnp.float32) + block_bias.astype(jnp.float32)
    inner = (slots.reshape(-1, channels).astype(jnp.float32) + conv_out).astype(jnp.bfloat16).reshape(slots.shape)
    second_act = jax.nn.silu(group_norm(inner.astype(jnp.float32), slot_types, final_gain, final_shift)).astype(jnp.bfloat16)
    tap_terms = jnp.dot(second_act.reshape(-1, channels), latent_weight, preferred_element_type=jnp.float32)
    tap_terms = tap_terms.reshape(slot_count, height, across, 9 * lat_width)
    padded_terms = jnp.pad(tap_terms, ((0, 0), (1, 1), (1, 1), (0, 0)))
    latent = jnp.zeros((slot_count, height, across, lat_width), jnp.float32) + latent_bias.astype(jnp.float32)
    for tap_number, (row_step, col_step) in enumerate(OFFSETS):
        piece_terms = padded_terms[..., tap_number * lat_width:(tap_number + 1) * lat_width]
        latent = latent + neighbour(piece_terms, slot_types, row_step, col_step)
    scaled = (latent - LATENT_SHIFT) * LATENT_SCALE
    patches = scaled.reshape(slot_count, height // 2, 2, across // 2, 2, lat_width).transpose(0, 1, 3, 2, 4, 5)
    return patches.reshape(slot_count * (height // 2) * (across // 2), 4 * lat_width).astype(jnp.bfloat16)

def reference(features, slot_kind, block_gain, block_shift, block_weight, block_bias, final_gain, final_shift, latent_weight, latent_bias, embed_weight, embed_bias):
    block_size = min(8, 2 * N_SEQ)

    def one_group(group_args):
        group_features, group_types = group_args
        live_slots = (group_types.reshape(N_SEQ, SLOTS) > 0).astype(jnp.int32)
        counts = lax.optimization_barrier(jnp.sum(live_slots, axis=1)).astype(jnp.int32)
        starts = (jnp.cumsum(counts) - counts).astype(jnp.int32)
        global_slot = jnp.arange(2 * N_SEQ, dtype=jnp.int32)
        owner = (lax.optimization_barrier(jnp.sum((starts[None, :] <= global_slot[:, None]).astype(jnp.int32), axis=1)) - 1).astype(jnp.int32)
        flat_index = (owner * SLOTS + global_slot - starts[owner]).astype(jnp.int32)
        chosen_types = group_types[flat_index]
        chosen = group_features.reshape(N_SEQ * SLOTS, SLOT_ROWS, SLOT_COLS, C)[flat_index]

        def encode_block(block_args):
            return encode(block_args[0], block_args[1], block_gain, block_shift, block_weight, block_bias, final_gain, final_shift, latent_weight, latent_bias)
        patches = lax.map(encode_block, (chosen.reshape(-1, block_size, SLOT_ROWS, SLOT_COLS, C), chosen_types.reshape(-1, block_size)))
        patches = patches.reshape(2 * N_SEQ * TOK_SLOT, FEAT)
        tokens = (jnp.dot(patches, embed_weight, preferred_element_type=jnp.float32) + embed_bias.astype(jnp.float32)).astype(jnp.bfloat16)
        return tokens.reshape(N_SEQ * TOK_SEQ, HID)
    return lax.map(one_group, (features, slot_kind))
```

```python
import functools
import jax
import jax.numpy as jnp
from jax import lax
from jax.sharding import PartitionSpec as P
from jax.experimental import pallas as pl
from jax.experimental.pallas import tpu as pltpu

GROUPS = 32
SLOT_ROWS = 32
SLOT_COLS = 8
LATENT_SHIFT = 0.0609
LATENT_SCALE = 1.5305
NORM_EPSILON = 1e-06
LANES = 128
VMEM_BYTES = 64 * 1024 * 1024
F32 = jnp.float32
BF16 = jnp.bfloat16


def group_total(stats, same_group):
    rows, channels = stats.shape
    chunks = channels // LANES
    packed = jnp.concatenate([stats[:, k * LANES:(k + 1) * LANES] for k in range(chunks)], axis=0)
    high = packed.astype(BF16)
    rest = packed - high.astype(F32)
    middle = rest.astype(BF16)
    low = (rest - middle.astype(F32)).astype(BF16)
    total = sum(jnp.dot(piece, same_group, preferred_element_type=F32) for piece in (high, middle, low))
    return jnp.concatenate([total[k * rows:(k + 1) * rows] for k in range(chunks)], axis=1)


def affine(stats, joined, gain, shift, same_group, count):
    total = group_total(stats, same_group)
    mean, square = total[0:2] * (1.0 / count), total[2:4] * (1.0 / count)
    both_mean = 0.5 * (mean[0:1] + mean[1:2])
    both_square = 0.5 * (square[0:1] + square[1:2])
    mean = jnp.where(joined, both_mean, mean)
    square = jnp.where(joined, both_square, square)
    spread = jnp.maximum(square - mean * mean, 0.0)
    scale = lax.rsqrt(spread + NORM_EPSILON) * (0.5 * gain)
    return scale, 0.5 * shift - mean * scale


def half_stats(half):
    total = jnp.sum(half, axis=0, keepdims=True)
    return total, jnp.sum(half * half, axis=0, keepdims=True)


def encode_slot(x_ref, joined, tables, prm, wbuf, wait_weights, lw_ref, z_ref, u_ref, y_ref):
    gain1, shift1, bias1, gain2, shift2, bias2 = prm
    same_group, perm, col_left, col_right, lane_b, lane_a = tables
    cells, channels = x_ref.shape
    half = cells // 2
    rows = cells // SLOT_COLS
    chunks = channels // LANES
    count = half * (channels // GROUPS)
    keep = jnp.where(joined, 1.0, 0.0).astype(F32)

    parts = []
    for k in range(chunks):
        x = x_ref[:, k * LANES:(k + 1) * LANES].astype(F32)
        t0, q0 = half_stats(x[:half])
        t1, q1 = half_stats(x[half:])
        parts.append(jnp.concatenate([t0, t1, q0, q1], axis=0))
    scale, offset = affine(jnp.concatenate(parts, axis=1), joined, gain1, shift1, same_group, count)
    zero = jnp.zeros((SLOT_COLS, LANES), F32)
    for k in range(chunks):
        lanes = slice(k * LANES, (k + 1) * LANES)
        x = x_ref[:, lanes].astype(F32)
        v = jnp.concatenate([x[:half] * scale[0:1, lanes] + offset[0:1, lanes],
                             x[half:] * scale[1:2, lanes] + offset[1:2, lanes]], axis=0)
        act = v + v * jnp.tanh(v)
        act3 = act.reshape(rows, SLOT_COLS, LANES)
        left = jnp.where(col_left, 0.0, pltpu.roll(act3, 1, 1)).reshape(cells, LANES)
        right = jnp.where(col_right, 0.0, pltpu.roll(act3, SLOT_COLS - 1, 1)).reshape(cells, LANES)
        for b, value in enumerate((left, act, right)):
            z_ref[b, :, lanes] = value.astype(BF16)
            over = value[half:half + SLOT_COLS] * keep
            under = value[half - SLOT_COLS:half] * keep
            u_ref[b, 0, :, lanes] = jnp.concatenate([zero, value[:half], over], axis=0).astype(BF16)
            u_ref[b, 1, :, lanes] = jnp.concatenate([under, value[half:], zero], axis=0).astype(BF16)

    conv = None
    for step, a in enumerate((0, -1, 1)):
        if a == 0:
            lhs = jnp.concatenate([z_ref[b] for b in range(3)], axis=1)
        else:
            first = 0 if a < 0 else 2 * SLOT_COLS
            lhs = jnp.concatenate(
                [jnp.concatenate([u_ref[b, h, first:first + half, :] for h in range(2)], axis=0) for b in range(3)],
                axis=1)
        wait_weights(step)
        depth = 3 * channels
        base = (a + 1) * depth
        term = jnp.dot(lhs, wbuf[base:base + depth, :], preferred_element_type=F32)
        conv = term if conv is None else conv + term

    parts = []
    for k in range(chunks):
        lanes = slice(k * LANES, (k + 1) * LANES)
        inner = (x_ref[:, lanes].astype(F32) + (conv[:, lanes] + bias1[0:1, lanes])).astype(BF16)
        y_ref[:, lanes] = inner
        inner = inner.astype(F32)
        t0, q0 = half_stats(inner[:half])
        t1, q1 = half_stats(inner[half:])
        parts.append(jnp.concatenate([t0, t1, q0, q1], axis=0))
    scale, offset = affine(jnp.concatenate(parts, axis=1), joined, gain2, shift2, same_group, count)
    for k in range(chunks):
        lanes = slice(k * LANES, (k + 1) * LANES)
        y = y_ref[:, lanes].astype(F32)
        v = jnp.concatenate([y[:half] * scale[0:1, lanes] + offset[0:1, lanes],
                             y[half:] * scale[1:2, lanes] + offset[1:2, lanes]], axis=0)
        y_ref[:, lanes] = (v + v * jnp.tanh(v)).astype(BF16)

    lat = lw_ref.shape[0] // 9
    taps = lax.dot_general(y_ref[...], lw_ref[...], (((1,), (1,)), ((), ())), preferred_element_type=F32)
    taps = jnp.concatenate([taps, jnp.zeros((cells, 2 * LANES - 9 * lat), F32)], axis=1).reshape(rows, SLOT_COLS, 2 * LANES)
    from_left = jnp.where(col_left, 0.0, pltpu.roll(taps, 1, 1))
    from_right = jnp.where(col_right, 0.0, pltpu.roll(taps, SLOT_COLS - 1, 1))
    moved = jnp.where(lane_b == 0, from_left, jnp.where(lane_b == 1, taps, from_right))
    blank = jnp.zeros((1, SLOT_COLS, 2 * LANES), F32)
    mid = rows // 2
    above = jnp.concatenate([blank, moved[:mid - 1], moved[mid - 1:mid] * keep, moved[mid:rows - 1]], axis=0)
    below = jnp.concatenate([moved[1:mid], moved[mid:mid + 1] * keep, moved[mid + 1:], blank], axis=0)
    moved = jnp.where(lane_a == 0, above, jnp.where(lane_a == 1, moved, below)).reshape(cells, 2 * LANES)
    folded = moved[:, :LANES]
    width = LANES // 2
    while width >= lat:
        folded = folded + pltpu.roll(folded, width, 1)
        width //= 2
    latent = (folded + moved[:, LANES:])[:, :lat]
    latent = ((latent + bias2) - LATENT_SHIFT) * LATENT_SCALE
    spread = jnp.dot(perm, latent.astype(BF16), preferred_element_type=F32)
    tokens = cells // 4
    return jnp.concatenate([spread[k * tokens:(k + 1) * tokens] for k in range(4)], axis=1).astype(BF16)


def make_tables(cells, channels, lat):
    width = channels // GROUPS
    r = lax.broadcasted_iota(jnp.int32, (LANES, LANES), 0) // width
    c = lax.broadcasted_iota(jnp.int32, (LANES, LANES), 1) // width
    same_group = jnp.where(r == c, 1.0, 0.0).astype(BF16)
    tokens = cells // 4
    half_cols = SLOT_COLS // 2
    row = lax.broadcasted_iota(jnp.int32, (cells, cells), 0)
    col = lax.broadcasted_iota(jnp.int32, (cells, cells), 1)
    block, token = row // tokens, row % tokens
    cell = (2 * (token // half_cols) + block // 2) * SLOT_COLS + 2 * (token % half_cols) + block % 2
    perm = jnp.where(cell == col, 1.0, 0.0).astype(BF16)
    sub = lax.broadcasted_iota(jnp.int32, (1, SLOT_COLS, 1), 1)
    lane = lax.broadcasted_iota(jnp.int32, (1, 1, 2 * LANES), 2)
    return same_group, perm, sub == 0, sub == SLOT_COLS - 1, (lane // lat) % 3, lane // (3 * lat)


def encode_kernel(ends, pack, kind_hbm, feat_ref, bw_ref, *rest):
    names = 7
    small_hbm, rest = rest[:names], rest[names:]
    if pack:
        ew_hbm, eb_hbm, out_ref, piece_ref, *rest = rest
    else:
        out_ref, *rest = rest
    kind_ref, xbuf, wbuf, z_ref, u_ref, y_ref, *rest = rest
    small, rest = rest[:names], rest[names:]
    if pack:
        ew_ref, eb_ref, *rest = rest
    ksem, xsem, wsem, ssem = rest
    slots = kind_ref.shape[1]
    cells, channels = xbuf.shape[1:]
    kcopy = pltpu.make_async_copy(kind_hbm, kind_ref, ksem)
    kcopy.start()
    xcopies = [pltpu.make_async_copy(feat_ref.at[0, pl.ds(s * cells, cells), :], xbuf.at[s], xsem.at[s])
               for s in range(slots)]
    depth = 3 * channels
    wcopies = [pltpu.make_async_copy(
        bw_ref.at[pl.ds((a + 1) * depth, depth), :], wbuf.at[pl.ds((a + 1) * depth, depth), :], wsem.at[i])
        for i, a in enumerate((0, -1, 1))]
    scopies = [pltpu.make_async_copy(src, dst, ssem.at[i]) for i, (src, dst) in enumerate(zip(small_hbm, small))]
    if pack:
        scopies += [pltpu.make_async_copy(ew_hbm, ew_ref, ssem.at[names]),
                    pltpu.make_async_copy(eb_hbm, eb_ref, ssem.at[names + 1])]
    for c in xcopies + scopies + wcopies:
        c.start()
    g1_ref, s1_ref, b1_ref, g2_ref, s2_ref, lw_ref, b2_ref = small
    lat = lw_ref.shape[0] // 9
    tables = make_tables(cells, channels, lat)
    kcopy.wait()
    live = jnp.int32(0)
    for s in range(slots):
        live = live + jnp.where(kind_ref[0, s] > 0, 1, 0).astype(jnp.int32)
    for c in scopies + xcopies:
        c.wait()
    row = lambda ref: ref[...].reshape(1, ref.shape[0])
    prm = (row(g1_ref), row(s1_ref), row(b1_ref), row(g2_ref), row(s2_ref), row(b2_ref))
    if pack:
        feats = ew_ref.shape[0]
        piece_ref[0:feats, :] = ew_ref[...]
        piece_ref[feats:, :] = jnp.broadcast_to(row(eb_ref), (piece_ref.shape[0] - feats, ew_ref.shape[1]))
    for k, end in enumerate(ends):
        slot = jnp.maximum(live - 1 - end, 0)
        wait = (lambda step: wcopies[step].wait()) if k == 0 else (lambda step: None)
        joined = kind_ref[0, slot] == 2
        out_ref[k] = encode_slot(xbuf.at[slot], joined, tables, prm, wbuf, wait, lw_ref, z_ref, u_ref, y_ref)


def encode(ends, features, slot_kind, block_gain, block_shift, block_weight, block_bias, final_gain, final_shift,
           latent_weight, latent_bias, embed=None):
    slots = slot_kind.shape[1]
    channels = features.shape[2]
    cells = SLOT_ROWS * SLOT_COLS
    lat = latent_weight.shape[1] // 9
    vmem = pl.BlockSpec(memory_space=pltpu.VMEM)
    hbm = pl.BlockSpec(memory_space=pltpu.HBM)
    n = len(ends)
    pack = embed is not None
    small = (block_gain, block_shift, block_bias, final_gain, final_shift, latent_weight.T, latent_bias)
    extra = tuple(embed) if pack else ()
    flops = n * cells * channels * 2 * (9 * channels + 9 * lat)
    outs = [jax.ShapeDtypeStruct((n, cells // 4, 4 * lat), BF16)]
    if pack:
        feats, width = embed[0].shape
        outs.append(jax.ShapeDtypeStruct((feats + 16, width), BF16))
    return pl.pallas_call(
        functools.partial(encode_kernel, ends, pack),
        out_shape=outs,
        in_specs=[hbm] * (3 + len(small) + len(extra)),
        out_specs=[vmem] * len(outs),
        scratch_shapes=[
            pltpu.SMEM(slot_kind.shape, jnp.int32),
            pltpu.VMEM((slots, cells, channels), BF16),
            pltpu.VMEM((9 * channels, channels), BF16),
            pltpu.VMEM((3, cells, channels), BF16),
            pltpu.VMEM((3, 2, cells // 2 + 2 * SLOT_COLS, channels), BF16),
            pltpu.VMEM((cells, channels), BF16),
        ] + [pltpu.VMEM(v.shape, v.dtype) for v in small + extra] + [
            pltpu.SemaphoreType.DMA,
            pltpu.SemaphoreType.DMA((slots,)),
            pltpu.SemaphoreType.DMA((3,)),
            pltpu.SemaphoreType.DMA((len(small + extra),)),
        ],
        compiler_params=pltpu.CompilerParams(vmem_limit_bytes=VMEM_BYTES),
        cost_estimate=pl.CostEstimate(flops=flops, bytes_accessed=9 * channels * channels * 2, transcendentals=0),
        name="encode_" + "_".join(map(str, ends)),
    )(slot_kind, features, block_weight, *small, *extra)


def join_kernel(parts, info_ref, own_ref, third_ref, even_ref, odd_ref, *rest):
    pieces, out_ref, embed_ref, source_ref = rest[:parts], *rest[parts:]
    carry, live, odd, group = (info_ref[k] for k in range(4))
    feats = pieces[0].shape[0] - 16
    width = pieces[0].shape[1]
    for j in range(parts):
        value = pieces[0][...]
        for k in range(1, parts):
            value = jnp.where((group ^ j) == k, pieces[k][...], value)
        embed_ref[:, j * width:(j + 1) * width] = value
    source_ref[0:2] = even_ref[...]
    source_ref[2:4] = odd_ref[...]
    source_ref[4:6] = own_ref[...]
    source_ref[6:7] = third_ref[...]
    tokens = own_ref.shape[1]
    weight = embed_ref[0:feats, :]
    bias = embed_ref[feats:feats + 1, :].astype(F32)
    for i in range(2):
        incoming = (1 - odd) * 2 + carry - 1 - i
        kept = 4 + live - 1 - (i - carry)
        patch = source_ref[jnp.clip(jnp.where(i < carry, incoming, kept), 0, 6)]
        value = jnp.dot(patch, weight, preferred_element_type=F32) + bias
        out_ref[0, i * tokens:(i + 1) * tokens, :] = value.astype(BF16)


def join(info, own, third, even, odd, pieces):
    parts = len(pieces)
    tall, width = pieces[0].shape
    vmem = pl.BlockSpec(memory_space=pltpu.VMEM)
    smem = pl.BlockSpec(memory_space=pltpu.SMEM)
    _, tokens, feats = own.shape
    return pl.pallas_call(
        functools.partial(join_kernel, parts),
        out_shape=jax.ShapeDtypeStruct((1, 2 * tokens, parts * width), BF16),
        in_specs=[smem] + [vmem] * (4 + parts),
        out_specs=vmem,
        scratch_shapes=[pltpu.VMEM((tall, parts * width), BF16), pltpu.VMEM((7, tokens, feats), BF16)],
        compiler_params=pltpu.CompilerParams(vmem_limit_bytes=8 * 1024 * 1024),
        cost_estimate=pl.CostEstimate(flops=4 * tokens * feats * parts * width, bytes_accessed=4 * tokens * parts * width,
                                      transcendentals=0),
        name="join",
    )(info, own, third, even, odd, *pieces)


def exchange(value, axis, offset):
    count = lax.axis_size(axis)
    return lax.ppermute(value, axis, [(i, i ^ offset) for i in range(count)])


def swap_odd_pairs(value, axis):
    count = lax.axis_size(axis)
    pairs = [(0, 0), (count - 1, count - 1)]
    for i in range(1, count - 1, 2):
        pairs += [(i, i + 1), (i + 1, i)]
    return lax.ppermute(value, axis, pairs)


def live_excess(kinds):
    return jnp.sum((kinds > 0).astype(jnp.int32)) - 2


def local(features, slot_kind, block_gain, block_shift, block_weight, block_bias, final_gain, final_shift,
          latent_weight, latent_bias, embed_weight, embed_bias):
    seq, dp = lax.axis_size("seq"), lax.axis_size("dp")
    position, group = lax.axis_index("seq"), lax.axis_index("dp")
    net = (features, slot_kind, block_gain, block_shift, block_weight, block_bias, final_gain, final_shift,
           latent_weight, latent_bias)
    excess = live_excess(slot_kind)
    below = jnp.int32(0)
    for offset in range(2, seq, 2):
        other = live_excess(exchange(slot_kind, "seq", offset))
        below = below + jnp.where((position ^ offset) < position, other, 0)
    own, piece = encode((0, 1), *net, embed=(embed_weight, embed_bias))
    sums = exchange(jnp.stack([below, below + excess]), "seq", 1)
    even = exchange(own, "seq", 1)
    odd = swap_odd_pairs(own, "seq")
    pieces = [piece] + [exchange(piece, "dp", offset) for offset in range(1, dp)]
    third, = encode((2,), *net)
    is_odd = position % 2
    carry = below + jnp.where(is_odd == 1, sums[1], sums[0])
    info = jnp.stack([carry, excess + 2, is_odd, group])
    return join(info, own, third, even, odd, pieces)


def solution(mesh):
    in_specs = (P("dp", "seq", None), P("dp", "seq")) + (P(),) * 8 + (P(None, "dp"), P("dp"))
    return jax.shard_map(local, mesh=mesh, in_specs=in_specs, out_specs=P("dp", "seq", None), check_vma=False)
```

```python
import functools
import jax
import jax.numpy as jnp
from jax import lax
from jax.sharding import PartitionSpec as P
from jax.experimental import pallas as pl
from jax.experimental.pallas import tpu as pltpu

GROUPS = 32
SLOT_ROWS = 32
SLOT_COLS = 8
LATENT_SHIFT = 0.0609
LATENT_SCALE = 1.5305
NORM_EPSILON = 1e-06
LANES = 128
VMEM_BYTES = 64 * 1024 * 1024
F32 = jnp.float32
BF16 = jnp.bfloat16


def group_total(stats, same_group):
    rows, channels = stats.shape
    chunks = channels // LANES
    packed = jnp.concatenate([stats[:, k * LANES:(k + 1) * LANES] for k in range(chunks)], axis=0)
    high = packed.astype(BF16)
    rest = packed - high.astype(F32)
    middle = rest.astype(BF16)
    low = (rest - middle.astype(F32)).astype(BF16)
    total = sum(jnp.dot(piece, same_group, preferred_element_type=F32) for piece in (high, middle, low))
    return jnp.concatenate([total[k * rows:(k + 1) * rows] for k in range(chunks)], axis=1)


def affine(stats, joined, gain, shift, same_group, count):
    total = group_total(stats, same_group)
    mean, square = total[0:2] * (1.0 / count), total[2:4] * (1.0 / count)
    both_mean = 0.5 * (mean[0:1] + mean[1:2])
    both_square = 0.5 * (square[0:1] + square[1:2])
    mean = jnp.where(joined, both_mean, mean)
    square = jnp.where(joined, both_square, square)
    spread = jnp.maximum(square - mean * mean, 0.0)
    scale = lax.rsqrt(spread + NORM_EPSILON) * (0.5 * gain)
    return scale, 0.5 * shift - mean * scale


def half_stats(half):
    total = jnp.sum(half, axis=0, keepdims=True)
    return total, jnp.sum(half * half, axis=0, keepdims=True)


def norm_first(x_ref, joined, gain, shift, same_group, z_ref, u_ref):
    cells, channels = x_ref.shape
    half = cells // 2
    rows = cells // SLOT_COLS
    chunks = channels // LANES
    count = half * (channels // GROUPS)
    keep = jnp.where(joined, 1.0, 0.0).astype(F32)
    column = lax.broadcasted_iota(jnp.int32, (1, SLOT_COLS, 1), 1)
    parts = []
    for k in range(chunks):
        x = x_ref[:, k * LANES:(k + 1) * LANES].astype(F32)
        t0, q0 = half_stats(x[:half])
        t1, q1 = half_stats(x[half:])
        parts.append(jnp.concatenate([t0, t1, q0, q1], axis=0))
    scale, offset = affine(jnp.concatenate(parts, axis=1), joined, gain, shift, same_group, count)
    zero = jnp.zeros((SLOT_COLS, LANES), F32)
    for k in range(chunks):
        lanes = slice(k * LANES, (k + 1) * LANES)
        x = x_ref[:, lanes].astype(F32)
        v = jnp.concatenate([x[:half] * scale[0:1, lanes] + offset[0:1, lanes],
                             x[half:] * scale[1:2, lanes] + offset[1:2, lanes]], axis=0)
        act = v + v * jnp.tanh(v)
        act3 = act.reshape(rows, SLOT_COLS, LANES)
        left = jnp.where(column == 0, 0.0, pltpu.roll(act3, 1, 1)).reshape(cells, LANES)
        right = jnp.where(column == SLOT_COLS - 1, 0.0, pltpu.roll(act3, SLOT_COLS - 1, 1)).reshape(cells, LANES)
        for b, value in enumerate((left, act, right)):
            z_ref[b, :, lanes] = value.astype(BF16)
            over = value[half:half + SLOT_COLS] * keep
            under = value[half - SLOT_COLS:half] * keep
            u_ref[b, 0, :, lanes] = jnp.concatenate([zero, value[:half], over], axis=0).astype(BF16)
            u_ref[b, 1, :, lanes] = jnp.concatenate([under, value[half:], zero], axis=0).astype(BF16)


def conv(x_ref, bias, wbuf, wait_weights, z_ref, u_ref, y_ref):
    cells, channels = x_ref.shape
    half = cells // 2
    total = None
    for step, a in enumerate((0, -1, 1)):
        if a == 0:
            lhs = jnp.concatenate([z_ref[b] for b in range(3)], axis=1)
        else:
            first = 0 if a < 0 else 2 * SLOT_COLS
            lhs = jnp.concatenate(
                [jnp.concatenate([u_ref[b, h, first:first + half, :] for h in range(2)], axis=0) for b in range(3)],
                axis=1)
        wait_weights(step)
        depth = 3 * channels
        base = (a + 1) * depth
        term = jnp.dot(lhs, wbuf[base:base + depth, :], preferred_element_type=F32)
        total = term if total is None else total + term
    y_ref[...] = (x_ref[...].astype(F32) + (total + bias)).astype(BF16)


def norm_second(y_ref, joined, gain, shift, same_group):
    cells, channels = y_ref.shape
    half = cells // 2
    chunks = channels // LANES
    count = half * (channels // GROUPS)
    parts = []
    for k in range(chunks):
        lanes = slice(k * LANES, (k + 1) * LANES)
        inner = y_ref[:, lanes].astype(F32)
        t0, q0 = half_stats(inner[:half])
        t1, q1 = half_stats(inner[half:])
        parts.append(jnp.concatenate([t0, t1, q0, q1], axis=0))
    scale, offset = affine(jnp.concatenate(parts, axis=1), joined, gain, shift, same_group, count)
    for k in range(chunks):
        lanes = slice(k * LANES, (k + 1) * LANES)
        y = y_ref[:, lanes].astype(F32)
        v = jnp.concatenate([y[:half] * scale[0:1, lanes] + offset[0:1, lanes],
                             y[half:] * scale[1:2, lanes] + offset[1:2, lanes]], axis=0)
        y_ref[:, lanes] = (v + v * jnp.tanh(v)).astype(BF16)


def to_patches(y_ref, joined, lw_ref, bias, perm):
    cells, channels = y_ref.shape
    rows = cells // SLOT_COLS
    keep = jnp.where(joined, 1.0, 0.0).astype(F32)
    column = lax.broadcasted_iota(jnp.int32, (1, SLOT_COLS, 1), 1)
    lane = lax.broadcasted_iota(jnp.int32, (1, 1, 2 * LANES), 2)
    lat = lw_ref.shape[0] // 9
    lane_a, lane_b = lane // (3 * lat), (lane // lat) % 3
    taps = lax.dot_general(y_ref[...], lw_ref[...], (((1,), (1,)), ((), ())), preferred_element_type=F32)
    taps = jnp.concatenate([taps, jnp.zeros((cells, 2 * LANES - 9 * lat), F32)], axis=1).reshape(rows, SLOT_COLS, 2 * LANES)
    from_left = jnp.where(column == 0, 0.0, pltpu.roll(taps, 1, 1))
    from_right = jnp.where(column == SLOT_COLS - 1, 0.0, pltpu.roll(taps, SLOT_COLS - 1, 1))
    moved = jnp.where(lane_b == 0, from_left, jnp.where(lane_b == 1, taps, from_right))
    blank = jnp.zeros((1, SLOT_COLS, 2 * LANES), F32)
    mid = rows // 2
    above = jnp.concatenate([blank, moved[:mid - 1], moved[mid - 1:mid] * keep, moved[mid:rows - 1]], axis=0)
    below = jnp.concatenate([moved[1:mid], moved[mid:mid + 1] * keep, moved[mid + 1:], blank], axis=0)
    moved = jnp.where(lane_a == 0, above, jnp.where(lane_a == 1, moved, below)).reshape(cells, 2 * LANES)
    folded = moved[:, :LANES]
    width = LANES // 2
    while width >= lat:
        folded = folded + pltpu.roll(folded, width, 1)
        width //= 2
    latent = (folded + moved[:, LANES:])[:, :lat]
    latent = ((latent + bias) - LATENT_SHIFT) * LATENT_SCALE
    spread = jnp.dot(perm, latent.astype(BF16), preferred_element_type=F32)
    tokens = cells // 4
    return jnp.concatenate([spread[k * tokens:(k + 1) * tokens] for k in range(4)], axis=1).astype(BF16)


def group_table(channels):
    width = channels // GROUPS
    r = lax.broadcasted_iota(jnp.int32, (LANES, LANES), 0) // width
    c = lax.broadcasted_iota(jnp.int32, (LANES, LANES), 1) // width
    return jnp.where(r == c, 1.0, 0.0).astype(BF16)


def patch_table(cells):
    tokens = cells // 4
    half_cols = SLOT_COLS // 2
    row = lax.broadcasted_iota(jnp.int32, (cells, cells), 0)
    col = lax.broadcasted_iota(jnp.int32, (cells, cells), 1)
    block, token = row // tokens, row % tokens
    cell = (2 * (token // half_cols) + block // 2) * SLOT_COLS + 2 * (token % half_cols) + block % 2
    return jnp.where(cell == col, 1.0, 0.0).astype(BF16)


ENDS = 3


def vector(ref):
    return ref[...].reshape(1, ref.shape[0])


def begin_kernel(kind_hbm, feat_hbm, bw_hbm, ew_hbm, eb_hbm, *rest):
    names = 7
    small_hbm, rest = rest[:names], rest[names:]
    state_ref, x_ref, w_ref, perm_ref, piece_ref, out_ref, *rest = rest
    small, rest = rest[:names], rest[names:]
    kind_ref, ew_ref, eb_ref, z_ref, u_ref, y_ref, ksem, xsem, wsem, ssem = rest
    gain1, shift1, bias1, gain2, shift2, lw_ref, bias2 = small
    slots, cells, channels = x_ref.shape
    kcopy = pltpu.make_async_copy(kind_hbm, kind_ref, ksem)
    kcopy.start()
    xcopies = [pltpu.make_async_copy(feat_hbm.at[0, pl.ds(s * cells, cells), :], x_ref.at[s], xsem.at[s])
               for s in range(slots)]
    depth = 3 * channels
    wcopies = [pltpu.make_async_copy(
        bw_hbm.at[pl.ds((a + 1) * depth, depth), :], w_ref.at[pl.ds((a + 1) * depth, depth), :], wsem.at[i])
        for i, a in enumerate((0, -1, 1))]
    scopies = [pltpu.make_async_copy(src, dst, ssem.at[i])
               for i, (src, dst) in enumerate(zip(small_hbm + (ew_hbm, eb_hbm), small + [ew_ref, eb_ref]))]
    for c in xcopies + scopies + wcopies:
        c.start()
    perm_ref[...] = patch_table(cells)
    same_group = group_table(channels)
    kcopy.wait()
    live = jnp.int32(0)
    for s in range(slots):
        live = live + jnp.where(kind_ref[0, s] > 0, 1, 0).astype(jnp.int32)
    state_ref[0] = live
    for end in range(ENDS):
        slot = jnp.maximum(live - 1 - end, 0)
        state_ref[1 + end] = slot
        state_ref[1 + ENDS + end] = kind_ref[0, slot]
    for c in scopies + xcopies:
        c.wait()
    feats = ew_ref.shape[0]
    piece_ref[0:feats, :] = ew_ref[...]
    piece_ref[feats:, :] = jnp.broadcast_to(vector(eb_ref), (piece_ref.shape[0] - feats, ew_ref.shape[1]))
    x = x_ref.at[state_ref[1]]
    joined = state_ref[1 + ENDS] == 2
    norm_first(x, joined, vector(gain1), vector(shift1), same_group, z_ref, u_ref)
    conv(x, vector(bias1), w_ref, lambda step: wcopies[step].wait(), z_ref, u_ref, y_ref)
    norm_second(y_ref, joined, vector(gain2), vector(shift2), same_group)
    out_ref[...] = to_patches(y_ref, joined, lw_ref, vector(bias2), perm_ref[...])


def encode_end(end, state_ref, x_ref, w_ref, perm_ref, small, scratch):
    gain1, shift1, bias1, gain2, shift2, lw_ref, bias2 = small
    z_ref, u_ref, y_ref = scratch
    same_group = group_table(x_ref.shape[2])
    x = x_ref.at[state_ref[1 + end]]
    joined = state_ref[1 + ENDS + end] == 2
    norm_first(x, joined, vector(gain1), vector(shift1), same_group, z_ref, u_ref)
    conv(x, vector(bias1), w_ref, lambda step: None, z_ref, u_ref, y_ref)
    norm_second(y_ref, joined, vector(gain2), vector(shift2), same_group)
    return to_patches(y_ref, joined, lw_ref, vector(bias2), perm_ref[...])


def count_live(kind_ref):
    total = jnp.int32(-2)
    for s in range(kind_ref.shape[1]):
        total = total + jnp.where(kind_ref[0, s] > 0, 1, 0).astype(jnp.int32)
    return total


def middle_kernel(offsets, state_ref, x_ref, w_ref, perm_ref, last_ref, *rest):
    names = 7
    small, rest = rest[:names], rest[names:]
    others, rest = rest[:len(offsets)], rest[len(offsets):]
    message_ref, sums_ref, *rest = rest
    scratch, rest = rest[:3], rest[3:]
    kinds, ksem = rest[:-1], rest[-1]
    copies = [pltpu.make_async_copy(src, dst, ksem.at[i]) for i, (src, dst) in enumerate(zip(others, kinds))]
    for c in copies:
        c.start()
    tokens, feats = last_ref.shape
    message_ref[0:tokens, :] = last_ref[...]
    message_ref[tokens:2 * tokens, :] = encode_end(1, state_ref, x_ref, w_ref, perm_ref, small, scratch)
    for c in copies:
        c.wait()
    position = lax.axis_index("seq")
    mine = state_ref[0] - 2
    below, above = jnp.int32(0), mine
    for offset, kind_ref in zip(offsets, kinds):
        other = count_live(kind_ref)
        lower = (position ^ offset) < position
        below = below + jnp.where(lower, other, 0)
        above = above + jnp.where(lower, 0, other)
    first_half = position < lax.axis_size("seq") // 2
    passed = jnp.where(position % 2 == 0, mine, 0)
    sums_ref[0] = jnp.where(first_half, below, -above)
    told = jnp.where(first_half, below + passed, passed - above)
    message_ref[2 * tokens:, :] = jnp.full((message_ref.shape[0] - 2 * tokens, feats), told.astype(F32)).astype(BF16)


def final_kernel(state_ref, x_ref, w_ref, perm_ref, *rest):
    small, rest = rest[:7], rest[7:]
    out_ref, *scratch = rest

    @pl.when(state_ref[0] > 2)
    def _():
        out_ref[...] = encode_end(2, state_ref, x_ref, w_ref, perm_ref, small, scratch)

    @pl.when(state_ref[0] <= 2)
    def _():
        out_ref[...] = jnp.zeros_like(out_ref)


def join_kernel(parts, state_ref, sums_ref, own_ref, third_ref, even_ref, odd_ref, *rest):
    pieces, out_ref, embed_ref, source_ref = rest[:parts], *rest[parts:]
    live = state_ref[0]
    group, position = lax.axis_index("dp"), lax.axis_index("seq")
    odd = position % 2
    tokens, feats = third_ref.shape
    width = pieces[0].shape[1]
    told = even_ref[2 * tokens:, :].astype(F32)[0, 0].astype(jnp.int32)
    carry = sums_ref[0] + told
    for j in range(parts):
        value = pieces[0][...]
        for k in range(1, parts):
            value = jnp.where((group ^ j) == k, pieces[k][...], value)
        embed_ref[:, j * width:(j + 1) * width] = value
    for k, ref in enumerate((even_ref, odd_ref, own_ref)):
        source_ref[2 * k] = ref[0:tokens, :]
        source_ref[2 * k + 1] = ref[tokens:2 * tokens, :]
    source_ref[6] = third_ref[...]
    weight = embed_ref[0:feats, :]
    bias = embed_ref[feats:feats + 1, :].astype(F32)
    for i in range(2):
        incoming = (1 - odd) * 2 + carry - 1 - i
        kept = 4 + live - 1 - (i - carry)
        patch = source_ref[jnp.clip(jnp.where(i < carry, incoming, kept), 0, 6)]
        value = jnp.dot(patch, weight, preferred_element_type=F32) + bias
        out_ref[0, i * tokens:(i + 1) * tokens, :] = value.astype(BF16)


def exchange(value, axis, offset):
    count = lax.axis_size(axis)
    return lax.ppermute(value, axis, [(i, i ^ offset) for i in range(count)])


def swap_odd_pairs(value, axis):
    count = lax.axis_size(axis)
    pairs = [(0, 0), (count - 1, count - 1)]
    for i in range(1, count - 1, 2):
        pairs += [(i, i + 1), (i + 1, i)]
    return lax.ppermute(value, axis, pairs)


VMEM_SPEC = pl.BlockSpec(memory_space=pltpu.VMEM)
SMEM_SPEC = pl.BlockSpec(memory_space=pltpu.SMEM)
ANY_SPEC = pl.BlockSpec(memory_space=pl.ANY)
MIB = 1024 * 1024


def cost(flops, moved):
    return pl.CostEstimate(flops=flops, bytes_accessed=moved, transcendentals=0)


def local(features, slot_kind, block_gain, block_shift, block_weight, block_bias, final_gain, final_shift,
          latent_weight, latent_bias, embed_weight, embed_bias):
    seq, dp = lax.axis_size("seq"), lax.axis_size("dp")
    slots = slot_kind.shape[1]
    channels = features.shape[2]
    cells = SLOT_ROWS * SLOT_COLS
    tokens = cells // 4
    feats, width = embed_weight.shape
    small = (block_gain, block_shift, block_bias, final_gain, final_shift, latent_weight.T, latent_bias)
    offsets = tuple(range(2, seq // 2, 2))
    others = [exchange(slot_kind, "seq", offset) for offset in offsets]
    buffers = [
        pltpu.VMEM((3, cells, channels), BF16),
        pltpu.VMEM((3, 2, cells // 2 + 2 * SLOT_COLS, channels), BF16),
        pltpu.VMEM((cells, channels), BF16),
    ]
    flops = cells * channels * 2 * 9 * (channels + latent_weight.shape[1] // 9)
    state, x, w, perm, piece, last, *small = pl.pallas_call(
        begin_kernel,
        out_shape=[
            pltpu.SMEM((8,), jnp.int32),
            pltpu.VMEM((slots, cells, channels), BF16),
            pltpu.VMEM(block_weight.shape, BF16),
            pltpu.VMEM((cells, cells), BF16),
            jax.ShapeDtypeStruct((feats + 16, width), BF16),
            pltpu.VMEM((tokens, feats), BF16),
        ] + [pltpu.VMEM(v.shape, v.dtype) for v in small],
        in_specs=[ANY_SPEC] * (5 + len(small)),
        out_specs=[SMEM_SPEC] + [VMEM_SPEC] * (5 + len(small)),
        scratch_shapes=[
            pltpu.SMEM(slot_kind.shape, jnp.int32),
            pltpu.VMEM(embed_weight.shape, BF16),
            pltpu.VMEM(embed_bias.shape, BF16),
        ] + buffers + [
            pltpu.SemaphoreType.DMA,
            pltpu.SemaphoreType.DMA((slots,)),
            pltpu.SemaphoreType.DMA((3,)),
            pltpu.SemaphoreType.DMA((len(small) + 2,)),
        ],
        compiler_params=pltpu.CompilerParams(vmem_limit_bytes=55 * MIB),
        cost_estimate=cost(flops, block_weight.size * 2),
        name="begin",
    )(slot_kind, features, block_weight, embed_weight, embed_bias, *small)
    message, sums = pl.pallas_call(
        functools.partial(middle_kernel, offsets),
        out_shape=[jax.ShapeDtypeStruct((2 * tokens + 16, feats), BF16), pltpu.SMEM((1,), jnp.int32)],
        in_specs=[SMEM_SPEC] + [VMEM_SPEC] * (4 + len(small)) + [ANY_SPEC] * len(others),
        out_specs=[VMEM_SPEC, SMEM_SPEC],
        scratch_shapes=buffers + [pltpu.SMEM(slot_kind.shape, jnp.int32) for _ in others]
        + [pltpu.SemaphoreType.DMA((len(others),))],
        compiler_params=pltpu.CompilerParams(vmem_limit_bytes=24 * MIB),
        cost_estimate=cost(flops, block_weight.size * 2),
        name="middle",
    )(state, x, w, perm, last, *small, *others)
    even = exchange(message, "seq", 1)
    odd = swap_odd_pairs(message, "seq")
    pieces = [piece] + [exchange(piece, "dp", offset) for offset in range(1, dp)]
    third = pl.pallas_call(
        final_kernel,
        out_shape=pltpu.VMEM((tokens, feats), BF16),
        in_specs=[SMEM_SPEC] + [VMEM_SPEC] * (3 + len(small)),
        out_specs=VMEM_SPEC,
        scratch_shapes=buffers,
        compiler_params=pltpu.CompilerParams(vmem_limit_bytes=24 * MIB),
        cost_estimate=cost(flops, block_weight.size * 2),
        name="final",
    )(state, x, w, perm, *small)
    return pl.pallas_call(
        functools.partial(join_kernel, dp),
        out_shape=jax.ShapeDtypeStruct((1, 2 * tokens, dp * width), BF16),
        in_specs=[SMEM_SPEC] * 2 + [VMEM_SPEC] * (4 + dp),
        out_specs=VMEM_SPEC,
        scratch_shapes=[pltpu.VMEM((feats + 16, dp * width), BF16), pltpu.VMEM((7, tokens, feats), BF16)],
        compiler_params=pltpu.CompilerParams(vmem_limit_bytes=8 * MIB),
        cost_estimate=cost(4 * tokens * feats * dp * width, 4 * tokens * dp * width),
        name="join",
    )(state, sums, message, third, even, odd, *pieces)


def solution(mesh):
    in_specs = (P("dp", "seq", None), P("dp", "seq")) + (P(),) * 8 + (P(None, "dp"), P("dp"))
    return jax.shard_map(local, mesh=mesh, in_specs=in_specs, out_specs=P("dp", "seq", None), check_vma=False)
```

```python
import functools
import jax
import jax.numpy as jnp
from jax import lax
from jax.sharding import PartitionSpec as P
from jax.experimental import pallas as pl
from jax.experimental.pallas import tpu as pltpu

GROUPS = 32
SLOT_ROWS = 32
SLOT_COLS = 8
LATENT_SHIFT = 0.0609
LATENT_SCALE = 1.5305
NORM_EPSILON = 1e-06
LANES = 128
VMEM_BYTES = 64 * 1024 * 1024
F32 = jnp.float32
BF16 = jnp.bfloat16


def group_total(stats, same_group):
    rows, channels = stats.shape
    chunks = channels // LANES
    packed = jnp.concatenate([stats[:, k * LANES:(k + 1) * LANES] for k in range(chunks)], axis=0)
    high = packed.astype(BF16)
    rest = packed - high.astype(F32)
    middle = rest.astype(BF16)
    low = (rest - middle.astype(F32)).astype(BF16)
    total = sum(jnp.dot(piece, same_group, preferred_element_type=F32) for piece in (high, middle, low))
    return jnp.concatenate([total[k * rows:(k + 1) * rows] for k in range(chunks)], axis=1)


def affine(stats, joined, gain, shift, same_group, count):
    total = group_total(stats, same_group)
    mean, square = total[0:2] * (1.0 / count), total[2:4] * (1.0 / count)
    both_mean = 0.5 * (mean[0:1] + mean[1:2])
    both_square = 0.5 * (square[0:1] + square[1:2])
    mean = jnp.where(joined, both_mean, mean)
    square = jnp.where(joined, both_square, square)
    spread = jnp.maximum(square - mean * mean, 0.0)
    scale = lax.rsqrt(spread + NORM_EPSILON) * (0.5 * gain)
    return scale, 0.5 * shift - mean * scale


def half_stats(half):
    total = jnp.sum(half, axis=0, keepdims=True)
    return total, jnp.sum(half * half, axis=0, keepdims=True)


def norm_first(x_ref, joined, gain, shift, same_group, z_ref, u_ref):
    cells, channels = x_ref.shape
    half = cells // 2
    rows = cells // SLOT_COLS
    chunks = channels // LANES
    count = half * (channels // GROUPS)
    keep = jnp.where(joined, 1.0, 0.0).astype(F32)
    column = lax.broadcasted_iota(jnp.int32, (1, SLOT_COLS, 1), 1)
    parts = []
    for k in range(chunks):
        x = x_ref[:, k * LANES:(k + 1) * LANES].astype(F32)
        t0, q0 = half_stats(x[:half])
        t1, q1 = half_stats(x[half:])
        parts.append(jnp.concatenate([t0, t1, q0, q1], axis=0))
    scale, offset = affine(jnp.concatenate(parts, axis=1), joined, gain, shift, same_group, count)
    zero = jnp.zeros((SLOT_COLS, LANES), F32)
    for k in range(chunks):
        lanes = slice(k * LANES, (k + 1) * LANES)
        x = x_ref[:, lanes].astype(F32)
        v = jnp.concatenate([x[:half] * scale[0:1, lanes] + offset[0:1, lanes],
                             x[half:] * scale[1:2, lanes] + offset[1:2, lanes]], axis=0)
        act = v + v * jnp.tanh(v)
        act3 = act.reshape(rows, SLOT_COLS, LANES)
        left = jnp.where(column == 0, 0.0, pltpu.roll(act3, 1, 1)).reshape(cells, LANES)
        right = jnp.where(column == SLOT_COLS - 1, 0.0, pltpu.roll(act3, SLOT_COLS - 1, 1)).reshape(cells, LANES)
        for b, value in enumerate((left, act, right)):
            z_ref[b, :, lanes] = value.astype(BF16)
            over = value[half:half + SLOT_COLS] * keep
            under = value[half - SLOT_COLS:half] * keep
            u_ref[b, 0, :, lanes] = jnp.concatenate([zero, value[:half], over], axis=0).astype(BF16)
            u_ref[b, 1, :, lanes] = jnp.concatenate([under, value[half:], zero], axis=0).astype(BF16)


def conv(x_ref, bias, wbuf, wait_weights, z_ref, u_ref, y_ref):
    cells, channels = x_ref.shape
    half = cells // 2
    total = None
    for step, a in enumerate((0, -1, 1)):
        if a == 0:
            lhs = jnp.concatenate([z_ref[b] for b in range(3)], axis=1)
        else:
            first = 0 if a < 0 else 2 * SLOT_COLS
            lhs = jnp.concatenate(
                [jnp.concatenate([u_ref[b, h, first:first + half, :] for h in range(2)], axis=0) for b in range(3)],
                axis=1)
        wait_weights(step)
        depth = 3 * channels
        base = (a + 1) * depth
        term = jnp.dot(lhs, wbuf[base:base + depth, :], preferred_element_type=F32)
        total = term if total is None else total + term
    y_ref[...] = (x_ref[...].astype(F32) + (total + bias)).astype(BF16)


def norm_second(y_ref, joined, gain, shift, same_group):
    cells, channels = y_ref.shape
    half = cells // 2
    chunks = channels // LANES
    count = half * (channels // GROUPS)
    parts = []
    for k in range(chunks):
        lanes = slice(k * LANES, (k + 1) * LANES)
        inner = y_ref[:, lanes].astype(F32)
        t0, q0 = half_stats(inner[:half])
        t1, q1 = half_stats(inner[half:])
        parts.append(jnp.concatenate([t0, t1, q0, q1], axis=0))
    scale, offset = affine(jnp.concatenate(parts, axis=1), joined, gain, shift, same_group, count)
    for k in range(chunks):
        lanes = slice(k * LANES, (k + 1) * LANES)
        y = y_ref[:, lanes].astype(F32)
        v = jnp.concatenate([y[:half] * scale[0:1, lanes] + offset[0:1, lanes],
                             y[half:] * scale[1:2, lanes] + offset[1:2, lanes]], axis=0)
        y_ref[:, lanes] = (v + v * jnp.tanh(v)).astype(BF16)


def to_patches(y_ref, joined, lw_ref, bias, perm):
    cells, channels = y_ref.shape
    rows = cells // SLOT_COLS
    keep = jnp.where(joined, 1.0, 0.0).astype(F32)
    column = lax.broadcasted_iota(jnp.int32, (1, SLOT_COLS, 1), 1)
    lane = lax.broadcasted_iota(jnp.int32, (1, 1, 2 * LANES), 2)
    lat = lw_ref.shape[0] // 9
    tap = whole(lane, lat)
    lane_a = jnp.where(tap < 3, 0, jnp.where(tap < 6, 1, 2))
    lane_b = tap - 3 * lane_a
    taps = lax.dot_general(y_ref[...], lw_ref[...], (((1,), (1,)), ((), ())), preferred_element_type=F32)
    taps = jnp.concatenate([taps, jnp.zeros((cells, 2 * LANES - 9 * lat), F32)], axis=1).reshape(rows, SLOT_COLS, 2 * LANES)
    from_left = jnp.where(column == 0, 0.0, pltpu.roll(taps, 1, 1))
    from_right = jnp.where(column == SLOT_COLS - 1, 0.0, pltpu.roll(taps, SLOT_COLS - 1, 1))
    moved = jnp.where(lane_b == 0, from_left, jnp.where(lane_b == 1, taps, from_right))
    blank = jnp.zeros((1, SLOT_COLS, 2 * LANES), F32)
    mid = rows // 2
    above = jnp.concatenate([blank, moved[:mid - 1], moved[mid - 1:mid] * keep, moved[mid:rows - 1]], axis=0)
    below = jnp.concatenate([moved[1:mid], moved[mid:mid + 1] * keep, moved[mid + 1:], blank], axis=0)
    moved = jnp.where(lane_a == 0, above, jnp.where(lane_a == 1, moved, below)).reshape(cells, 2 * LANES)
    folded = moved[:, :LANES]
    width = LANES // 2
    while width >= lat:
        folded = folded + pltpu.roll(folded, width, 1)
        width //= 2
    latent = (folded + moved[:, LANES:])[:, :lat]
    latent = ((latent + bias) - LATENT_SHIFT) * LATENT_SCALE
    spread = jnp.dot(perm, latent.astype(BF16), preferred_element_type=F32)
    tokens = cells // 4
    return jnp.concatenate([spread[k * tokens:(k + 1) * tokens] for k in range(4)], axis=1).astype(BF16)


def whole(value, size):
    return value >> (size.bit_length() - 1)


def part(value, size):
    return value & (size - 1)


def group_table(channels):
    width = channels // GROUPS
    r = whole(lax.broadcasted_iota(jnp.int32, (LANES, LANES), 0), width)
    c = whole(lax.broadcasted_iota(jnp.int32, (LANES, LANES), 1), width)
    return jnp.where(r == c, 1.0, 0.0).astype(BF16)


def patch_table(cells):
    tokens = cells // 4
    half_cols = SLOT_COLS // 2
    row = lax.broadcasted_iota(jnp.int32, (cells, cells), 0)
    col = lax.broadcasted_iota(jnp.int32, (cells, cells), 1)
    block, token = whole(row, tokens), part(row, tokens)
    cell = (2 * whole(token, half_cols) + whole(block, 2)) * SLOT_COLS + 2 * part(token, half_cols) + part(block, 2)
    return jnp.where(cell == col, 1.0, 0.0).astype(BF16)


FIRST = 1


def vector(ref):
    return ref[...].reshape(1, ref.shape[0])


def begin_kernel(kind_hbm, feat_hbm, bw_hbm, ew_hbm, eb_hbm, *rest):
    names = 7
    small_hbm, rest = rest[:names], rest[names:]
    state_ref, x_ref, w_ref, perm_ref, piece_ref, out_ref, *rest = rest
    small, rest = rest[:names], rest[names:]
    kind_ref, ew_ref, eb_ref, z_ref, u_ref, y_ref, ksem, xsem, wsem, ssem = rest
    gain1, shift1, bias1, gain2, shift2, lw_ref, bias2 = small
    slots, cells, channels = x_ref.shape
    kcopy = pltpu.make_async_copy(kind_hbm, kind_ref, ksem)
    kcopy.start()
    xcopies = [pltpu.make_async_copy(feat_hbm.at[0, pl.ds(s * cells, cells), :], x_ref.at[s], xsem.at[s])
               for s in range(slots)]
    depth = 3 * channels
    wcopies = [pltpu.make_async_copy(
        bw_hbm.at[pl.ds((a + 1) * depth, depth), :], w_ref.at[pl.ds((a + 1) * depth, depth), :], wsem.at[i])
        for i, a in enumerate((0, -1, 1))]
    scopies = [pltpu.make_async_copy(src, dst, ssem.at[i])
               for i, (src, dst) in enumerate(zip(small_hbm + (ew_hbm, eb_hbm), small + [ew_ref, eb_ref]))]
    xcopies[FIRST].start()
    for c in scopies + wcopies + [c for k, c in enumerate(xcopies) if k != FIRST]:
        c.start()
    perm_ref[...] = patch_table(cells)
    same_group = group_table(channels)
    kcopy.wait()
    live = jnp.int32(0)
    for s in range(slots):
        live = live + jnp.where(kind_ref[0, s] > 0, 1, 0).astype(jnp.int32)
    second = jnp.where(live > 2, 2, 0)
    state_ref[0] = live
    state_ref[1] = second
    state_ref[2] = kind_ref[0, second]
    state_ref[3] = kind_ref[0, 0]
    for c in scopies + [xcopies[FIRST]]:
        c.wait()
    feats = ew_ref.shape[0]
    piece_ref[0:feats, :] = ew_ref[...]
    piece_ref[feats:, :] = jnp.broadcast_to(vector(eb_ref), (piece_ref.shape[0] - feats, ew_ref.shape[1]))
    x = x_ref.at[FIRST]
    joined = kind_ref[0, FIRST] == 2
    norm_first(x, joined, vector(gain1), vector(shift1), same_group, z_ref, u_ref)
    conv(x, vector(bias1), w_ref, lambda step: wcopies[step].wait(), z_ref, u_ref, y_ref)
    norm_second(y_ref, joined, vector(gain2), vector(shift2), same_group)
    out_ref[...] = to_patches(y_ref, joined, lw_ref, vector(bias2), perm_ref[...])
    for k, c in enumerate(xcopies):
        if k != FIRST:
            c.wait()


def encode_slot(slot, kind, state_ref, x_ref, w_ref, perm_ref, small, scratch):
    gain1, shift1, bias1, gain2, shift2, lw_ref, bias2 = small
    z_ref, u_ref, y_ref = scratch
    same_group = group_table(x_ref.shape[2])
    x = x_ref.at[slot]
    joined = kind == 2
    norm_first(x, joined, vector(gain1), vector(shift1), same_group, z_ref, u_ref)
    conv(x, vector(bias1), w_ref, lambda step: None, z_ref, u_ref, y_ref)
    norm_second(y_ref, joined, vector(gain2), vector(shift2), same_group)
    return to_patches(y_ref, joined, lw_ref, vector(bias2), perm_ref[...])


def count_live(kind_ref):
    total = jnp.int32(-2)
    for s in range(kind_ref.shape[1]):
        total = total + jnp.where(kind_ref[0, s] > 0, 1, 0).astype(jnp.int32)
    return total


def middle_kernel(offsets, state_ref, x_ref, w_ref, perm_ref, last_ref, *rest):
    names = 7
    small, rest = rest[:names], rest[names:]
    others, rest = rest[:len(offsets)], rest[len(offsets):]
    message_ref, sums_ref, *rest = rest
    scratch, rest = rest[:3], rest[3:]
    kinds, ksem = rest[:-1], rest[-1]
    copies = [pltpu.make_async_copy(src, dst, ksem.at[i]) for i, (src, dst) in enumerate(zip(others, kinds))]
    for c in copies:
        c.start()
    tokens, feats = last_ref.shape
    first_at = pl.multiple_of(jnp.where(state_ref[0] == 2, 0, tokens), tokens)
    message_ref[pl.ds(first_at, tokens), :] = last_ref[...]
    message_ref[pl.ds(tokens - first_at, tokens), :] = encode_slot(
        state_ref[1], state_ref[2], state_ref, x_ref, w_ref, perm_ref, small, scratch)
    for c in copies:
        c.wait()
    position = lax.axis_index("seq")
    mine = state_ref[0] - 2
    below, above = jnp.int32(0), mine
    for offset, kind_ref in zip(offsets, kinds):
        other = count_live(kind_ref)
        lower = (position ^ offset) < position
        below = below + jnp.where(lower, other, 0)
        above = above + jnp.where(lower, 0, other)
    first_half = position < lax.axis_size("seq") // 2
    passed = jnp.where(position % 2 == 0, mine, 0)
    sums_ref[0] = jnp.where(first_half, below, -above)
    told = jnp.where(first_half, below + passed, passed - above)
    message_ref[2 * tokens:, :] = jnp.full((message_ref.shape[0] - 2 * tokens, feats), told.astype(F32)).astype(BF16)


def final_kernel(state_ref, x_ref, w_ref, perm_ref, *rest):
    small, rest = rest[:7], rest[7:]
    out_ref, *scratch = rest

    @pl.when(state_ref[0] > 2)
    def _():
        out_ref[...] = encode_slot(0, state_ref[3], state_ref, x_ref, w_ref, perm_ref, small, scratch)

    @pl.when(state_ref[0] <= 2)
    def _():
        out_ref[...] = jnp.zeros_like(out_ref)


def join_kernel(parts, state_ref, sums_ref, own_ref, third_ref, even_ref, odd_ref, *rest):
    pieces, out_ref, embed_ref, source_ref = rest[:parts], *rest[parts:]
    live = state_ref[0]
    group, position = lax.axis_index("dp"), lax.axis_index("seq")
    odd = position % 2
    tokens, feats = third_ref.shape
    width = pieces[0].shape[1]
    told = even_ref[2 * tokens:, :].astype(F32)[0, 0].astype(jnp.int32)
    carry = sums_ref[0] + told
    for j in range(parts):
        value = pieces[0][...]
        for k in range(1, parts):
            value = jnp.where((group ^ j) == k, pieces[k][...], value)
        embed_ref[:, j * width:(j + 1) * width] = value
    for k, ref in enumerate((even_ref, odd_ref, own_ref)):
        source_ref[2 * k] = ref[0:tokens, :]
        source_ref[2 * k + 1] = ref[tokens:2 * tokens, :]
    source_ref[6] = third_ref[...]
    weight = embed_ref[0:feats, :]
    bias = embed_ref[feats:feats + 1, :].astype(F32)
    for i in range(2):
        incoming = (1 - odd) * 2 + carry - 1 - i
        kept = 4 + live - 1 - (i - carry)
        patch = source_ref[jnp.clip(jnp.where(i < carry, incoming, kept), 0, 6)]
        value = jnp.dot(patch, weight, preferred_element_type=F32) + bias
        out_ref[0, i * tokens:(i + 1) * tokens, :] = value.astype(BF16)


def exchange(value, axis, offset):
    count = lax.axis_size(axis)
    return lax.ppermute(value, axis, [(i, i ^ offset) for i in range(count)])


def swap_odd_pairs(value):
    groups, count = lax.axis_size("dp"), lax.axis_size("seq")
    pairs = []
    for g in range(groups):
        pairs += [(g * count + end, (g ^ 1) * count + end) for end in (0, count - 1)]
        for i in range(1, count - 1, 2):
            pairs += [(g * count + i, g * count + i + 1), (g * count + i + 1, g * count + i)]
    return lax.ppermute(value, ("dp", "seq"), pairs)


VMEM_SPEC = pl.BlockSpec(memory_space=pltpu.VMEM)
SMEM_SPEC = pl.BlockSpec(memory_space=pltpu.SMEM)
ANY_SPEC = pl.BlockSpec(memory_space=pl.ANY)
MIB = 1024 * 1024


def cost(flops, moved):
    return pl.CostEstimate(flops=flops, bytes_accessed=moved, transcendentals=0)


def encode_buffers(cells, channels):
    return [
        pltpu.VMEM((3, cells, channels), BF16),
        pltpu.VMEM((3, 2, cells // 2 + 2 * SLOT_COLS, channels), BF16),
        pltpu.VMEM((cells, channels), BF16),
    ]


def encode_flops(cells, channels, lat):
    return cells * channels * 2 * 9 * (channels + lat)


def begin(features, slot_kind, block_weight, embed_weight, embed_bias, small):
    slots = slot_kind.shape[1]
    channels = features.shape[2]
    cells = SLOT_ROWS * SLOT_COLS
    tokens = cells // 4
    feats, width = embed_weight.shape
    buffers = encode_buffers(cells, channels)
    flops = encode_flops(cells, channels, small[6].shape[0])
    return pl.pallas_call(
        begin_kernel,
        out_shape=[
            pltpu.SMEM((8,), jnp.int32),
            pltpu.VMEM((slots, cells, channels), BF16),
            pltpu.VMEM(block_weight.shape, BF16),
            pltpu.VMEM((cells, cells), BF16),
            pltpu.VMEM((feats + 16, width), BF16),
            pltpu.VMEM((tokens, feats), BF16),
        ] + [pltpu.VMEM(v.shape, v.dtype) for v in small],
        in_specs=[ANY_SPEC] * (5 + len(small)),
        out_specs=[SMEM_SPEC] + [VMEM_SPEC] * (5 + len(small)),
        scratch_shapes=[
            pltpu.SMEM(slot_kind.shape, jnp.int32),
            pltpu.VMEM(embed_weight.shape, BF16),
            pltpu.VMEM(embed_bias.shape, BF16),
        ] + buffers + [
            pltpu.SemaphoreType.DMA,
            pltpu.SemaphoreType.DMA((slots,)),
            pltpu.SemaphoreType.DMA((3,)),
            pltpu.SemaphoreType.DMA((len(small) + 2,)),
        ],
        compiler_params=pltpu.CompilerParams(vmem_limit_bytes=55 * MIB),
        cost_estimate=cost(flops, block_weight.size * 2),
        name="begin",
    )(slot_kind, features, block_weight, embed_weight, embed_bias, *small)


def local(features, slot_kind, block_gain, block_shift, block_weight, block_bias, final_gain, final_shift,
          latent_weight, latent_bias, embed_weight, embed_bias):
    seq, dp = lax.axis_size("seq"), lax.axis_size("dp")
    channels = features.shape[2]
    cells = SLOT_ROWS * SLOT_COLS
    tokens = cells // 4
    feats, width = embed_weight.shape
    small = (block_gain, block_shift, block_bias, final_gain, final_shift, latent_weight.T, latent_bias)
    offsets = tuple(range(2, seq // 2, 2))
    others = [exchange(slot_kind, "seq", offset) for offset in offsets]
    buffers = encode_buffers(cells, channels)
    flops = encode_flops(cells, channels, latent_bias.shape[0])
    state, x, w, perm, piece, last, *small = begin(features, slot_kind, block_weight, embed_weight, embed_bias, small)
    message, sums = pl.pallas_call(
        functools.partial(middle_kernel, offsets),
        out_shape=[jax.ShapeDtypeStruct((2 * tokens + 16, feats), BF16), pltpu.SMEM((1,), jnp.int32)],
        in_specs=[SMEM_SPEC] + [VMEM_SPEC] * (4 + len(small)) + [ANY_SPEC] * len(others),
        out_specs=[VMEM_SPEC, SMEM_SPEC],
        scratch_shapes=buffers + [pltpu.SMEM(slot_kind.shape, jnp.int32) for _ in others]
        + [pltpu.SemaphoreType.DMA((len(others),))],
        compiler_params=pltpu.CompilerParams(vmem_limit_bytes=24 * MIB),
        cost_estimate=cost(flops, block_weight.size * 2),
        name="middle",
    )(state, x, w, perm, last, *small, *others)
    even = exchange(message, "seq", 1)
    odd = swap_odd_pairs(message)
    pieces = [piece] + [exchange(piece, "dp", offset) for offset in range(1, dp)]
    third = pl.pallas_call(
        final_kernel,
        out_shape=pltpu.VMEM((tokens, feats), BF16),
        in_specs=[SMEM_SPEC] + [VMEM_SPEC] * (3 + len(small)),
        out_specs=VMEM_SPEC,
        scratch_shapes=buffers,
        compiler_params=pltpu.CompilerParams(vmem_limit_bytes=24 * MIB),
        cost_estimate=cost(flops, block_weight.size * 2),
        name="final",
    )(state, x, w, perm, *small)
    return pl.pallas_call(
        functools.partial(join_kernel, dp),
        out_shape=jax.ShapeDtypeStruct((1, 2 * tokens, dp * width), BF16),
        in_specs=[SMEM_SPEC] * 2 + [VMEM_SPEC] * (4 + dp),
        out_specs=VMEM_SPEC,
        scratch_shapes=[pltpu.VMEM((feats + 16, dp * width), BF16), pltpu.VMEM((7, tokens, feats), BF16)],
        compiler_params=pltpu.CompilerParams(vmem_limit_bytes=8 * MIB),
        cost_estimate=cost(4 * tokens * feats * dp * width, 4 * tokens * dp * width),
        name="join",
    )(state, sums, message, third, even, odd, *pieces)


def solution(mesh):
    in_specs = (P("dp", "seq", None), P("dp", "seq")) + (P(),) * 8 + (P(None, "dp"), P("dp"))
    return jax.shard_map(local, mesh=mesh, in_specs=in_specs, out_specs=P("dp", "seq", None), check_vma=False)
```

```python
import functools
import jax
import jax.numpy as jnp
from jax import lax
from jax.sharding import PartitionSpec as P
from jax.sharding import PartitionSpec as P
from jax.experimental import pallas as pl
from jax.experimental.pallas import tpu as pltpu

GROUPS = 32
SLOT_ROWS = 32
SLOT_COLS = 8
LATENT_SHIFT = 0.0609
LATENT_SCALE = 1.5305
NORM_EPSILON = 1e-06
LANES = 128
ROW_STEPS = (0, -1, 1)
VMEM_BYTES = 64 * 1024 * 1024
F32 = jnp.float32
BF16 = jnp.bfloat16


def group_total(stats, same_group):
    rows, channels = stats.shape
    chunks = channels // LANES
    packed = jnp.concatenate([stats[:, k * LANES:(k + 1) * LANES] for k in range(chunks)], axis=0)
    high = packed.astype(BF16)
    rest = packed - high.astype(F32)
    middle = rest.astype(BF16)
    low = (rest - middle.astype(F32)).astype(BF16)
    total = sum(jnp.dot(piece, same_group, preferred_element_type=F32) for piece in (high, middle, low))
    return jnp.concatenate([total[k * rows:(k + 1) * rows] for k in range(chunks)], axis=1)


def affine(stats, joined, gain, shift, same_group, count):
    total = group_total(stats, same_group)
    mean, square = total[0:2] * (1.0 / count), total[2:4] * (1.0 / count)
    both_mean = 0.5 * (mean[0:1] + mean[1:2])
    both_square = 0.5 * (square[0:1] + square[1:2])
    mean = jnp.where(joined, both_mean, mean)
    square = jnp.where(joined, both_square, square)
    spread = jnp.maximum(square - mean * mean, 0.0)
    scale = lax.rsqrt(spread + NORM_EPSILON) * (0.5 * gain)
    return scale, 0.5 * shift - mean * scale


def half_stats(half):
    total = jnp.sum(half, axis=0, keepdims=True)
    return total, jnp.sum(half * half, axis=0, keepdims=True)


def norm_first_steps(x_ref, joined, gain, shift, same_group, z_ref, u_ref):
    cells, channels = x_ref.shape
    half = cells // 2
    rows = cells // SLOT_COLS
    chunks = channels // LANES
    count = half * (channels // GROUPS)
    keep = jnp.where(joined, 1.0, 0.0).astype(F32)
    column = lax.broadcasted_iota(jnp.int32, (1, SLOT_COLS, 1), 1)
    parts = []
    for k in range(chunks):
        x = x_ref[:, k * LANES:(k + 1) * LANES].astype(F32)
        t0, q0 = half_stats(x[:half])
        t1, q1 = half_stats(x[half:])
        parts.append(jnp.concatenate([t0, t1, q0, q1], axis=0))
        yield
    scale, offset = affine(jnp.concatenate(parts, axis=1), joined, gain, shift, same_group, count)
    zero = jnp.zeros((SLOT_COLS, LANES), F32)
    for k in range(chunks):
        lanes = slice(k * LANES, (k + 1) * LANES)
        x = x_ref[:, lanes].astype(F32)
        v = jnp.concatenate([x[:half] * scale[0:1, lanes] + offset[0:1, lanes],
                             x[half:] * scale[1:2, lanes] + offset[1:2, lanes]], axis=0)
        act = v + v * jnp.tanh(v)
        act3 = act.reshape(rows, SLOT_COLS, LANES)
        left = jnp.where(column == 0, 0.0, pltpu.roll(act3, 1, 1)).reshape(cells, LANES)
        right = jnp.where(column == SLOT_COLS - 1, 0.0, pltpu.roll(act3, SLOT_COLS - 1, 1)).reshape(cells, LANES)
        for b, value in enumerate((left, act, right)):
            z_ref[b, :, lanes] = value.astype(BF16)
            over = value[half:half + SLOT_COLS] * keep
            under = value[half - SLOT_COLS:half] * keep
            u_ref[b, 0, :, lanes] = jnp.concatenate([zero, value[:half], over], axis=0).astype(BF16)
            u_ref[b, 1, :, lanes] = jnp.concatenate([under, value[half:], zero], axis=0).astype(BF16)
        yield


def conv_steps(x_ref, bias, wbuf, wait_weights, z_ref, u_ref, y_ref):
    cells, channels = x_ref.shape
    half = cells // 2
    tile = channels // 2
    totals = [x_ref[:, k * tile:(k + 1) * tile].astype(F32) + bias[:, k * tile:(k + 1) * tile] for k in range(2)]
    for step, a in enumerate(ROW_STEPS):
        wait_weights(step)
        for b in range(3):
            if a == 0:
                lhs = z_ref[b]
            else:
                first = 0 if a < 0 else 2 * SLOT_COLS
                lhs = jnp.concatenate([u_ref[b, h, first:first + half, :] for h in range(2)], axis=0)
            base = (3 * (a + 1) + b) * channels
            for k in range(2):
                totals[k] = totals[k] + jnp.dot(lhs, wbuf[base:base + channels, k * tile:(k + 1) * tile],
                                                preferred_element_type=F32)
                yield
    for k in range(2):
        y_ref[:, k * tile:(k + 1) * tile] = totals[k].astype(BF16)
    yield


def drain(steps):
    for _ in steps:
        pass


def interleave(main, *others):
    for _ in main:
        for steps in others:
            next(steps, None)
    for steps in others:
        drain(steps)


def norm_second_steps(y_ref, joined, gain, shift, same_group):
    cells, channels = y_ref.shape
    half = cells // 2
    chunks = channels // LANES
    count = half * (channels // GROUPS)
    parts = []
    for k in range(chunks):
        lanes = slice(k * LANES, (k + 1) * LANES)
        inner = y_ref[:, lanes].astype(F32)
        t0, q0 = half_stats(inner[:half])
        t1, q1 = half_stats(inner[half:])
        parts.append(jnp.concatenate([t0, t1, q0, q1], axis=0))
        yield
    scale, offset = affine(jnp.concatenate(parts, axis=1), joined, gain, shift, same_group, count)
    for k in range(chunks):
        lanes = slice(k * LANES, (k + 1) * LANES)
        y = y_ref[:, lanes].astype(F32)
        v = jnp.concatenate([y[:half] * scale[0:1, lanes] + offset[0:1, lanes],
                             y[half:] * scale[1:2, lanes] + offset[1:2, lanes]], axis=0)
        y_ref[:, lanes] = (v + v * jnp.tanh(v)).astype(BF16)
        yield


def to_patches_steps(store, y_ref, joined, table_ref, bias, gather):
    cells, channels = y_ref.shape
    rows = cells // SLOT_COLS
    mid = rows // 2
    tokens = gather.shape[0]
    lat = channels // GROUPS
    keep = jnp.where(joined, 1.0, 0.0).astype(F32)
    column = lax.broadcasted_iota(jnp.int32, (1, SLOT_COLS, 1), 1)
    block = whole(lax.broadcasted_iota(jnp.int32, (1, SLOT_COLS, LANES), 2), lat)
    taps = jnp.dot(y_ref[...], table_ref[...], preferred_element_type=F32)
    yield
    from_left, here, from_right = (taps[:, k * LANES:(k + 1) * LANES].reshape(rows, SLOT_COLS, LANES) for k in range(3))
    moved = here + jnp.where(column == 0, 0.0, pltpu.roll(from_left, 1, 1))
    moved = moved + jnp.where(column == SLOT_COLS - 1, 0.0, pltpu.roll(from_right, SLOT_COLS - 1, 1))
    yield
    blank = jnp.zeros((1, SLOT_COLS, LANES), F32)
    above = jnp.concatenate([blank, moved[:mid - 1], moved[mid - 1:mid] * keep, moved[mid:rows - 1]], axis=0)
    below = jnp.concatenate([moved[1:mid], moved[mid:mid + 1] * keep, moved[mid + 1:], blank], axis=0)
    step_up = (block == 0) | (block == 3)
    step_none = (block == 1) | (block == 4)
    mixed = jnp.where(step_up, above, jnp.where(step_none, moved, below)).reshape(cells, LANES)
    yield
    latent = mixed + pltpu.roll(mixed, LANES - lat, 1) + pltpu.roll(mixed, LANES - 2 * lat, 1)
    latent = ((latent + bias) - LATENT_SHIFT) * LATENT_SCALE
    corner = block - part(lax.broadcasted_iota(jnp.int32, (1, SLOT_COLS, LANES), 1), 2)
    corner = jnp.concatenate([corner, corner - 2], axis=0)
    latent = latent.reshape(rows // 2, 2, SLOT_COLS, LANES)
    latent = jnp.where((corner == 0)[None], latent, 0.0).reshape(cells, LANES)
    yield
    store(jnp.dot(gather, latent.astype(BF16), preferred_element_type=F32)[:, :4 * lat].astype(BF16))
    yield


def patch_tables(lw_ref, bias_ref, table_ref, bias4_ref):
    lat = lw_ref.shape[0] // 9
    weight = lw_ref[...].astype(F32)
    blank = jnp.zeros((2 * lat, weight.shape[1]), F32)
    for b in range(3):
        blocks = [weight[(3 * a + b) * lat:(3 * a + b + 1) * lat] for a in range(3)]
        table_ref[:, b * LANES:(b + 1) * LANES] = jnp.concatenate(blocks * 2 + [blank], axis=0).T.astype(BF16)
    bias4_ref[...] = jnp.concatenate([bias_ref[...].reshape(1, lat)] * (LANES // lat), axis=1)


def whole(value, size):
    return value >> (size.bit_length() - 1)


def part(value, size):
    return value & (size - 1)


def group_table(channels):
    width = channels // GROUPS
    r = whole(lax.broadcasted_iota(jnp.int32, (LANES, LANES), 0), width)
    c = whole(lax.broadcasted_iota(jnp.int32, (LANES, LANES), 1), width)
    return jnp.where(r == c, 1.0, 0.0).astype(BF16)


def patch_table(cells):
    half_cols = SLOT_COLS // 2
    token = lax.broadcasted_iota(jnp.int32, (cells // 4, cells), 0)
    cell = lax.broadcasted_iota(jnp.int32, (cells // 4, cells), 1)
    own = whole(whole(cell, SLOT_COLS), 2) * half_cols + whole(part(cell, SLOT_COLS), 2)
    return jnp.where(own == token, 1.0, 0.0).astype(BF16)


def finish_steps(store, y_ref, joined, gain, shift, same_group, table_ref, bias4, gather):
    yield from norm_second_steps(y_ref, joined, gain, shift, same_group)
    yield from to_patches_steps(store, y_ref, joined, table_ref, bias4, gather)


FIRST = 1


def vector(ref):
    return ref[...].reshape(1, ref.shape[0])


def begin_kernel(kind_hbm, feat_hbm, bw_hbm, ew_hbm, eb_hbm, *rest):
    names = 7
    small_hbm, rest = rest[:names], rest[names:]
    state_ref, x_ref, w_ref, perm_ref, piece_ref, y_ref, z_ref, u_ref, *rest = rest
    small, rest = rest[:names - 2], rest[names - 2:]
    table_ref, bias4_ref, kind_ref, lw_ref, lb_ref, ew_ref, eb_ref, ksem, xsem, wsem, ssem = rest
    gain1, shift1, bias1 = small[:3]
    slots, cells, channels = x_ref.shape
    kcopy = pltpu.make_async_copy(kind_hbm, kind_ref, ksem)
    kcopy.start()
    xcopies = [pltpu.make_async_copy(feat_hbm.at[0, pl.ds(s * cells, cells), :], x_ref.at[s], xsem.at[s])
               for s in range(slots)]
    depth = 3 * channels
    wcopies = [pltpu.make_async_copy(
        bw_hbm.at[pl.ds((a + 1) * depth, depth), :], w_ref.at[pl.ds((a + 1) * depth, depth), :], wsem.at[i])
        for i, a in enumerate(ROW_STEPS)]
    scopies = [pltpu.make_async_copy(src, dst, ssem.at[i])
               for i, (src, dst) in enumerate(zip(small_hbm + (ew_hbm, eb_hbm), small + [lw_ref, lb_ref, ew_ref, eb_ref]))]
    others = [k for k in range(slots) if k != FIRST]
    for c in [xcopies[FIRST]] + scopies + [xcopies[k] for k in others]:
        c.start()
    for c in wcopies:
        c.start(priority=1)
    perm_ref[...] = patch_table(cells)
    same_group = group_table(channels)
    kcopy.wait()
    live = jnp.int32(0)
    for s in range(slots):
        live = live + jnp.where(kind_ref[0, s] > 0, 1, 0).astype(jnp.int32)
        state_ref[2 + s] = kind_ref[0, s]
    state_ref[0] = live
    state_ref[1] = jnp.where(live > 2, 2, 0)
    for c in scopies + [xcopies[FIRST]]:
        c.wait()
    feats = ew_ref.shape[0]
    piece_ref[0:feats, :] = ew_ref[...]
    piece_ref[feats:, :] = jnp.broadcast_to(vector(eb_ref), (piece_ref.shape[0] - feats, ew_ref.shape[1]))

    def first_norm(k):
        return norm_first_steps(x_ref.at[k], kind_ref[0, k] == 2, vector(gain1), vector(shift1), same_group,
                                z_ref.at[k], u_ref.at[k])

    def side_work():
        for k in others:
            yield from first_norm(k)
        patch_tables(lw_ref, lb_ref, table_ref, bias4_ref)
        yield

    drain(first_norm(FIRST))
    for k in others:
        xcopies[k].wait()
    interleave(conv_steps(x_ref.at[FIRST], vector(bias1), w_ref, lambda step: wcopies[step].wait(),
                          z_ref.at[FIRST], u_ref.at[FIRST], y_ref), side_work())


def second_norm(y_ref, kind, small):
    return norm_second_steps(y_ref, kind == 2, vector(small[3]), vector(small[4]), group_table(y_ref.shape[1]))


def patches(store, y_ref, kind, small, perm_ref):
    return to_patches_steps(store, y_ref, kind == 2, small[5], small[6][...], perm_ref[...])


def chain(*parts):
    for steps in parts:
        yield from steps


def count_live(kind_ref):
    total = jnp.int32(-2)
    for s in range(kind_ref.shape[1]):
        total = total + jnp.where(kind_ref[0, s] > 0, 1, 0).astype(jnp.int32)
    return total


def middle_kernel(offsets, state_ref, x_ref, w_ref, perm_ref, first_ref, z_ref, u_ref, *rest):
    names = 7
    small, rest = rest[:names], rest[names:]
    others, rest = rest[:len(offsets)], rest[len(offsets):]
    message_ref, sums_ref, *rest = rest
    early_ref, y_ref, *rest = rest
    kinds, ksem = rest[:-1], rest[-1]
    copies = [pltpu.make_async_copy(src, dst, ksem.at[i]) for i, (src, dst) in enumerate(zip(others, kinds))]
    for c in copies:
        c.start()
    tokens = first_ref.shape[0] // 4
    feats = message_ref.shape[1]
    slot = state_ref[1]
    early_ref[...] = first_ref[...]
    first_at = jnp.where(state_ref[0] == 2, 0, tokens)

    def store_at(row):
        def store(value):
            message_ref[pl.ds(pl.multiple_of(row, tokens), tokens), :] = value
        return store

    kind, early_kind = state_ref[2 + slot], state_ref[2 + FIRST]
    interleave(conv_steps(x_ref.at[slot], vector(small[2]), w_ref, lambda step: None, z_ref.at[slot], u_ref.at[slot],
                          y_ref), second_norm(early_ref, early_kind, small))
    interleave(chain(second_norm(y_ref, kind, small), patches(store_at(tokens - first_at), y_ref, kind, small, perm_ref)),
               patches(store_at(first_at), early_ref, early_kind, small, perm_ref))
    for c in copies:
        c.wait()
    position = lax.axis_index("seq")
    mine = state_ref[0] - 2
    below, above = jnp.int32(0), mine
    for offset, kind_ref in zip(offsets, kinds):
        other = count_live(kind_ref)
        lower = (position ^ offset) < position
        below = below + jnp.where(lower, other, 0)
        above = above + jnp.where(lower, 0, other)
    first_half = position < lax.axis_size("seq") // 2
    passed = jnp.where(position % 2 == 0, mine, 0)
    sums_ref[0] = jnp.where(first_half, below, -above)
    told = jnp.where(first_half, below + passed, passed - above)
    message_ref[2 * tokens:, :] = jnp.full((message_ref.shape[0] - 2 * tokens, feats), told.astype(F32)).astype(BF16)


def final_kernel(state_ref, x_ref, w_ref, perm_ref, z_ref, u_ref, *rest):
    small, rest = rest[:7], rest[7:]
    out_ref, y_ref = rest

    @pl.when(state_ref[0] > 2)
    def _():
        def store(value):
            out_ref[...] = value

        drain(conv_steps(x_ref.at[0], vector(small[2]), w_ref, lambda step: None, z_ref.at[0], u_ref.at[0], y_ref))
        drain(second_norm(y_ref, state_ref[2], small))
        drain(patches(store, y_ref, state_ref[2], small, perm_ref))

    @pl.when(state_ref[0] <= 2)
    def _():
        out_ref[...] = jnp.zeros_like(out_ref)


def join_kernel(parts, state_ref, sums_ref, own_ref, third_ref, even_ref, odd_ref, *rest):
    pieces, out_ref, embed_ref, source_ref = rest[:parts], *rest[parts:]
    live = state_ref[0]
    group, position = lax.axis_index("dp"), lax.axis_index("seq")
    odd = position % 2
    tokens, feats = third_ref.shape
    width = pieces[0].shape[1]
    told = even_ref[2 * tokens:, :].astype(F32)[0, 0].astype(jnp.int32)
    carry = sums_ref[0] + told
    for j in range(parts):
        value = pieces[0][...]
        for k in range(1, parts):
            value = jnp.where((group ^ j) == k, pieces[k][...], value)
        embed_ref[:, j * width:(j + 1) * width] = value
    for k, ref in enumerate((even_ref, odd_ref, own_ref)):
        source_ref[2 * k] = ref[0:tokens, :]
        source_ref[2 * k + 1] = ref[tokens:2 * tokens, :]
    source_ref[6] = third_ref[...]
    weight = embed_ref[0:feats, :]
    bias = embed_ref[feats:feats + 1, :].astype(F32)
    for i in range(2):
        incoming = (1 - odd) * 2 + carry - 1 - i
        kept = 4 + live - 1 - (i - carry)
        patch = source_ref[jnp.clip(jnp.where(i < carry, incoming, kept), 0, 6)]
        value = jnp.dot(patch, weight, preferred_element_type=F32) + bias
        out_ref[0, i * tokens:(i + 1) * tokens, :] = value.astype(BF16)


def exchange(value, axis, offset):
    count = lax.axis_size(axis)
    return lax.ppermute(value, axis, [(i, i ^ offset) for i in range(count)])


def swap_odd_pairs(value):
    groups, count = lax.axis_size("dp"), lax.axis_size("seq")
    pairs = []
    for g in range(groups):
        pairs += [(g * count + end, (g ^ 1) * count + end) for end in (0, count - 1)]
        for i in range(1, count - 1, 2):
            pairs += [(g * count + i, g * count + i + 1), (g * count + i + 1, g * count + i)]
    return lax.ppermute(value, ("dp", "seq"), pairs)


VMEM_SPEC = pl.BlockSpec(memory_space=pltpu.VMEM)
SMEM_SPEC = pl.BlockSpec(memory_space=pltpu.SMEM)
ANY_SPEC = pl.BlockSpec(memory_space=pl.ANY)
MIB = 1024 * 1024


def cost(flops, moved):
    return pl.CostEstimate(flops=flops, bytes_accessed=moved, transcendentals=0)


def encode_flops(cells, channels, lat):
    return cells * channels * 2 * 9 * (channels + lat)


def begin(features, slot_kind, block_weight, embed_weight, embed_bias, small):
    slots = slot_kind.shape[1]
    channels = features.shape[2]
    cells = SLOT_ROWS * SLOT_COLS
    feats, width = embed_weight.shape
    flops = encode_flops(cells, channels, small[6].shape[0])
    return pl.pallas_call(
        begin_kernel,
        out_shape=[
            pltpu.SMEM((8,), jnp.int32),
            pltpu.VMEM((slots, cells, channels), BF16),
            pltpu.VMEM(block_weight.shape, BF16),
            pltpu.VMEM((cells // 4, cells), BF16),
            pltpu.VMEM((feats + 16, width), BF16),
            pltpu.VMEM((cells, channels), BF16),
            pltpu.VMEM((slots, 3, cells, channels), BF16),
            pltpu.VMEM((slots, 3, 2, cells // 2 + 2 * SLOT_COLS, channels), BF16),
        ] + [pltpu.VMEM(v.shape, v.dtype) for v in small[:5]]
        + [pltpu.VMEM((channels, 3 * LANES), BF16), pltpu.VMEM((1, LANES), F32)],
        in_specs=[ANY_SPEC] * (5 + len(small)),
        out_specs=[SMEM_SPEC] + [VMEM_SPEC] * (7 + len(small)),
        scratch_shapes=[
            pltpu.SMEM(slot_kind.shape, jnp.int32),
            pltpu.VMEM(small[5].shape, BF16),
            pltpu.VMEM(small[6].shape, F32),
            pltpu.VMEM(embed_weight.shape, BF16),
            pltpu.VMEM(embed_bias.shape, BF16),
            pltpu.SemaphoreType.DMA,
            pltpu.SemaphoreType.DMA((slots,)),
            pltpu.SemaphoreType.DMA((3,)),
            pltpu.SemaphoreType.DMA((len(small) + 2,)),
        ],
        compiler_params=pltpu.CompilerParams(vmem_limit_bytes=50 * MIB),
        cost_estimate=cost(flops, block_weight.size * 2),
        name="begin",
    )(slot_kind, features, block_weight, embed_weight, embed_bias, *small)


def local(features, slot_kind, block_gain, block_shift, block_weight, block_bias, final_gain, final_shift,
          latent_weight, latent_bias, embed_weight, embed_bias):
    seq, dp = lax.axis_size("seq"), lax.axis_size("dp")
    channels = features.shape[2]
    cells = SLOT_ROWS * SLOT_COLS
    tokens = cells // 4
    feats, width = embed_weight.shape
    small = (block_gain, block_shift, block_bias, final_gain, final_shift, latent_weight.T, latent_bias)
    offsets = tuple(range(2, seq // 2, 2))
    others = [exchange(slot_kind, "seq", offset) for offset in offsets]
    slot_buffer = pltpu.VMEM((cells, channels), BF16)
    flops = encode_flops(cells, channels, latent_bias.shape[0])
    state, x, w, perm, piece, first, z, u, *small = begin(features, slot_kind, block_weight, embed_weight, embed_bias, small)
    message, sums = pl.pallas_call(
        functools.partial(middle_kernel, offsets),
        out_shape=[jax.ShapeDtypeStruct((2 * tokens + 16, feats), BF16), pltpu.SMEM((1,), jnp.int32)],
        in_specs=[SMEM_SPEC] + [VMEM_SPEC] * (6 + len(small)) + [ANY_SPEC] * len(others),
        out_specs=[VMEM_SPEC, SMEM_SPEC],
        scratch_shapes=[slot_buffer] * 2 + [pltpu.SMEM(slot_kind.shape, jnp.int32) for _ in others]
        + [pltpu.SemaphoreType.DMA((len(others),))],
        compiler_params=pltpu.CompilerParams(vmem_limit_bytes=16 * MIB),
        cost_estimate=cost(flops, block_weight.size * 2),
        name="middle",
    )(state, x, w, perm, first, z, u, *small, *others)
    even = exchange(message, "seq", 1)
    odd = swap_odd_pairs(message)
    pieces = [piece] + [exchange(piece, "dp", offset) for offset in range(1, dp)]
    third = pl.pallas_call(
        final_kernel,
        out_shape=pltpu.VMEM((tokens, feats), BF16),
        in_specs=[SMEM_SPEC] + [VMEM_SPEC] * (5 + len(small)),
        out_specs=VMEM_SPEC,
        scratch_shapes=[slot_buffer],
        compiler_params=pltpu.CompilerParams(vmem_limit_bytes=16 * MIB),
        cost_estimate=cost(flops, block_weight.size * 2),
        name="final",
    )(state, x, w, perm, z, u, *small)
    return pl.pallas_call(
        functools.partial(join_kernel, dp),
        out_shape=jax.ShapeDtypeStruct((1, 2 * tokens, dp * width), BF16),
        in_specs=[SMEM_SPEC] * 2 + [VMEM_SPEC] * (4 + dp),
        out_specs=VMEM_SPEC,
        scratch_shapes=[pltpu.VMEM((feats + 16, dp * width), BF16), pltpu.VMEM((7, tokens, feats), BF16)],
        compiler_params=pltpu.CompilerParams(vmem_limit_bytes=8 * MIB),
        cost_estimate=cost(4 * tokens * feats * dp * width, 4 * tokens * dp * width),
        name="join",
    )(state, sums, message, third, even, odd, *pieces)


def solution(mesh):
    in_specs = (P("dp", "seq", None), P("dp", "seq")) + (P(),) * 8 + (P(None, "dp"), P("dp"))
    return jax.shard_map(local, mesh=mesh, in_specs=in_specs, out_specs=P("dp", "seq", None), check_vma=False)
```

```python
import functools
import jax
import jax.numpy as jnp
from jax import lax
from jax.sharding import PartitionSpec as P
from jax.sharding import PartitionSpec as P
from jax.experimental import pallas as pl
from jax.experimental.pallas import tpu as pltpu

GROUPS = 32
SLOT_ROWS = 32
SLOT_COLS = 8
LATENT_SHIFT = 0.0609
LATENT_SCALE = 1.5305
NORM_EPSILON = 1e-06
LANES = 128
ROW_STEPS = (0, -1, 1)
VMEM_BYTES = 64 * 1024 * 1024
F32 = jnp.float32
BF16 = jnp.bfloat16


def group_total(stats, same_group):
    rows, channels = stats.shape
    chunks = channels // LANES
    packed = jnp.concatenate([stats[:, k * LANES:(k + 1) * LANES] for k in range(chunks)], axis=0)
    high = packed.astype(BF16)
    rest = packed - high.astype(F32)
    middle = rest.astype(BF16)
    low = (rest - middle.astype(F32)).astype(BF16)
    total = sum(jnp.dot(piece, same_group, preferred_element_type=F32) for piece in (high, middle, low))
    return jnp.concatenate([total[k * rows:(k + 1) * rows] for k in range(chunks)], axis=1)


def affine(stats, joined, gain, shift, same_group, count):
    total = group_total(stats, same_group)
    mean, square = total[0:2] * (1.0 / count), total[2:4] * (1.0 / count)
    both_mean = 0.5 * (mean[0:1] + mean[1:2])
    both_square = 0.5 * (square[0:1] + square[1:2])
    mean = jnp.where(joined, both_mean, mean)
    square = jnp.where(joined, both_square, square)
    spread = jnp.maximum(square - mean * mean, 0.0)
    scale = lax.rsqrt(spread + NORM_EPSILON) * (0.5 * gain)
    return scale, 0.5 * shift - mean * scale


def half_stats(half):
    total = jnp.sum(half, axis=0, keepdims=True)
    return total, jnp.sum(half * half, axis=0, keepdims=True)


def norm_first_steps(x_ref, joined, gain, shift, same_group, z_ref, u_ref):
    cells, channels = x_ref.shape
    half = cells // 2
    rows = cells // SLOT_COLS
    chunks = channels // LANES
    count = half * (channels // GROUPS)
    keep = jnp.where(joined, 1.0, 0.0).astype(F32)
    column = lax.broadcasted_iota(jnp.int32, (1, SLOT_COLS, 1), 1)
    parts = []
    for k in range(chunks):
        x = x_ref[:, k * LANES:(k + 1) * LANES].astype(F32)
        t0, q0 = half_stats(x[:half])
        t1, q1 = half_stats(x[half:])
        parts.append(jnp.concatenate([t0, t1, q0, q1], axis=0))
        yield
    scale, offset = affine(jnp.concatenate(parts, axis=1), joined, gain, shift, same_group, count)
    zero = jnp.zeros((SLOT_COLS, LANES), F32)
    for k in range(chunks):
        lanes = slice(k * LANES, (k + 1) * LANES)
        x = x_ref[:, lanes].astype(F32)
        v = jnp.concatenate([x[:half] * scale[0:1, lanes] + offset[0:1, lanes],
                             x[half:] * scale[1:2, lanes] + offset[1:2, lanes]], axis=0)
        act = v + v * jnp.tanh(v)
        act3 = act.reshape(rows, SLOT_COLS, LANES)
        left = jnp.where(column == 0, 0.0, pltpu.roll(act3, 1, 1)).reshape(cells, LANES)
        right = jnp.where(column == SLOT_COLS - 1, 0.0, pltpu.roll(act3, SLOT_COLS - 1, 1)).reshape(cells, LANES)
        for b, value in enumerate((left, act, right)):
            z_ref[b, :, lanes] = value.astype(BF16)
            over = value[half:half + SLOT_COLS] * keep
            under = value[half - SLOT_COLS:half] * keep
            u_ref[b, 0, :, lanes] = jnp.concatenate([zero, value[:half], over], axis=0).astype(BF16)
            u_ref[b, 1, :, lanes] = jnp.concatenate([under, value[half:], zero], axis=0).astype(BF16)
        yield


def conv_steps(x_ref, bias, wbuf, wait_weights, z_ref, u_ref, y_ref):
    cells, channels = x_ref.shape
    half = cells // 2
    tile = channels // 2
    totals = [x_ref[:, k * tile:(k + 1) * tile].astype(F32) + bias[:, k * tile:(k + 1) * tile] for k in range(2)]
    for step, a in enumerate(ROW_STEPS):
        wait_weights(step)
        for b in range(3):
            if a == 0:
                lhs = z_ref[b]
            else:
                first = 0 if a < 0 else 2 * SLOT_COLS
                lhs = jnp.concatenate([u_ref[b, h, first:first + half, :] for h in range(2)], axis=0)
            base = (3 * (a + 1) + b) * channels
            for k in range(2):
                totals[k] = totals[k] + jnp.dot(lhs, wbuf[base:base + channels, k * tile:(k + 1) * tile],
                                                preferred_element_type=F32)
                yield
    for k in range(2):
        y_ref[:, k * tile:(k + 1) * tile] = totals[k].astype(BF16)
    yield


def drain(steps):
    for _ in steps:
        pass


def interleave(main, *others):
    for _ in main:
        for steps in others:
            next(steps, None)
    for steps in others:
        drain(steps)


def norm_second_steps(y_ref, joined, gain, shift, same_group):
    cells, channels = y_ref.shape
    half = cells // 2
    chunks = channels // LANES
    count = half * (channels // GROUPS)
    parts = []
    for k in range(chunks):
        lanes = slice(k * LANES, (k + 1) * LANES)
        inner = y_ref[:, lanes].astype(F32)
        t0, q0 = half_stats(inner[:half])
        t1, q1 = half_stats(inner[half:])
        parts.append(jnp.concatenate([t0, t1, q0, q1], axis=0))
        yield
    scale, offset = affine(jnp.concatenate(parts, axis=1), joined, gain, shift, same_group, count)
    for k in range(chunks):
        lanes = slice(k * LANES, (k + 1) * LANES)
        y = y_ref[:, lanes].astype(F32)
        v = jnp.concatenate([y[:half] * scale[0:1, lanes] + offset[0:1, lanes],
                             y[half:] * scale[1:2, lanes] + offset[1:2, lanes]], axis=0)
        y_ref[:, lanes] = (v + v * jnp.tanh(v)).astype(BF16)
        yield


def to_patches_steps(store, y_ref, joined, table_ref, bias, gather):
    cells, channels = y_ref.shape
    rows = cells // SLOT_COLS
    mid = rows // 2
    tokens = gather.shape[0]
    lat = channels // GROUPS
    keep = jnp.where(joined, 1.0, 0.0).astype(F32)
    column = lax.broadcasted_iota(jnp.int32, (1, SLOT_COLS, 1), 1)
    block = whole(lax.broadcasted_iota(jnp.int32, (1, SLOT_COLS, LANES), 2), lat)
    taps = jnp.dot(y_ref[...], table_ref[...], preferred_element_type=F32)
    yield
    from_left, here, from_right = (taps[:, k * LANES:(k + 1) * LANES].reshape(rows, SLOT_COLS, LANES) for k in range(3))
    moved = here + jnp.where(column == 0, 0.0, pltpu.roll(from_left, 1, 1))
    moved = moved + jnp.where(column == SLOT_COLS - 1, 0.0, pltpu.roll(from_right, SLOT_COLS - 1, 1))
    yield
    blank = jnp.zeros((1, SLOT_COLS, LANES), F32)
    above = jnp.concatenate([blank, moved[:mid - 1], moved[mid - 1:mid] * keep, moved[mid:rows - 1]], axis=0)
    below = jnp.concatenate([moved[1:mid], moved[mid:mid + 1] * keep, moved[mid + 1:], blank], axis=0)
    step_up = (block == 0) | (block == 3)
    step_none = (block == 1) | (block == 4)
    mixed = jnp.where(step_up, above, jnp.where(step_none, moved, below)).reshape(cells, LANES)
    yield
    latent = mixed + pltpu.roll(mixed, LANES - lat, 1) + pltpu.roll(mixed, LANES - 2 * lat, 1)
    latent = ((latent + bias) - LATENT_SHIFT) * LATENT_SCALE
    corner = block - part(lax.broadcasted_iota(jnp.int32, (1, SLOT_COLS, LANES), 1), 2)
    corner = jnp.concatenate([corner, corner - 2], axis=0)
    latent = latent.reshape(rows // 2, 2, SLOT_COLS, LANES)
    latent = jnp.where((corner == 0)[None], latent, 0.0).reshape(cells, LANES)
    yield
    store(jnp.dot(gather, latent.astype(BF16), preferred_element_type=F32)[:, :4 * lat].astype(BF16))
    yield


def patch_tables(lw_ref, bias_ref, table_ref, bias4_ref):
    lat = lw_ref.shape[0] // 9
    weight = lw_ref[...].astype(F32)
    blank = jnp.zeros((2 * lat, weight.shape[1]), F32)
    for b in range(3):
        blocks = [weight[(3 * a + b) * lat:(3 * a + b + 1) * lat] for a in range(3)]
        table_ref[:, b * LANES:(b + 1) * LANES] = jnp.concatenate(blocks * 2 + [blank], axis=0).T.astype(BF16)
    bias4_ref[...] = jnp.concatenate([bias_ref[...].reshape(1, lat)] * (LANES // lat), axis=1)


def whole(value, size):
    return value >> (size.bit_length() - 1)


def part(value, size):
    return value & (size - 1)


def group_table(channels):
    width = channels // GROUPS
    r = whole(lax.broadcasted_iota(jnp.int32, (LANES, LANES), 0), width)
    c = whole(lax.broadcasted_iota(jnp.int32, (LANES, LANES), 1), width)
    return jnp.where(r == c, 1.0, 0.0).astype(BF16)


def patch_table(cells):
    half_cols = SLOT_COLS // 2
    token = lax.broadcasted_iota(jnp.int32, (cells // 4, cells), 0)
    cell = lax.broadcasted_iota(jnp.int32, (cells // 4, cells), 1)
    own = whole(whole(cell, SLOT_COLS), 2) * half_cols + whole(part(cell, SLOT_COLS), 2)
    return jnp.where(own == token, 1.0, 0.0).astype(BF16)


def finish_steps(store, y_ref, joined, gain, shift, same_group, table_ref, bias4, gather):
    yield from norm_second_steps(y_ref, joined, gain, shift, same_group)
    yield from to_patches_steps(store, y_ref, joined, table_ref, bias4, gather)


FIRST = 1


def vector(ref):
    return ref[...].reshape(1, ref.shape[0])


def begin_kernel(kind_hbm, feat_hbm, bw_hbm, ew_hbm, eb_hbm, *rest):
    names = 7
    small_hbm, rest = rest[:names], rest[names:]
    state_ref, x_ref, w_ref, perm_ref, piece_ref, y_ref, z_ref, u_ref, *rest = rest
    small, rest = rest[:names - 2], rest[names - 2:]
    table_ref, bias4_ref, kind_ref, lw_ref, lb_ref, ew_ref, eb_ref, ksem, xsem, wsem, ssem = rest
    gain1, shift1, bias1 = small[:3]
    slots, cells, channels = x_ref.shape
    kcopy = pltpu.make_async_copy(kind_hbm, kind_ref, ksem)
    kcopy.start()
    xcopies = [pltpu.make_async_copy(feat_hbm.at[0, pl.ds(s * cells, cells), :], x_ref.at[s], xsem.at[s])
               for s in range(slots)]
    depth = 3 * channels
    wcopies = [pltpu.make_async_copy(
        bw_hbm.at[pl.ds((a + 1) * depth, depth), :], w_ref.at[pl.ds((a + 1) * depth, depth), :], wsem.at[i])
        for i, a in enumerate(ROW_STEPS)]
    scopies = [pltpu.make_async_copy(src, dst, ssem.at[i])
               for i, (src, dst) in enumerate(zip(small_hbm + (ew_hbm, eb_hbm), small + [lw_ref, lb_ref, ew_ref, eb_ref]))]
    others = [k for k in range(slots) if k != FIRST]
    for c in [xcopies[FIRST]] + scopies + [xcopies[k] for k in others]:
        c.start()
    for c in wcopies:
        c.start(priority=1)
    perm_ref[...] = patch_table(cells)
    same_group = group_table(channels)
    kcopy.wait()
    live = jnp.int32(0)
    for s in range(slots):
        live = live + jnp.where(kind_ref[0, s] > 0, 1, 0).astype(jnp.int32)
        state_ref[2 + s] = kind_ref[0, s]
    state_ref[0] = live
    state_ref[1] = jnp.where(live > 2, 2, 0)
    for c in scopies + [xcopies[FIRST]]:
        c.wait()
    feats = ew_ref.shape[0]
    piece_ref[0:feats, :] = ew_ref[...]
    piece_ref[feats:, :] = jnp.broadcast_to(vector(eb_ref), (piece_ref.shape[0] - feats, ew_ref.shape[1]))

    def first_norm(k):
        return norm_first_steps(x_ref.at[k], kind_ref[0, k] == 2, vector(gain1), vector(shift1), same_group,
                                z_ref.at[k], u_ref.at[k])

    def side_work():
        for k in others:
            yield from first_norm(k)
        patch_tables(lw_ref, lb_ref, table_ref, bias4_ref)
        yield

    drain(first_norm(FIRST))
    for k in others:
        xcopies[k].wait()
    interleave(conv_steps(x_ref.at[FIRST], vector(bias1), w_ref, lambda step: wcopies[step].wait(),
                          z_ref.at[FIRST], u_ref.at[FIRST], y_ref), side_work())


def second_norm(y_ref, kind, small):
    return norm_second_steps(y_ref, kind == 2, vector(small[3]), vector(small[4]), group_table(y_ref.shape[1]))


def patches(store, y_ref, kind, small, perm_ref):
    return to_patches_steps(store, y_ref, kind == 2, small[5], small[6][...], perm_ref[...])


def chain(*parts):
    for steps in parts:
        yield from steps


def count_live(kind_ref):
    total = jnp.int32(-2)
    for s in range(kind_ref.shape[1]):
        total = total + jnp.where(kind_ref[0, s] > 0, 1, 0).astype(jnp.int32)
    return total


def middle_kernel(offsets, state_ref, x_ref, w_ref, perm_ref, first_ref, z_ref, u_ref, *rest):
    names = 7
    small, rest = rest[:names], rest[names:]
    others, rest = rest[:len(offsets)], rest[len(offsets):]
    message_ref, sums_ref, *rest = rest
    early_ref, y_ref, *rest = rest
    kinds, ksem = rest[:-1], rest[-1]
    copies = [pltpu.make_async_copy(src, dst, ksem.at[i]) for i, (src, dst) in enumerate(zip(others, kinds))]
    for c in copies:
        c.start()
    tokens = first_ref.shape[0] // 4
    feats = message_ref.shape[1] // 2
    slot = state_ref[1]
    early_ref[...] = first_ref[...]
    found = {}

    def keep_as(name):
        def store(value):
            found[name] = value
        return store

    kind, early_kind = state_ref[2 + slot], state_ref[2 + FIRST]
    interleave(conv_steps(x_ref.at[slot], vector(small[2]), w_ref, lambda step: None, z_ref.at[slot], u_ref.at[slot],
                          y_ref), second_norm(early_ref, early_kind, small))
    interleave(chain(second_norm(y_ref, kind, small), patches(keep_as("second"), y_ref, kind, small, perm_ref)),
               patches(keep_as("first"), early_ref, early_kind, small, perm_ref))
    first_is_last = state_ref[0] == 2
    last = jnp.where(first_is_last, found["first"], found["second"])
    before = jnp.where(first_is_last, found["second"], found["first"])
    message_ref[0:tokens, :] = jnp.concatenate([last, before], axis=1)
    for c in copies:
        c.wait()
    position = lax.axis_index("seq")
    mine = state_ref[0] - 2
    below, above = jnp.int32(0), mine
    for offset, kind_ref in zip(offsets, kinds):
        other = count_live(kind_ref)
        lower = (position ^ offset) < position
        below = below + jnp.where(lower, other, 0)
        above = above + jnp.where(lower, 0, other)
    first_half = position < lax.axis_size("seq") // 2
    passed = jnp.where(position % 2 == 0, mine, 0)
    sums_ref[0] = jnp.where(first_half, below, -above)
    told = jnp.where(first_half, below + passed, passed - above)
    message_ref[tokens:, :] = jnp.full((message_ref.shape[0] - tokens, 2 * feats), told.astype(F32)).astype(BF16)


def final_kernel(parts, state_ref, x_ref, w_ref, perm_ref, z_ref, u_ref, *rest):
    pieces, small, rest = rest[:parts], rest[parts:parts + 7], rest[parts + 7:]
    out_ref, embed_ref, y_ref = rest
    group = lax.axis_index("dp")
    width = pieces[0].shape[1]

    def lay_out():
        for j in range(parts):
            value = pieces[0][...]
            for k in range(1, parts):
                value = jnp.where((group ^ j) == k, pieces[k][...], value)
            embed_ref[:, j * width:(j + 1) * width] = value
            yield

    @pl.when(state_ref[0] > 2)
    def _():
        def store(value):
            out_ref[...] = value

        interleave(conv_steps(x_ref.at[0], vector(small[2]), w_ref, lambda step: None, z_ref.at[0], u_ref.at[0], y_ref),
                   lay_out())
        drain(second_norm(y_ref, state_ref[2], small))
        drain(patches(store, y_ref, state_ref[2], small, perm_ref))

    @pl.when(state_ref[0] <= 2)
    def _():
        drain(lay_out())
        out_ref[...] = jnp.zeros_like(out_ref)


def join_kernel(state_ref, sums_ref, own_ref, third_ref, odd_ref, even_ref, embed_ref, out_ref, source_ref, value_ref, sem):
    live = state_ref[0]
    odd = lax.axis_index("seq") % 2
    tokens, feats = third_ref.shape
    told = even_ref[tokens:, :].astype(F32)[0, 0].astype(jnp.int32)
    carry = sums_ref[0] + told
    for k, ref in enumerate((even_ref, odd_ref, own_ref)):
        source_ref[2 * k] = ref[0:tokens, 0:feats]
        source_ref[2 * k + 1] = ref[0:tokens, feats:]
    source_ref[6] = third_ref[...]
    weight = embed_ref[0:feats, :]
    bias = embed_ref[feats:feats + 1, :].astype(F32)
    copies = []
    for i in range(2):
        incoming = (1 - odd) * 2 + carry - 1 - i
        kept = 4 + live - 1 - (i - carry)
        patch = source_ref[jnp.clip(jnp.where(i < carry, incoming, kept), 0, 6)]
        value = jnp.dot(patch, weight, preferred_element_type=F32) + bias
        rows = pl.ds(i * tokens, tokens)
        value_ref[rows, :] = value.astype(BF16)
        copies.append(pltpu.make_async_copy(value_ref.at[rows, :], out_ref.at[0, rows, :], sem.at[i]))
        copies[i].start()
    for c in copies:
        c.wait()


def exchange(value, axis, offset):
    count = lax.axis_size(axis)
    return lax.ppermute(value, axis, [(i, i ^ offset) for i in range(count)])


def swap_odd_pairs(value):
    groups, count = lax.axis_size("dp"), lax.axis_size("seq")
    pairs = []
    for g in range(groups):
        pairs += [(g * count + end, (g ^ 1) * count + end) for end in (0, count - 1)]
        for i in range(1, count - 1, 2):
            pairs += [(g * count + i, g * count + i + 1), (g * count + i + 1, g * count + i)]
    return lax.ppermute(value, ("dp", "seq"), pairs)


VMEM_SPEC = pl.BlockSpec(memory_space=pltpu.VMEM)
SMEM_SPEC = pl.BlockSpec(memory_space=pltpu.SMEM)
ANY_SPEC = pl.BlockSpec(memory_space=pl.ANY)
MIB = 1024 * 1024


def cost(flops, moved):
    return pl.CostEstimate(flops=flops, bytes_accessed=moved, transcendentals=0)


def encode_flops(cells, channels, lat):
    return cells * channels * 2 * 9 * (channels + lat)


def begin(features, slot_kind, block_weight, embed_weight, embed_bias, small):
    slots = slot_kind.shape[1]
    channels = features.shape[2]
    cells = SLOT_ROWS * SLOT_COLS
    feats, width = embed_weight.shape
    flops = encode_flops(cells, channels, small[6].shape[0])
    return pl.pallas_call(
        begin_kernel,
        out_shape=[
            pltpu.SMEM((8,), jnp.int32),
            pltpu.VMEM((slots, cells, channels), BF16),
            pltpu.VMEM(block_weight.shape, BF16),
            pltpu.VMEM((cells // 4, cells), BF16),
            pltpu.VMEM((feats + 16, width), BF16),
            pltpu.VMEM((cells, channels), BF16),
            pltpu.VMEM((slots, 3, cells, channels), BF16),
            pltpu.VMEM((slots, 3, 2, cells // 2 + 2 * SLOT_COLS, channels), BF16),
        ] + [pltpu.VMEM(v.shape, v.dtype) for v in small[:5]]
        + [pltpu.VMEM((channels, 3 * LANES), BF16), pltpu.VMEM((1, LANES), F32)],
        in_specs=[ANY_SPEC] * (5 + len(small)),
        out_specs=[SMEM_SPEC] + [VMEM_SPEC] * (7 + len(small)),
        scratch_shapes=[
            pltpu.SMEM(slot_kind.shape, jnp.int32),
            pltpu.VMEM(small[5].shape, BF16),
            pltpu.VMEM(small[6].shape, F32),
            pltpu.VMEM(embed_weight.shape, BF16),
            pltpu.VMEM(embed_bias.shape, BF16),
            pltpu.SemaphoreType.DMA,
            pltpu.SemaphoreType.DMA((slots,)),
            pltpu.SemaphoreType.DMA((3,)),
            pltpu.SemaphoreType.DMA((len(small) + 2,)),
        ],
        compiler_params=pltpu.CompilerParams(vmem_limit_bytes=50 * MIB),
        cost_estimate=cost(flops, block_weight.size * 2),
        name="begin",
    )(slot_kind, features, block_weight, embed_weight, embed_bias, *small)


def local(features, slot_kind, block_gain, block_shift, block_weight, block_bias, final_gain, final_shift,
          latent_weight, latent_bias, embed_weight, embed_bias):
    seq, dp = lax.axis_size("seq"), lax.axis_size("dp")
    channels = features.shape[2]
    cells = SLOT_ROWS * SLOT_COLS
    tokens = cells // 4
    feats, width = embed_weight.shape
    small = (block_gain, block_shift, block_bias, final_gain, final_shift, latent_weight.T, latent_bias)
    offsets = tuple(range(2, seq // 2, 2))
    others = [exchange(slot_kind, "seq", offset) for offset in offsets]
    slot_buffer = pltpu.VMEM((cells, channels), BF16)
    flops = encode_flops(cells, channels, latent_bias.shape[0])
    state, x, w, perm, piece, first, z, u, *small = begin(features, slot_kind, block_weight, embed_weight, embed_bias, small)
    message, sums = pl.pallas_call(
        functools.partial(middle_kernel, offsets),
        out_shape=[jax.ShapeDtypeStruct((tokens + 16, 2 * feats), BF16), pltpu.SMEM((1,), jnp.int32)],
        in_specs=[SMEM_SPEC] + [VMEM_SPEC] * (6 + len(small)) + [ANY_SPEC] * len(others),
        out_specs=[VMEM_SPEC, SMEM_SPEC],
        scratch_shapes=[slot_buffer] * 2 + [pltpu.SMEM(slot_kind.shape, jnp.int32) for _ in others]
        + [pltpu.SemaphoreType.DMA((len(others),))],
        compiler_params=pltpu.CompilerParams(vmem_limit_bytes=16 * MIB),
        cost_estimate=cost(flops, block_weight.size * 2),
        name="middle",
    )(state, x, w, perm, first, z, u, *small, *others)
    even = exchange(message, "seq", 1)
    odd = swap_odd_pairs(message)
    pieces = [piece] + [exchange(piece, "dp", offset) for offset in range(1, dp)]
    third, embed = pl.pallas_call(
        functools.partial(final_kernel, dp),
        out_shape=[pltpu.VMEM((tokens, feats), BF16), pltpu.VMEM((feats + 16, dp * width), BF16)],
        in_specs=[SMEM_SPEC] + [VMEM_SPEC] * (5 + dp + len(small)),
        out_specs=[VMEM_SPEC] * 2,
        scratch_shapes=[slot_buffer],
        compiler_params=pltpu.CompilerParams(vmem_limit_bytes=16 * MIB),
        cost_estimate=cost(flops, block_weight.size * 2),
        name="final",
    )(state, x, w, perm, z, u, *pieces, *small)
    return pl.pallas_call(
        join_kernel,
        out_shape=jax.ShapeDtypeStruct((1, 2 * tokens, dp * width), BF16),
        in_specs=[SMEM_SPEC] * 2 + [VMEM_SPEC] * 5,
        out_specs=ANY_SPEC,
        scratch_shapes=[pltpu.VMEM((7, tokens, feats), BF16), pltpu.VMEM((2 * tokens, dp * width), BF16),
                        pltpu.SemaphoreType.DMA((2,))],
        compiler_params=pltpu.CompilerParams(vmem_limit_bytes=8 * MIB),
        cost_estimate=cost(4 * tokens * feats * dp * width, 4 * tokens * dp * width),
        name="join",
    )(state, sums, message, third, odd, even, embed)


def solution(mesh):
    in_specs = (P("dp", "seq", None), P("dp", "seq")) + (P(),) * 8 + (P(None, "dp"), P("dp"))
    return jax.shard_map(local, mesh=mesh, in_specs=in_specs, out_specs=P("dp", "seq", None), check_vma=False)
```

```python
import functools
import jax
import jax.numpy as jnp
from jax import lax
from jax.sharding import PartitionSpec as P
from jax.sharding import PartitionSpec as P
from jax.experimental import pallas as pl
from jax.experimental.pallas import tpu as pltpu

GROUPS = 32
SLOT_ROWS = 32
SLOT_COLS = 8
LATENT_SHIFT = 0.0609
LATENT_SCALE = 1.5305
NORM_EPSILON = 1e-06
LANES = 128
ROW_STEPS = (0, -1, 1)
VMEM_BYTES = 64 * 1024 * 1024
F32 = jnp.float32
BF16 = jnp.bfloat16


def group_total(stats, same_group):
    rows, channels = stats.shape
    chunks = channels // LANES
    packed = jnp.concatenate([stats[:, k * LANES:(k + 1) * LANES] for k in range(chunks)], axis=0)
    high = packed.astype(BF16)
    rest = packed - high.astype(F32)
    middle = rest.astype(BF16)
    low = (rest - middle.astype(F32)).astype(BF16)
    total = sum(jnp.dot(piece, same_group, preferred_element_type=F32) for piece in (high, middle, low))
    return jnp.concatenate([total[k * rows:(k + 1) * rows] for k in range(chunks)], axis=1)


def affine(stats, joined, gain, shift, same_group, count):
    total = group_total(stats, same_group)
    mean, square = total[0:2] * (1.0 / count), total[2:4] * (1.0 / count)
    both_mean = 0.5 * (mean[0:1] + mean[1:2])
    both_square = 0.5 * (square[0:1] + square[1:2])
    mean = jnp.where(joined, both_mean, mean)
    square = jnp.where(joined, both_square, square)
    spread = jnp.maximum(square - mean * mean, 0.0)
    scale = lax.rsqrt(spread + NORM_EPSILON) * (0.5 * gain)
    return scale, 0.5 * shift - mean * scale


def half_stats(half):
    total = jnp.sum(half, axis=0, keepdims=True)
    return total, jnp.sum(half * half, axis=0, keepdims=True)


def norm_first_steps(x_ref, joined, gain, shift, same_group, z_ref, u_ref):
    cells, channels = x_ref.shape
    half = cells // 2
    rows = cells // SLOT_COLS
    chunks = channels // LANES
    count = half * (channels // GROUPS)
    keep = jnp.where(joined, 1.0, 0.0).astype(F32)
    column = lax.broadcasted_iota(jnp.int32, (1, SLOT_COLS, 1), 1)
    parts = []
    for k in range(chunks):
        x = x_ref[:, k * LANES:(k + 1) * LANES].astype(F32)
        t0, q0 = half_stats(x[:half])
        t1, q1 = half_stats(x[half:])
        parts.append(jnp.concatenate([t0, t1, q0, q1], axis=0))
        yield
    scale, offset = affine(jnp.concatenate(parts, axis=1), joined, gain, shift, same_group, count)
    zero = jnp.zeros((SLOT_COLS, LANES), F32)
    for k in range(chunks):
        lanes = slice(k * LANES, (k + 1) * LANES)
        x = x_ref[:, lanes].astype(F32)
        v = jnp.concatenate([x[:half] * scale[0:1, lanes] + offset[0:1, lanes],
                             x[half:] * scale[1:2, lanes] + offset[1:2, lanes]], axis=0)
        act = v + v * jnp.tanh(v)
        act3 = act.reshape(rows, SLOT_COLS, LANES)
        left = jnp.where(column == 0, 0.0, pltpu.roll(act3, 1, 1)).reshape(cells, LANES)
        right = jnp.where(column == SLOT_COLS - 1, 0.0, pltpu.roll(act3, SLOT_COLS - 1, 1)).reshape(cells, LANES)
        for b, value in enumerate((left, act, right)):
            z_ref[b, :, lanes] = value.astype(BF16)
            over = value[half:half + SLOT_COLS] * keep
            under = value[half - SLOT_COLS:half] * keep
            u_ref[b, 0, :, lanes] = jnp.concatenate([zero, value[:half], over], axis=0).astype(BF16)
            u_ref[b, 1, :, lanes] = jnp.concatenate([under, value[half:], zero], axis=0).astype(BF16)
        yield


def conv_steps(x_ref, bias, wbuf, wait_weights, z_ref, u_ref, y_ref):
    cells, channels = x_ref.shape
    half = cells // 2
    tile = channels // 2
    totals = [x_ref[:, k * tile:(k + 1) * tile].astype(F32) + bias[:, k * tile:(k + 1) * tile] for k in range(2)]
    for step, a in enumerate(ROW_STEPS):
        wait_weights(step)
        for b in range(3):
            if a == 0:
                lhs = z_ref[b]
            else:
                first = 0 if a < 0 else 2 * SLOT_COLS
                lhs = jnp.concatenate([u_ref[b, h, first:first + half, :] for h in range(2)], axis=0)
            base = (3 * (a + 1) + b) * channels
            for k in range(2):
                totals[k] = totals[k] + jnp.dot(lhs, wbuf[base:base + channels, k * tile:(k + 1) * tile],
                                                preferred_element_type=F32)
                yield
    for k in range(2):
        y_ref[:, k * tile:(k + 1) * tile] = totals[k].astype(BF16)
    yield


def drain(steps):
    for _ in steps:
        pass


def interleave(main, *others):
    for _ in main:
        for steps in others:
            next(steps, None)
    for steps in others:
        drain(steps)


def norm_second_steps(y_ref, joined, gain, shift, same_group):
    cells, channels = y_ref.shape
    half = cells // 2
    chunks = channels // LANES
    count = half * (channels // GROUPS)
    parts = []
    for k in range(chunks):
        lanes = slice(k * LANES, (k + 1) * LANES)
        inner = y_ref[:, lanes].astype(F32)
        t0, q0 = half_stats(inner[:half])
        t1, q1 = half_stats(inner[half:])
        parts.append(jnp.concatenate([t0, t1, q0, q1], axis=0))
        yield
    scale, offset = affine(jnp.concatenate(parts, axis=1), joined, gain, shift, same_group, count)
    for k in range(chunks):
        lanes = slice(k * LANES, (k + 1) * LANES)
        y = y_ref[:, lanes].astype(F32)
        v = jnp.concatenate([y[:half] * scale[0:1, lanes] + offset[0:1, lanes],
                             y[half:] * scale[1:2, lanes] + offset[1:2, lanes]], axis=0)
        y_ref[:, lanes] = (v + v * jnp.tanh(v)).astype(BF16)
        yield


def to_patches_steps(store, y_ref, joined, table_ref, bias, gather):
    cells, channels = y_ref.shape
    rows = cells // SLOT_COLS
    mid = rows // 2
    tokens = gather.shape[0]
    lat = channels // GROUPS
    keep = jnp.where(joined, 1.0, 0.0).astype(F32)
    column = lax.broadcasted_iota(jnp.int32, (1, SLOT_COLS, 1), 1)
    block = whole(lax.broadcasted_iota(jnp.int32, (1, SLOT_COLS, LANES), 2), lat)
    taps = jnp.dot(y_ref[...], table_ref[...], preferred_element_type=F32)
    yield
    from_left, here, from_right = (taps[:, k * LANES:(k + 1) * LANES].reshape(rows, SLOT_COLS, LANES) for k in range(3))
    moved = here + jnp.where(column == 0, 0.0, pltpu.roll(from_left, 1, 1))
    moved = moved + jnp.where(column == SLOT_COLS - 1, 0.0, pltpu.roll(from_right, SLOT_COLS - 1, 1))
    yield
    blank = jnp.zeros((1, SLOT_COLS, LANES), F32)
    above = jnp.concatenate([blank, moved[:mid - 1], moved[mid - 1:mid] * keep, moved[mid:rows - 1]], axis=0)
    below = jnp.concatenate([moved[1:mid], moved[mid:mid + 1] * keep, moved[mid + 1:], blank], axis=0)
    step_up = (block == 0) | (block == 3)
    step_none = (block == 1) | (block == 4)
    mixed = jnp.where(step_up, above, jnp.where(step_none, moved, below)).reshape(cells, LANES)
    yield
    latent = mixed + pltpu.roll(mixed, LANES - lat, 1) + pltpu.roll(mixed, LANES - 2 * lat, 1)
    latent = ((latent + bias) - LATENT_SHIFT) * LATENT_SCALE
    corner = block - part(lax.broadcasted_iota(jnp.int32, (1, SLOT_COLS, LANES), 1), 2)
    corner = jnp.concatenate([corner, corner - 2], axis=0)
    latent = latent.reshape(rows // 2, 2, SLOT_COLS, LANES)
    latent = jnp.where((corner == 0)[None], latent, 0.0).reshape(cells, LANES)
    yield
    store(jnp.dot(gather, latent.astype(BF16), preferred_element_type=F32)[:, :4 * lat].astype(BF16))
    yield


def patch_tables(lw_ref, bias_ref, table_ref, bias4_ref):
    lat = lw_ref.shape[0] // 9
    weight = lw_ref[...].astype(F32)
    blank = jnp.zeros((2 * lat, weight.shape[1]), F32)
    for b in range(3):
        blocks = [weight[(3 * a + b) * lat:(3 * a + b + 1) * lat] for a in range(3)]
        table_ref[:, b * LANES:(b + 1) * LANES] = jnp.concatenate(blocks * 2 + [blank], axis=0).T.astype(BF16)
    bias4_ref[...] = jnp.concatenate([bias_ref[...].reshape(1, lat)] * (LANES // lat), axis=1)
    yield


def whole(value, size):
    return value >> (size.bit_length() - 1)


def part(value, size):
    return value & (size - 1)


def group_table(channels):
    width = channels // GROUPS
    r = whole(lax.broadcasted_iota(jnp.int32, (LANES, LANES), 0), width)
    c = whole(lax.broadcasted_iota(jnp.int32, (LANES, LANES), 1), width)
    return jnp.where(r == c, 1.0, 0.0).astype(BF16)


def patch_table(cells):
    half_cols = SLOT_COLS // 2
    token = lax.broadcasted_iota(jnp.int32, (cells // 4, cells), 0)
    cell = lax.broadcasted_iota(jnp.int32, (cells // 4, cells), 1)
    own = whole(whole(cell, SLOT_COLS), 2) * half_cols + whole(part(cell, SLOT_COLS), 2)
    return jnp.where(own == token, 1.0, 0.0).astype(BF16)


def finish_steps(store, y_ref, joined, gain, shift, same_group, table_ref, bias4, gather):
    yield from norm_second_steps(y_ref, joined, gain, shift, same_group)
    yield from to_patches_steps(store, y_ref, joined, table_ref, bias4, gather)


FIRST = 1


def vector(ref):
    return ref[...].reshape(1, ref.shape[0])


def begin_kernel(kind_hbm, feat_hbm, ew_hbm, eb_hbm, *rest):
    names = 7
    small_hbm, rest = rest[:names], rest[names:]
    state_ref, x_ref, perm_ref, piece_ref, z_ref, u_ref, *rest = rest
    small, rest = rest[:names - 2], rest[names - 2:]
    table_ref, bias4_ref, kind_ref, lw_ref, lb_ref, ew_ref, eb_ref, ksem, xsem, ssem = rest
    gain1, shift1 = small[:2]
    slots, cells, channels = x_ref.shape
    kcopy = pltpu.make_async_copy(kind_hbm, kind_ref, ksem)
    kcopy.start()
    xcopies = [pltpu.make_async_copy(feat_hbm.at[0, pl.ds(s * cells, cells), :], x_ref.at[s], xsem.at[s])
               for s in range(slots)]
    scopies = [pltpu.make_async_copy(src, dst, ssem.at[i])
               for i, (src, dst) in enumerate(zip(small_hbm + (ew_hbm, eb_hbm), small + [lw_ref, lb_ref, ew_ref, eb_ref]))]
    others = [k for k in range(slots) if k != FIRST]
    for c in [xcopies[FIRST]] + scopies + [xcopies[k] for k in others]:
        c.start()
    perm_ref[...] = patch_table(cells)
    same_group = group_table(channels)
    kcopy.wait()
    live = jnp.int32(0)
    for s in range(slots):
        live = live + jnp.where(kind_ref[0, s] > 0, 1, 0).astype(jnp.int32)
        state_ref[2 + s] = kind_ref[0, s]
    state_ref[0] = live
    second = jnp.where(live > 2, 2, 0)
    state_ref[1] = second
    for c in scopies + [xcopies[FIRST]]:
        c.wait()
    feats = ew_ref.shape[0]
    piece_ref[0:feats, :] = ew_ref[...]
    piece_ref[feats:, :] = jnp.broadcast_to(vector(eb_ref), (piece_ref.shape[0] - feats, ew_ref.shape[1]))

    interleave(norm_first_steps(x_ref.at[FIRST], kind_ref[0, FIRST] == 2, vector(gain1), vector(shift1), same_group,
                                z_ref, u_ref), patch_tables(lw_ref, lb_ref, table_ref, bias4_ref))
    for k in others:
        xcopies[k].wait()


def extra_kernel(state_ref, x_ref, gain_ref, shift_ref, piece_in, z_ref, u_ref, piece_ref):
    piece_ref[...] = piece_in[...]

    @pl.when(state_ref[0] > 2)
    def _():
        drain(norm_first_steps(x_ref.at[0], state_ref[2] == 2, vector(gain_ref), vector(shift_ref),
                               group_table(x_ref.shape[2]), z_ref, u_ref))


def second_norm(y_ref, kind, small):
    return norm_second_steps(y_ref, kind == 2, vector(small[3]), vector(small[4]), group_table(y_ref.shape[1]))


def patches(store, y_ref, kind, small, perm_ref):
    return to_patches_steps(store, y_ref, kind == 2, small[5], small[6][...], perm_ref[...])


def chain(*parts):
    for steps in parts:
        yield from steps


def count_live(kind_ref):
    total = jnp.int32(-2)
    for s in range(kind_ref.shape[1]):
        total = total + jnp.where(kind_ref[0, s] > 0, 1, 0).astype(jnp.int32)
    return total


def middle_kernel(offsets, state_ref, x_ref, w_ref, perm_ref, z_ref, u_ref, *rest):
    names = 7
    small, rest = rest[:names], rest[names:]
    others, rest = rest[:len(offsets)], rest[len(offsets):]
    message_ref, sums_ref, *rest = rest
    early_ref, y_ref, z2_ref, u2_ref, *rest = rest
    kinds, ksem = rest[:-1], rest[-1]
    copies = [pltpu.make_async_copy(src, dst, ksem.at[i]) for i, (src, dst) in enumerate(zip(others, kinds))]
    for c in copies:
        c.start()
    tokens = x_ref.shape[1] // 4
    feats = message_ref.shape[1] // 2
    slot = state_ref[1]
    found = {}

    def keep_as(name):
        def store(value):
            found[name] = value
        return store

    kind, early_kind = state_ref[2 + slot], state_ref[2 + FIRST]
    interleave(conv_steps(x_ref.at[FIRST], vector(small[2]), w_ref, lambda step: None, z_ref, u_ref, early_ref),
               norm_first_steps(x_ref.at[slot], kind == 2, vector(small[0]), vector(small[1]),
                                group_table(x_ref.shape[2]), z2_ref, u2_ref))
    interleave(conv_steps(x_ref.at[slot], vector(small[2]), w_ref, lambda step: None, z2_ref, u2_ref,
                          y_ref), second_norm(early_ref, early_kind, small))
    interleave(chain(second_norm(y_ref, kind, small), patches(keep_as("second"), y_ref, kind, small, perm_ref)),
               patches(keep_as("first"), early_ref, early_kind, small, perm_ref))
    first_is_last = state_ref[0] == 2
    last = jnp.where(first_is_last, found["first"], found["second"])
    before = jnp.where(first_is_last, found["second"], found["first"])
    message_ref[0:tokens, :] = jnp.concatenate([last, before], axis=1)
    for c in copies:
        c.wait()
    position = lax.axis_index("seq")
    mine = state_ref[0] - 2
    below, above = jnp.int32(0), mine
    for offset, kind_ref in zip(offsets, kinds):
        other = count_live(kind_ref)
        lower = (position ^ offset) < position
        below = below + jnp.where(lower, other, 0)
        above = above + jnp.where(lower, 0, other)
    first_half = position < lax.axis_size("seq") // 2
    passed = jnp.where(position % 2 == 0, mine, 0)
    sums_ref[0] = jnp.where(first_half, below, -above)
    told = jnp.where(first_half, below + passed, passed - above)
    message_ref[tokens:, :] = jnp.full((message_ref.shape[0] - tokens, 2 * feats), told.astype(F32)).astype(BF16)


def final_kernel(parts, state_ref, x_ref, w_ref, perm_ref, z_ref, u_ref, *rest):
    pieces, small, rest = rest[:parts], rest[parts:parts + 7], rest[parts + 7:]
    out_ref, embed_ref, y_ref = rest
    group = lax.axis_index("dp")
    width = pieces[0].shape[1]

    def lay_out():
        for j in range(parts):
            value = pieces[0][...]
            for k in range(1, parts):
                value = jnp.where((group ^ j) == k, pieces[k][...], value)
            embed_ref[:, j * width:(j + 1) * width] = value
            yield

    @pl.when(state_ref[0] > 2)
    def _():
        def store(value):
            out_ref[...] = value

        interleave(conv_steps(x_ref.at[0], vector(small[2]), w_ref, lambda step: None, z_ref, u_ref, y_ref),
                   lay_out())
        drain(second_norm(y_ref, state_ref[2], small))
        drain(patches(store, y_ref, state_ref[2], small, perm_ref))

    @pl.when(state_ref[0] <= 2)
    def _():
        drain(lay_out())
        out_ref[...] = jnp.zeros_like(out_ref)


def join_kernel(state_ref, sums_ref, own_ref, third_ref, odd_ref, even_ref, embed_ref, out_ref, source_ref, value_ref, sem):
    live = state_ref[0]
    odd = lax.axis_index("seq") % 2
    tokens, feats = third_ref.shape
    told = even_ref[tokens:, :].astype(F32)[0, 0].astype(jnp.int32)
    carry = sums_ref[0] + told
    for k, ref in enumerate((even_ref, odd_ref, own_ref)):
        source_ref[2 * k] = ref[0:tokens, 0:feats]
        source_ref[2 * k + 1] = ref[0:tokens, feats:]
    source_ref[6] = third_ref[...]
    weight = embed_ref[0:feats, :]
    bias = embed_ref[feats:feats + 1, :].astype(F32)
    copies = []
    for i in range(2):
        incoming = (1 - odd) * 2 + carry - 1 - i
        kept = 4 + live - 1 - (i - carry)
        patch = source_ref[jnp.clip(jnp.where(i < carry, incoming, kept), 0, 6)]
        value = jnp.dot(patch, weight, preferred_element_type=F32) + bias
        rows = pl.ds(i * tokens, tokens)
        value_ref[rows, :] = value.astype(BF16)
        copies.append(pltpu.make_async_copy(value_ref.at[rows, :], out_ref.at[0, rows, :], sem.at[i]))
        copies[i].start()
    for c in copies:
        c.wait()


def exchange(value, axis, offset):
    count = lax.axis_size(axis)
    return lax.ppermute(value, axis, [(i, i ^ offset) for i in range(count)])


def swap_odd_pairs(value):
    groups, count = lax.axis_size("dp"), lax.axis_size("seq")
    pairs = []
    for g in range(groups):
        pairs += [(g * count + end, (g ^ 1) * count + end) for end in (0, count - 1)]
        for i in range(1, count - 1, 2):
            pairs += [(g * count + i, g * count + i + 1), (g * count + i + 1, g * count + i)]
    return lax.ppermute(value, ("dp", "seq"), pairs)


VMEM_SPEC = pl.BlockSpec(memory_space=pltpu.VMEM)
SMEM_SPEC = pl.BlockSpec(memory_space=pltpu.SMEM)
ANY_SPEC = pl.BlockSpec(memory_space=pl.ANY)
MIB = 1024 * 1024


def cost(flops, moved):
    return pl.CostEstimate(flops=flops, bytes_accessed=moved, transcendentals=0)


def encode_flops(cells, channels, lat):
    return cells * channels * 2 * 9 * (channels + lat)


def begin(features, slot_kind, embed_weight, embed_bias, small):
    slots = slot_kind.shape[1]
    channels = features.shape[2]
    cells = SLOT_ROWS * SLOT_COLS
    feats, width = embed_weight.shape
    return pl.pallas_call(
        begin_kernel,
        out_shape=[
            pltpu.SMEM((8,), jnp.int32),
            pltpu.VMEM((slots, cells, channels), BF16),
            pltpu.VMEM((cells // 4, cells), BF16),
            pltpu.VMEM((feats + 16, width), BF16),
            pltpu.VMEM((3, cells, channels), BF16),
            pltpu.VMEM((3, 2, cells // 2 + 2 * SLOT_COLS, channels), BF16),
        ] + [pltpu.VMEM(v.shape, v.dtype) for v in small[:5]]
        + [pltpu.VMEM((channels, 3 * LANES), BF16), pltpu.VMEM((1, LANES), F32)],
        in_specs=[ANY_SPEC] * (4 + len(small)),
        out_specs=[SMEM_SPEC] + [VMEM_SPEC] * (5 + len(small)),
        scratch_shapes=[
            pltpu.SMEM(slot_kind.shape, jnp.int32),
            pltpu.VMEM(small[5].shape, BF16),
            pltpu.VMEM(small[6].shape, F32),
            pltpu.VMEM(embed_weight.shape, BF16),
            pltpu.VMEM(embed_bias.shape, BF16),
            pltpu.SemaphoreType.DMA,
            pltpu.SemaphoreType.DMA((slots,)),
            pltpu.SemaphoreType.DMA((len(small) + 2,)),
        ],
        compiler_params=pltpu.CompilerParams(vmem_limit_bytes=60 * MIB),
        cost_estimate=cost(0, features.size),
        name="begin",
    )(slot_kind, features, embed_weight, embed_bias, *small)


def local(features, slot_kind, block_gain, block_shift, block_weight, block_bias, final_gain, final_shift,
          latent_weight, latent_bias, embed_weight, embed_bias):
    seq, dp = lax.axis_size("seq"), lax.axis_size("dp")
    channels = features.shape[2]
    cells = SLOT_ROWS * SLOT_COLS
    tokens = cells // 4
    feats, width = embed_weight.shape
    small = (block_gain, block_shift, block_bias, final_gain, final_shift, latent_weight.T, latent_bias)
    offsets = tuple(range(2, seq // 2, 2))
    others = [exchange(slot_kind, "seq", offset) for offset in offsets]
    slot_buffer = pltpu.VMEM((cells, channels), BF16)
    flops = encode_flops(cells, channels, latent_bias.shape[0])
    state, x, perm, piece, z, u, *small = begin(features, slot_kind, embed_weight, embed_bias, small)
    z3, u3, piece = pl.pallas_call(
        extra_kernel,
        out_shape=[pltpu.VMEM(z.shape, BF16), pltpu.VMEM(u.shape, BF16), pltpu.VMEM(piece.shape, BF16)],
        in_specs=[SMEM_SPEC] + [VMEM_SPEC] * 4,
        out_specs=[VMEM_SPEC] * 3,
        compiler_params=pltpu.CompilerParams(vmem_limit_bytes=16 * MIB),
        cost_estimate=cost(2 * flops, features.size),
        name="extra",
    )(state, x, *small[:2], piece)
    message, sums = pl.pallas_call(
        functools.partial(middle_kernel, offsets),
        out_shape=[jax.ShapeDtypeStruct((tokens + 16, 2 * feats), BF16), pltpu.SMEM((1,), jnp.int32)],
        in_specs=[SMEM_SPEC] + [VMEM_SPEC] * (5 + len(small)) + [ANY_SPEC] * len(others),
        out_specs=[VMEM_SPEC, SMEM_SPEC],
        scratch_shapes=[slot_buffer] * 2 + [pltpu.VMEM(z.shape, BF16), pltpu.VMEM(u.shape, BF16)] + [pltpu.SMEM(slot_kind.shape, jnp.int32) for _ in others]
        + [pltpu.SemaphoreType.DMA((len(others),))],
        compiler_params=pltpu.CompilerParams(vmem_limit_bytes=16 * MIB),
        cost_estimate=cost(flops, block_weight.size * 2),
        name="middle",
    )(state, x, block_weight, perm, z, u, *small, *others)
    even = exchange(message, "seq", 1)
    odd = swap_odd_pairs(message)
    pieces = [piece] + [exchange(piece, "dp", offset) for offset in range(1, dp)]
    third, embed = pl.pallas_call(
        functools.partial(final_kernel, dp),
        out_shape=[pltpu.VMEM((tokens, feats), BF16), pltpu.VMEM((feats + 16, dp * width), BF16)],
        in_specs=[SMEM_SPEC] + [VMEM_SPEC] * (5 + dp + len(small)),
        out_specs=[VMEM_SPEC] * 2,
        scratch_shapes=[slot_buffer],
        compiler_params=pltpu.CompilerParams(vmem_limit_bytes=16 * MIB),
        cost_estimate=cost(flops, block_weight.size * 2),
        name="final",
    )(state, x, block_weight, perm, z3, u3, *pieces, *small)
    return pl.pallas_call(
        join_kernel,
        out_shape=jax.ShapeDtypeStruct((1, 2 * tokens, dp * width), BF16),
        in_specs=[SMEM_SPEC] * 2 + [VMEM_SPEC] * 5,
        out_specs=ANY_SPEC,
        scratch_shapes=[pltpu.VMEM((7, tokens, feats), BF16), pltpu.VMEM((2 * tokens, dp * width), BF16),
                        pltpu.SemaphoreType.DMA((2,))],
        compiler_params=pltpu.CompilerParams(vmem_limit_bytes=8 * MIB),
        cost_estimate=cost(4 * tokens * feats * dp * width, 4 * tokens * dp * width),
        name="join",
    )(state, sums, message, third, odd, even, embed)


def solution(mesh):
    in_specs = (P("dp", "seq", None), P("dp", "seq")) + (P(),) * 8 + (P(None, "dp"), P("dp"))
    return jax.shard_map(local, mesh=mesh, in_specs=in_specs, out_specs=P("dp", "seq", None), check_vma=False)
```

```python
import functools
import jax
import jax.numpy as jnp
from jax import lax
from jax.sharding import PartitionSpec as P
from jax.sharding import PartitionSpec as P
from jax.experimental import pallas as pl
from jax.experimental.pallas import tpu as pltpu

GROUPS = 32
SLOT_ROWS = 32
SLOT_COLS = 8
LATENT_SHIFT = 0.0609
LATENT_SCALE = 1.5305
NORM_EPSILON = 1e-06
LANES = 128
ROW_STEPS = (0, -1, 1)
VMEM_BYTES = 64 * 1024 * 1024
F32 = jnp.float32
BF16 = jnp.bfloat16


def group_total(stats, same_group):
    rows, channels = stats.shape
    chunks = channels // LANES
    packed = jnp.concatenate([stats[:, k * LANES:(k + 1) * LANES] for k in range(chunks)], axis=0)
    high = packed.astype(BF16)
    rest = packed - high.astype(F32)
    middle = rest.astype(BF16)
    low = (rest - middle.astype(F32)).astype(BF16)
    total = sum(jnp.dot(piece, same_group, preferred_element_type=F32) for piece in (high, middle, low))
    return jnp.concatenate([total[k * rows:(k + 1) * rows] for k in range(chunks)], axis=1)


def affine(stats, joined, gain, shift, same_group, count):
    total = group_total(stats, same_group)
    mean, square = total[0:2] * (1.0 / count), total[2:4] * (1.0 / count)
    both_mean = 0.5 * (mean[0:1] + mean[1:2])
    both_square = 0.5 * (square[0:1] + square[1:2])
    mean = jnp.where(joined, both_mean, mean)
    square = jnp.where(joined, both_square, square)
    spread = jnp.maximum(square - mean * mean, 0.0)
    scale = lax.rsqrt(spread + NORM_EPSILON) * (0.5 * gain)
    return scale, 0.5 * shift - mean * scale


def half_stats(half):
    total = jnp.sum(half, axis=0, keepdims=True)
    return total, jnp.sum(half * half, axis=0, keepdims=True)


def norm_first_steps(x_ref, joined, gain, shift, same_group, z_ref, u_ref):
    cells, channels = x_ref.shape
    half = cells // 2
    rows = cells // SLOT_COLS
    chunks = channels // LANES
    count = half * (channels // GROUPS)
    keep = jnp.where(joined, 1.0, 0.0).astype(F32)
    column = lax.broadcasted_iota(jnp.int32, (1, SLOT_COLS, 1), 1)
    parts = []
    for k in range(chunks):
        x = x_ref[:, k * LANES:(k + 1) * LANES].astype(F32)
        t0, q0 = half_stats(x[:half])
        t1, q1 = half_stats(x[half:])
        parts.append(jnp.concatenate([t0, t1, q0, q1], axis=0))
        yield
    scale, offset = affine(jnp.concatenate(parts, axis=1), joined, gain, shift, same_group, count)
    zero = jnp.zeros((SLOT_COLS, LANES), F32)
    for k in range(chunks):
        lanes = slice(k * LANES, (k + 1) * LANES)
        x = x_ref[:, lanes].astype(F32)
        v = jnp.concatenate([x[:half] * scale[0:1, lanes] + offset[0:1, lanes],
                             x[half:] * scale[1:2, lanes] + offset[1:2, lanes]], axis=0)
        act = v + v * jnp.tanh(v)
        act3 = act.reshape(rows, SLOT_COLS, LANES)
        left = jnp.where(column == 0, 0.0, pltpu.roll(act3, 1, 1)).reshape(cells, LANES)
        right = jnp.where(column == SLOT_COLS - 1, 0.0, pltpu.roll(act3, SLOT_COLS - 1, 1)).reshape(cells, LANES)
        for b, value in enumerate((left, act, right)):
            z_ref[b, :, lanes] = value.astype(BF16)
            over = value[half:half + SLOT_COLS] * keep
            under = value[half - SLOT_COLS:half] * keep
            u_ref[b, 0, :, lanes] = jnp.concatenate([zero, value[:half], over], axis=0).astype(BF16)
            u_ref[b, 1, :, lanes] = jnp.concatenate([under, value[half:], zero], axis=0).astype(BF16)
        yield


def conv_steps(x_ref, bias, wbuf, wait_weights, z_ref, u_ref, y_ref):
    cells, channels = x_ref.shape
    half = cells // 2
    tile = channels // 2
    totals = [x_ref[:, k * tile:(k + 1) * tile].astype(F32) + bias[:, k * tile:(k + 1) * tile] for k in range(2)]
    for step, a in enumerate(ROW_STEPS):
        wait_weights(step)
        for b in range(3):
            if a == 0:
                lhs = z_ref[b]
            else:
                first = 0 if a < 0 else 2 * SLOT_COLS
                lhs = jnp.concatenate([u_ref[b, h, first:first + half, :] for h in range(2)], axis=0)
            base = (3 * (a + 1) + b) * channels
            for k in range(2):
                totals[k] = totals[k] + jnp.dot(lhs, wbuf[base:base + channels, k * tile:(k + 1) * tile],
                                                preferred_element_type=F32)
                yield
    for k in range(2):
        y_ref[:, k * tile:(k + 1) * tile] = totals[k].astype(BF16)
    yield


def drain(steps):
    for _ in steps:
        pass


def interleave(main, *others):
    for _ in main:
        for steps in others:
            next(steps, None)
    for steps in others:
        drain(steps)


def norm_second_steps(y_ref, joined, gain, shift, same_group):
    cells, channels = y_ref.shape
    half = cells // 2
    chunks = channels // LANES
    count = half * (channels // GROUPS)
    parts = []
    for k in range(chunks):
        lanes = slice(k * LANES, (k + 1) * LANES)
        inner = y_ref[:, lanes].astype(F32)
        t0, q0 = half_stats(inner[:half])
        t1, q1 = half_stats(inner[half:])
        parts.append(jnp.concatenate([t0, t1, q0, q1], axis=0))
        yield
    scale, offset = affine(jnp.concatenate(parts, axis=1), joined, gain, shift, same_group, count)
    for k in range(chunks):
        lanes = slice(k * LANES, (k + 1) * LANES)
        y = y_ref[:, lanes].astype(F32)
        v = jnp.concatenate([y[:half] * scale[0:1, lanes] + offset[0:1, lanes],
                             y[half:] * scale[1:2, lanes] + offset[1:2, lanes]], axis=0)
        y_ref[:, lanes] = (v + v * jnp.tanh(v)).astype(BF16)
        yield


def to_patches_steps(store, y_ref, joined, table_ref, bias, gather):
    cells, channels = y_ref.shape
    rows = cells // SLOT_COLS
    mid = rows // 2
    tokens = gather.shape[0]
    lat = channels // GROUPS
    keep = jnp.where(joined, 1.0, 0.0).astype(F32)
    column = lax.broadcasted_iota(jnp.int32, (1, SLOT_COLS, 1), 1)
    block = whole(lax.broadcasted_iota(jnp.int32, (1, SLOT_COLS, LANES), 2), lat)
    taps = jnp.dot(y_ref[...], table_ref[...], preferred_element_type=F32)
    yield
    from_left, here, from_right = (taps[:, k * LANES:(k + 1) * LANES].reshape(rows, SLOT_COLS, LANES) for k in range(3))
    moved = here + jnp.where(column == 0, 0.0, pltpu.roll(from_left, 1, 1))
    moved = moved + jnp.where(column == SLOT_COLS - 1, 0.0, pltpu.roll(from_right, SLOT_COLS - 1, 1))
    yield
    blank = jnp.zeros((1, SLOT_COLS, LANES), F32)
    above = jnp.concatenate([blank, moved[:mid - 1], moved[mid - 1:mid] * keep, moved[mid:rows - 1]], axis=0)
    below = jnp.concatenate([moved[1:mid], moved[mid:mid + 1] * keep, moved[mid + 1:], blank], axis=0)
    step_up = (block == 0) | (block == 3)
    step_none = (block == 1) | (block == 4)
    mixed = jnp.where(step_up, above, jnp.where(step_none, moved, below)).reshape(cells, LANES)
    yield
    latent = mixed + pltpu.roll(mixed, LANES - lat, 1) + pltpu.roll(mixed, LANES - 2 * lat, 1)
    latent = ((latent + bias) - LATENT_SHIFT) * LATENT_SCALE
    corner = block - part(lax.broadcasted_iota(jnp.int32, (1, SLOT_COLS, LANES), 1), 2)
    corner = jnp.concatenate([corner, corner - 2], axis=0)
    latent = latent.reshape(rows // 2, 2, SLOT_COLS, LANES)
    latent = jnp.where((corner == 0)[None], latent, 0.0).reshape(cells, LANES)
    yield
    store(jnp.dot(gather, latent.astype(BF16), preferred_element_type=F32)[:, :4 * lat].astype(BF16))
    yield


def patch_tables(lw_ref, bias_ref, table_ref, bias4_ref):
    lat = lw_ref.shape[0] // 9
    weight = lw_ref[...].astype(F32)
    blank = jnp.zeros((2 * lat, weight.shape[1]), F32)
    for b in range(3):
        blocks = [weight[(3 * a + b) * lat:(3 * a + b + 1) * lat] for a in range(3)]
        table_ref[:, b * LANES:(b + 1) * LANES] = jnp.concatenate(blocks * 2 + [blank], axis=0).T.astype(BF16)
    bias4_ref[...] = jnp.concatenate([bias_ref[...].reshape(1, lat)] * (LANES // lat), axis=1)
    yield


def whole(value, size):
    return value >> (size.bit_length() - 1)


def part(value, size):
    return value & (size - 1)


def group_table(channels):
    width = channels // GROUPS
    r = whole(lax.broadcasted_iota(jnp.int32, (LANES, LANES), 0), width)
    c = whole(lax.broadcasted_iota(jnp.int32, (LANES, LANES), 1), width)
    return jnp.where(r == c, 1.0, 0.0).astype(BF16)


def patch_table(cells):
    half_cols = SLOT_COLS // 2
    token = lax.broadcasted_iota(jnp.int32, (cells // 4, cells), 0)
    cell = lax.broadcasted_iota(jnp.int32, (cells // 4, cells), 1)
    own = whole(whole(cell, SLOT_COLS), 2) * half_cols + whole(part(cell, SLOT_COLS), 2)
    return jnp.where(own == token, 1.0, 0.0).astype(BF16)


def finish_steps(store, y_ref, joined, gain, shift, same_group, table_ref, bias4, gather):
    yield from norm_second_steps(y_ref, joined, gain, shift, same_group)
    yield from to_patches_steps(store, y_ref, joined, table_ref, bias4, gather)


FIRST = 1


def vector(ref):
    return ref[...].reshape(1, ref.shape[0])


def load_kernel(kind_hbm, feat_hbm, ew_hbm, eb_hbm, *rest):
    names = 7
    small_hbm, rest = rest[:names], rest[names:]
    state_ref, x_ref, piece_ref, *rest = rest
    small, rest = rest[:names], rest[names:]
    kind_ref, ew_ref, eb_ref, ksem, xsem, ssem = rest
    slots = kind_ref.shape[1]
    cells = x_ref.shape[0]
    kcopy = pltpu.make_async_copy(kind_hbm, kind_ref, ksem)
    kcopy.start()
    xcopy = pltpu.make_async_copy(feat_hbm.at[0, pl.ds(FIRST * cells, cells), :], x_ref, xsem)
    scopies = [pltpu.make_async_copy(src, dst, ssem.at[i])
               for i, (src, dst) in enumerate(zip(small_hbm + (ew_hbm, eb_hbm), small + [ew_ref, eb_ref]))]
    for c in [xcopy] + scopies:
        c.start()
    kcopy.wait()
    live = jnp.int32(0)
    for s in range(slots):
        live = live + jnp.where(kind_ref[0, s] > 0, 1, 0).astype(jnp.int32)
        state_ref[2 + s] = kind_ref[0, s]
    state_ref[0] = live
    state_ref[1] = jnp.where(live > 2, 2, 0)
    for c in scopies:
        c.wait()
    feats = ew_ref.shape[0]
    piece_ref[0:feats, :] = ew_ref[...]
    piece_ref[feats:, :] = jnp.broadcast_to(vector(eb_ref), (piece_ref.shape[0] - feats, ew_ref.shape[1]))
    xcopy.wait()


def begin_kernel(state_ref, x_ref, gain_ref, shift_ref, lw_ref, lb_ref, piece_in,
                 z_ref, u_ref, table_ref, bias4_ref, perm_ref, piece_ref):
    piece_ref[...] = piece_in[...]
    perm_ref[...] = patch_table(x_ref.shape[0])
    interleave(norm_first_steps(x_ref, state_ref[2 + FIRST] == 2, vector(gain_ref), vector(shift_ref),
                                group_table(x_ref.shape[1]), z_ref, u_ref),
               patch_tables(lw_ref, lb_ref, table_ref, bias4_ref))


def second_norm(y_ref, kind, small):
    return norm_second_steps(y_ref, kind == 2, vector(small[3]), vector(small[4]), group_table(y_ref.shape[1]))


def patches(store, y_ref, kind, small, perm_ref):
    return to_patches_steps(store, y_ref, kind == 2, small[5], small[6][...], perm_ref[...])


def chain(*parts):
    for steps in parts:
        yield from steps


def count_live(kind_ref):
    total = jnp.int32(-2)
    for s in range(kind_ref.shape[1]):
        total = total + jnp.where(kind_ref[0, s] > 0, 1, 0).astype(jnp.int32)
    return total


def middle_kernel(offsets, state_ref, x_ref, w_ref, perm_ref, z_ref, u_ref, *rest):
    names = 7
    small, rest = rest[:names], rest[names:]
    others, rest = rest[:len(offsets)], rest[len(offsets):]
    message_ref, sums_ref, z3_ref, u3_ref, *rest = rest
    early_ref, y_ref, z2_ref, u2_ref, *rest = rest
    kinds, ksem = rest[:-1], rest[-1]
    copies = [pltpu.make_async_copy(src, dst, ksem.at[i]) for i, (src, dst) in enumerate(zip(others, kinds))]
    for c in copies:
        c.start()
    cells = early_ref.shape[0]
    tokens = cells // 4
    feats = message_ref.shape[1] // 2
    slot = state_ref[1]

    def features_of(at):
        return x_ref.at[0, pl.ds(pl.multiple_of(at * cells, cells), cells), :]

    def first_norm(at, z_to, u_to):
        return norm_first_steps(features_of(at), state_ref[2 + at] == 2, vector(small[0]), vector(small[1]),
                                group_table(x_ref.shape[2]), z_to, u_to)

    def encode_two(with_third):
        found = {}

        def keep_as(name):
            def store(value):
                found[name] = value
            return store

        kind, early_kind = state_ref[2 + slot], state_ref[2 + FIRST]
        third = [first_norm(0, z3_ref, u3_ref)] if with_third else []
        interleave(conv_steps(features_of(FIRST), vector(small[2]), w_ref, lambda step: None, z_ref, u_ref, early_ref),
                   first_norm(slot, z2_ref, u2_ref))
        interleave(conv_steps(features_of(slot), vector(small[2]), w_ref, lambda step: None, z2_ref, u2_ref, y_ref),
                   chain(second_norm(early_ref, early_kind, small), *third))
        interleave(chain(second_norm(y_ref, kind, small), patches(keep_as("second"), y_ref, kind, small, perm_ref)),
                   patches(keep_as("first"), early_ref, early_kind, small, perm_ref))
        first_is_last = state_ref[0] == 2
        last = jnp.where(first_is_last, found["first"], found["second"])
        before = jnp.where(first_is_last, found["second"], found["first"])
        message_ref[0:tokens, :] = jnp.concatenate([last, before], axis=1)

    pl.when(state_ref[0] > 2)(lambda: encode_two(True))
    pl.when(state_ref[0] <= 2)(lambda: encode_two(False))
    for c in copies:
        c.wait()
    position = lax.axis_index("seq")
    mine = state_ref[0] - 2
    below, above = jnp.int32(0), mine
    for offset, kind_ref in zip(offsets, kinds):
        other = count_live(kind_ref)
        lower = (position ^ offset) < position
        below = below + jnp.where(lower, other, 0)
        above = above + jnp.where(lower, 0, other)
    first_half = position < lax.axis_size("seq") // 2
    passed = jnp.where(position % 2 == 0, mine, 0)
    sums_ref[0] = jnp.where(first_half, below, -above)
    told = jnp.where(first_half, below + passed, passed - above)
    message_ref[tokens:, :] = jnp.full((message_ref.shape[0] - tokens, 2 * feats), told.astype(F32)).astype(BF16)


def final_kernel(parts, state_ref, x_ref, w_ref, perm_ref, z_ref, u_ref, *rest):
    pieces, small, rest = rest[:parts], rest[parts:parts + 7], rest[parts + 7:]
    out_ref, embed_ref, y_ref = rest
    group = lax.axis_index("dp")
    width = pieces[0].shape[1]

    def lay_out():
        for j in range(parts):
            value = pieces[0][...]
            for k in range(1, parts):
                value = jnp.where((group ^ j) == k, pieces[k][...], value)
            embed_ref[:, j * width:(j + 1) * width] = value
            yield

    @pl.when(state_ref[0] > 2)
    def _():
        def store(value):
            out_ref[...] = value

        interleave(conv_steps(x_ref.at[0, 0:y_ref.shape[0], :], vector(small[2]), w_ref, lambda step: None, z_ref, u_ref, y_ref),
                   lay_out())
        drain(second_norm(y_ref, state_ref[2], small))
        drain(patches(store, y_ref, state_ref[2], small, perm_ref))

    @pl.when(state_ref[0] <= 2)
    def _():
        drain(lay_out())
        out_ref[...] = jnp.zeros_like(out_ref)


def join_kernel(state_ref, sums_ref, own_ref, third_ref, even_ref, odd_ref, embed_ref, out_ref, source_ref, value_ref, sem):
    live = state_ref[0]
    odd = lax.axis_index("seq") % 2
    tokens, feats = third_ref.shape
    told = even_ref[tokens:, :].astype(F32)[0, 0].astype(jnp.int32)
    carry = sums_ref[0] + told
    for k, ref in enumerate((even_ref, odd_ref, own_ref)):
        source_ref[2 * k] = ref[0:tokens, 0:feats]
        source_ref[2 * k + 1] = ref[0:tokens, feats:]
    source_ref[6] = third_ref[...]
    weight = embed_ref[0:feats, :]
    bias = embed_ref[feats:feats + 1, :].astype(F32)
    copies = []
    for i in range(2):
        incoming = (1 - odd) * 2 + carry - 1 - i
        kept = 4 + live - 1 - (i - carry)
        patch = source_ref[jnp.clip(jnp.where(i < carry, incoming, kept), 0, 6)]
        value = jnp.dot(patch, weight, preferred_element_type=F32) + bias
        rows = pl.ds(i * tokens, tokens)
        value_ref[rows, :] = value.astype(BF16)
        copies.append(pltpu.make_async_copy(value_ref.at[rows, :], out_ref.at[0, rows, :], sem.at[i]))
        copies[i].start()
    for c in copies:
        c.wait()


def exchange(value, axis, offset):
    count = lax.axis_size(axis)
    return lax.ppermute(value, axis, [(i, i ^ offset) for i in range(count)])


def swap_odd_pairs(value):
    groups, count = lax.axis_size("dp"), lax.axis_size("seq")
    pairs = []
    for g in range(groups):
        pairs += [(g * count + end, (g ^ 1) * count + end) for end in (0, count - 1)]
        for i in range(1, count - 1, 2):
            pairs += [(g * count + i, g * count + i + 1), (g * count + i + 1, g * count + i)]
    return lax.ppermute(value, ("dp", "seq"), pairs)


VMEM_SPEC = pl.BlockSpec(memory_space=pltpu.VMEM)
SMEM_SPEC = pl.BlockSpec(memory_space=pltpu.SMEM)
ANY_SPEC = pl.BlockSpec(memory_space=pl.ANY)
MIB = 1024 * 1024


def cost(flops, moved):
    return pl.CostEstimate(flops=flops, bytes_accessed=moved, transcendentals=0)


def encode_flops(cells, channels, lat):
    return cells * channels * 2 * 9 * (channels + lat)


def load(features, slot_kind, embed_weight, embed_bias, small):
    channels = features.shape[2]
    cells = SLOT_ROWS * SLOT_COLS
    feats, width = embed_weight.shape
    return pl.pallas_call(
        load_kernel,
        out_shape=[
            pltpu.SMEM((8,), jnp.int32),
            pltpu.VMEM((cells, channels), BF16),
            pltpu.VMEM((feats + 16, width), BF16),
        ] + [pltpu.VMEM(v.shape, v.dtype) for v in small],
        in_specs=[ANY_SPEC] * (4 + len(small)),
        out_specs=[SMEM_SPEC] + [VMEM_SPEC] * (2 + len(small)),
        scratch_shapes=[
            pltpu.SMEM(slot_kind.shape, jnp.int32),
            pltpu.VMEM(embed_weight.shape, BF16),
            pltpu.VMEM(embed_bias.shape, BF16),
            pltpu.SemaphoreType.DMA,
            pltpu.SemaphoreType.DMA,
            pltpu.SemaphoreType.DMA((len(small) + 2,)),
        ],
        compiler_params=pltpu.CompilerParams(vmem_limit_bytes=63 * MIB),
        cost_estimate=cost(0, features.size),
        name="load",
    )(slot_kind, features, embed_weight, embed_bias, *small)


def local(features, slot_kind, block_gain, block_shift, block_weight, block_bias, final_gain, final_shift,
          latent_weight, latent_bias, embed_weight, embed_bias):
    seq, dp = lax.axis_size("seq"), lax.axis_size("dp")
    channels = features.shape[2]
    cells = SLOT_ROWS * SLOT_COLS
    tokens = cells // 4
    feats, width = embed_weight.shape
    small = (block_gain, block_shift, block_bias, final_gain, final_shift, latent_weight.T, latent_bias)
    offsets = tuple(range(2, seq // 2, 2))
    others = [exchange(slot_kind, "seq", offset) for offset in offsets]
    slot_buffer = pltpu.VMEM((cells, channels), BF16)
    flops = encode_flops(cells, channels, latent_bias.shape[0])
    state, x, piece, *small = load(features, slot_kind, embed_weight, embed_bias, small)
    z_buffer = pltpu.VMEM((3, cells, channels), BF16)
    u_buffer = pltpu.VMEM((3, 2, cells // 2 + 2 * SLOT_COLS, channels), BF16)
    z, u, table, bias4, perm, piece = pl.pallas_call(
        begin_kernel,
        out_shape=[z_buffer, u_buffer, pltpu.VMEM((channels, 3 * LANES), BF16), pltpu.VMEM((1, LANES), F32),
                   pltpu.VMEM((tokens, cells), BF16), pltpu.VMEM(piece.shape, BF16)],
        in_specs=[SMEM_SPEC] + [VMEM_SPEC] * 6,
        out_specs=[VMEM_SPEC] * 6,
        compiler_params=pltpu.CompilerParams(vmem_limit_bytes=16 * MIB),
        cost_estimate=cost(2 * flops, features.size),
        name="begin",
    )(state, x, *small[:2], *small[5:], piece)
    small = (*small[:5], table, bias4)
    message, sums, z3, u3 = pl.pallas_call(
        functools.partial(middle_kernel, offsets),
        out_shape=[jax.ShapeDtypeStruct((tokens + 16, 2 * feats), BF16), pltpu.SMEM((1,), jnp.int32), z_buffer, u_buffer],
        in_specs=[SMEM_SPEC] + [VMEM_SPEC] * (5 + len(small)) + [ANY_SPEC] * len(others),
        out_specs=[VMEM_SPEC, SMEM_SPEC] + [VMEM_SPEC] * 2,
        scratch_shapes=[slot_buffer] * 2 + [z_buffer, u_buffer] + [pltpu.SMEM(slot_kind.shape, jnp.int32) for _ in others]
        + [pltpu.SemaphoreType.DMA((len(others),))],
        compiler_params=pltpu.CompilerParams(vmem_limit_bytes=16 * MIB),
        cost_estimate=cost(flops, block_weight.size * 2),
        name="middle",
    )(state, features, block_weight, perm, z, u, *small, *others)
    even = exchange(message, "seq", 1)
    odd = swap_odd_pairs(message)
    pieces = [piece] + [exchange(piece, "dp", offset) for offset in range(1, dp)]
    third, embed = pl.pallas_call(
        functools.partial(final_kernel, dp),
        out_shape=[pltpu.VMEM((tokens, feats), BF16), pltpu.VMEM((feats + 16, dp * width), BF16)],
        in_specs=[SMEM_SPEC] + [VMEM_SPEC] * (5 + dp + len(small)),
        out_specs=[VMEM_SPEC] * 2,
        scratch_shapes=[slot_buffer],
        compiler_params=pltpu.CompilerParams(vmem_limit_bytes=16 * MIB),
        cost_estimate=cost(flops, block_weight.size * 2),
        name="final",
    )(state, features, block_weight, perm, z3, u3, *pieces, *small)
    return pl.pallas_call(
        join_kernel,
        out_shape=jax.ShapeDtypeStruct((1, 2 * tokens, dp * width), BF16),
        in_specs=[SMEM_SPEC] * 2 + [VMEM_SPEC] * 5,
        out_specs=ANY_SPEC,
        scratch_shapes=[pltpu.VMEM((7, tokens, feats), BF16), pltpu.VMEM((2 * tokens, dp * width), BF16),
                        pltpu.SemaphoreType.DMA((2,))],
        compiler_params=pltpu.CompilerParams(vmem_limit_bytes=8 * MIB),
        cost_estimate=cost(4 * tokens * feats * dp * width, 4 * tokens * dp * width),
        name="join",
    )(state, sums, message, third, even, odd, embed)


def solution(mesh):
    in_specs = (P("dp", "seq", None), P("dp", "seq")) + (P(),) * 8 + (P(None, "dp"), P("dp"))
    return jax.shard_map(local, mesh=mesh, in_specs=in_specs, out_specs=P("dp", "seq", None), check_vma=False)
```

```python
import functools
import jax
import jax.numpy as jnp
from jax import lax
from jax.sharding import PartitionSpec as P
from jax.sharding import PartitionSpec as P
from jax.experimental import pallas as pl
from jax.experimental.pallas import tpu as pltpu

GROUPS = 32
SLOT_ROWS = 32
SLOT_COLS = 8
LATENT_SHIFT = 0.0609
LATENT_SCALE = 1.5305
NORM_EPSILON = 1e-06
LANES = 128
VMEM_BYTES = 64 * 1024 * 1024
F32 = jnp.float32
BF16 = jnp.bfloat16


def group_total(stats, same_group):
    rows, channels = stats.shape
    chunks = channels // LANES
    packed = jnp.concatenate([stats[:, k * LANES:(k + 1) * LANES] for k in range(chunks)], axis=0)
    high = packed.astype(BF16)
    rest = packed - high.astype(F32)
    middle = rest.astype(BF16)
    low = (rest - middle.astype(F32)).astype(BF16)
    total = sum(jnp.dot(piece, same_group, preferred_element_type=F32) for piece in (high, middle, low))
    return jnp.concatenate([total[k * rows:(k + 1) * rows] for k in range(chunks)], axis=1)


def affine(stats, joined, gain, shift, same_group, count):
    total = group_total(stats, same_group)
    mean, square = total[0:2] * (1.0 / count), total[2:4] * (1.0 / count)
    both_mean = 0.5 * (mean[0:1] + mean[1:2])
    both_square = 0.5 * (square[0:1] + square[1:2])
    mean = jnp.where(joined, both_mean, mean)
    square = jnp.where(joined, both_square, square)
    spread = jnp.maximum(square - mean * mean, 0.0)
    scale = lax.rsqrt(spread + NORM_EPSILON) * (0.5 * gain)
    return scale, 0.5 * shift - mean * scale


def half_stats(half):
    total = jnp.sum(half, axis=0, keepdims=True)
    return total, jnp.sum(half * half, axis=0, keepdims=True)


def halves_together(upper, lower):
    return jnp.stack([upper, lower], axis=1)


def norm_first_steps(x_ref, joined, gain, shift, same_group, v_ref):
    cells, channels = x_ref.shape
    half = cells // 2
    rows = cells // SLOT_COLS
    chunks = channels // LANES
    count = half * (channels // GROUPS)
    keep = jnp.where(joined, 1.0, 0.0).astype(F32)
    column = lax.broadcasted_iota(jnp.int32, (1, SLOT_COLS, 1), 1)
    parts = []
    for k in range(chunks):
        x = x_ref[:, k * LANES:(k + 1) * LANES].astype(F32)
        t0, q0 = half_stats(x[:half])
        t1, q1 = half_stats(x[half:])
        parts.append(jnp.concatenate([t0, t1, q0, q1], axis=0))
        yield
    scale, offset = affine(jnp.concatenate(parts, axis=1), joined, gain, shift, same_group, count)
    zero = jnp.zeros((1, SLOT_COLS, LANES), F32)
    mid = rows // 2
    for k in range(chunks):
        lanes = slice(k * LANES, (k + 1) * LANES)
        x = x_ref[:, lanes].astype(F32)
        v = jnp.concatenate([x[:half] * scale[0:1, lanes] + offset[0:1, lanes],
                             x[half:] * scale[1:2, lanes] + offset[1:2, lanes]], axis=0)
        act = v + v * jnp.tanh(v)
        act3 = act.reshape(rows, SLOT_COLS, LANES)
        left = jnp.where(column == 0, 0.0, pltpu.roll(act3, 1, 1))
        right = jnp.where(column == SLOT_COLS - 1, 0.0, pltpu.roll(act3, SLOT_COLS - 1, 1))
        for b, value in enumerate((left, act3, right)):
            upper, lower = value[:mid], value[mid:]
            top = halves_together(zero, upper[mid - 1:] * keep)
            bottom = halves_together(lower[:1] * keep, zero)
            tiles = jnp.concatenate([top, halves_together(upper, lower), bottom], axis=0)
            v_ref[b, :, lanes] = tiles.reshape(cells + 4 * SLOT_COLS, LANES).astype(BF16)
        yield


def conv_steps(x_ref, bias, w_ref, v_ref, y_ref):
    cells, channels = x_ref.shape
    half = cells // 2
    tile = channels // 2
    totals = []
    for k in range(2):
        lanes = slice(k * tile, (k + 1) * tile)
        x = x_ref[:, lanes].astype(F32).reshape(2, half // SLOT_COLS, SLOT_COLS, tile)
        totals.append(halves_together(x[0], x[1]).reshape(cells, tile) + bias[:, lanes])
    for a in range(3):
        for b in range(3):
            lhs = v_ref[b, 2 * SLOT_COLS * a:2 * SLOT_COLS * a + cells, :]
            base = (3 * a + b) * channels
            for k in range(2):
                totals[k] = totals[k] + jnp.dot(lhs, w_ref[base:base + channels, k * tile:(k + 1) * tile],
                                                preferred_element_type=F32)
                yield
    for k in range(2):
        y_ref[:, k * tile:(k + 1) * tile] = totals[k].astype(BF16)
    yield


def drain(steps):
    for _ in steps:
        pass


def interleave(main, *others):
    for _ in main:
        for steps in others:
            next(steps, None)
    for steps in others:
        drain(steps)


def norm_second_steps(y_ref, joined, gain, shift, same_group):
    cells, channels = y_ref.shape
    half = cells // 2
    rows = half // SLOT_COLS
    chunks = channels // LANES
    count = half * (channels // GROUPS)
    parts = []
    for k in range(chunks):
        inner = y_ref[:, k * LANES:(k + 1) * LANES].astype(F32).reshape(rows, 2, SLOT_COLS, LANES)
        t0, q0 = half_stats(inner[:, 0].reshape(half, LANES))
        t1, q1 = half_stats(inner[:, 1].reshape(half, LANES))
        parts.append(jnp.concatenate([t0, t1, q0, q1], axis=0))
        yield
    scale, offset = affine(jnp.concatenate(parts, axis=1), joined, gain, shift, same_group, count)
    for k in range(chunks):
        lanes = slice(k * LANES, (k + 1) * LANES)
        y = y_ref[:, lanes].astype(F32).reshape(rows, 2, SLOT_COLS, LANES)
        acts = []
        for h in range(2):
            v = y[:, h].reshape(half, LANES) * scale[h:h + 1, lanes] + offset[h:h + 1, lanes]
            acts.append((v + v * jnp.tanh(v)).reshape(rows, SLOT_COLS, LANES))
        y_ref[:, lanes] = halves_together(*acts).reshape(cells, LANES).astype(BF16)
        yield


def to_patches_steps(store, y_ref, joined, table_ref, bias, gather):
    cells, channels = y_ref.shape
    rows = cells // SLOT_COLS
    mid = rows // 2
    tokens = gather.shape[0]
    lat = channels // GROUPS
    keep = jnp.where(joined, 1.0, 0.0).astype(F32)
    column = lax.broadcasted_iota(jnp.int32, (1, SLOT_COLS, 1), 1)
    block = whole(lax.broadcasted_iota(jnp.int32, (1, SLOT_COLS, LANES), 2), lat)
    taps = jnp.dot(y_ref[...], table_ref[...], preferred_element_type=F32)
    yield
    from_left, here, from_right = (taps[:, k * LANES:(k + 1) * LANES].reshape(rows, SLOT_COLS, LANES) for k in range(3))
    moved = here + jnp.where(column == 0, 0.0, pltpu.roll(from_left, 1, 1))
    moved = moved + jnp.where(column == SLOT_COLS - 1, 0.0, pltpu.roll(from_right, SLOT_COLS - 1, 1))
    yield
    moved = moved.reshape(mid, 2, SLOT_COLS, LANES)
    upper, lower = moved[:, 0], moved[:, 1]
    blank = jnp.zeros((1, SLOT_COLS, LANES), F32)
    above = jnp.concatenate([halves_together(blank, upper[mid - 1:] * keep), moved[:mid - 1]], axis=0)
    below = jnp.concatenate([moved[1:], halves_together(lower[:1] * keep, blank)], axis=0)
    step_up = (block == 0) | (block == 3)
    step_none = (block == 1) | (block == 4)
    mixed = jnp.where(step_up, above, jnp.where(step_none, moved, below)).reshape(cells, LANES)
    yield
    latent = mixed + pltpu.roll(mixed, LANES - lat, 1) + pltpu.roll(mixed, LANES - 2 * lat, 1)
    latent = ((latent + bias) - LATENT_SHIFT) * LATENT_SCALE
    corner = block - part(lax.broadcasted_iota(jnp.int32, (1, SLOT_COLS, LANES), 1), 2)
    corner = jnp.stack([corner, corner - 2], axis=0)
    latent = latent.reshape(mid // 2, 2, 2, SLOT_COLS, LANES)
    latent = jnp.where((corner == 0)[None], latent, 0.0).reshape(cells, LANES)
    yield
    store(jnp.dot(gather, latent.astype(BF16), preferred_element_type=F32)[:, :4 * lat].astype(BF16))
    yield


def patch_tables(lw_ref, bias_ref, table_ref, bias4_ref):
    lat = lw_ref.shape[0] // 9
    weight = lw_ref[...].astype(F32)
    blank = jnp.zeros((2 * lat, weight.shape[1]), F32)
    for b in range(3):
        blocks = [weight[(3 * a + b) * lat:(3 * a + b + 1) * lat] for a in range(3)]
        table_ref[:, b * LANES:(b + 1) * LANES] = jnp.concatenate(blocks * 2 + [blank], axis=0).T.astype(BF16)
    bias4_ref[...] = jnp.concatenate([bias_ref[...].reshape(1, lat)] * (LANES // lat), axis=1)
    yield


def whole(value, size):
    return value >> (size.bit_length() - 1)


def part(value, size):
    return value & (size - 1)


def group_table(channels):
    width = channels // GROUPS
    r = whole(lax.broadcasted_iota(jnp.int32, (LANES, LANES), 0), width)
    c = whole(lax.broadcasted_iota(jnp.int32, (LANES, LANES), 1), width)
    return jnp.where(r == c, 1.0, 0.0).astype(BF16)


def patch_table(cells):
    half_cols = SLOT_COLS // 2
    token = lax.broadcasted_iota(jnp.int32, (cells // 4, cells), 0)
    cell = lax.broadcasted_iota(jnp.int32, (cells // 4, cells), 1)
    row_pair = whole(cell, 4 * SLOT_COLS) + part(whole(cell, SLOT_COLS), 2) * (cells // (4 * SLOT_COLS))
    own = row_pair * half_cols + whole(part(cell, SLOT_COLS), 2)
    return jnp.where(own == token, 1.0, 0.0).astype(BF16)


def finish_steps(store, y_ref, joined, gain, shift, same_group, table_ref, bias4, gather):
    yield from norm_second_steps(y_ref, joined, gain, shift, same_group)
    yield from to_patches_steps(store, y_ref, joined, table_ref, bias4, gather)


FIRST = 1


def vector(ref):
    return ref[...].reshape(1, ref.shape[0])


def load_kernel(kind_hbm, feat_hbm, ew_hbm, eb_hbm, *rest):
    names = 7
    small_hbm, rest = rest[:names], rest[names:]
    state_ref, x_ref, piece_ref, *rest = rest
    small, rest = rest[:names], rest[names:]
    kind_ref, ew_ref, eb_ref, ksem, xsem, ssem = rest
    slots = kind_ref.shape[1]
    cells = x_ref.shape[0]
    kcopy = pltpu.make_async_copy(kind_hbm, kind_ref, ksem)
    kcopy.start()
    xcopy = pltpu.make_async_copy(feat_hbm.at[0, pl.ds(FIRST * cells, cells), :], x_ref, xsem)
    scopies = [pltpu.make_async_copy(src, dst, ssem.at[i])
               for i, (src, dst) in enumerate(zip(small_hbm + (ew_hbm, eb_hbm), small + [ew_ref, eb_ref]))]
    for c in [xcopy] + scopies:
        c.start()
    kcopy.wait()
    live = jnp.int32(0)
    for s in range(slots):
        live = live + jnp.where(kind_ref[0, s] > 0, 1, 0).astype(jnp.int32)
        state_ref[2 + s] = kind_ref[0, s]
    state_ref[0] = live
    state_ref[1] = jnp.where(live > 2, 2, 0)
    for c in scopies:
        c.wait()
    feats = ew_ref.shape[0]
    piece_ref[0:feats, :] = ew_ref[...]
    piece_ref[feats:, :] = jnp.broadcast_to(vector(eb_ref), (piece_ref.shape[0] - feats, ew_ref.shape[1]))
    xcopy.wait()


def begin_kernel(state_ref, x_ref, gain_ref, shift_ref, lw_ref, lb_ref, piece_in,
                 v_ref, table_ref, bias4_ref, perm_ref, piece_ref):
    piece_ref[...] = piece_in[...]
    perm_ref[...] = patch_table(x_ref.shape[0])
    interleave(norm_first_steps(x_ref, state_ref[2 + FIRST] == 2, vector(gain_ref), vector(shift_ref),
                                group_table(x_ref.shape[1]), v_ref),
               patch_tables(lw_ref, lb_ref, table_ref, bias4_ref))


def second_norm(y_ref, kind, small):
    return norm_second_steps(y_ref, kind == 2, vector(small[3]), vector(small[4]), group_table(y_ref.shape[1]))


def patches(store, y_ref, kind, small, perm_ref):
    return to_patches_steps(store, y_ref, kind == 2, small[5], small[6][...], perm_ref[...])


def chain(*parts):
    for steps in parts:
        yield from steps


def count_live(kind_ref):
    total = jnp.int32(-2)
    for s in range(kind_ref.shape[1]):
        total = total + jnp.where(kind_ref[0, s] > 0, 1, 0).astype(jnp.int32)
    return total


def middle_kernel(offsets, state_ref, x_ref, w_ref, perm_ref, v_ref, *rest):
    names = 7
    small, rest = rest[:names], rest[names:]
    others, rest = rest[:len(offsets)], rest[len(offsets):]
    message_ref, sums_ref, v3_ref, *rest = rest
    early_ref, y_ref, v2_ref, *rest = rest
    kinds, ksem = rest[:-1], rest[-1]
    copies = [pltpu.make_async_copy(src, dst, ksem.at[i]) for i, (src, dst) in enumerate(zip(others, kinds))]
    for c in copies:
        c.start()
    cells = early_ref.shape[0]
    tokens = cells // 4
    feats = message_ref.shape[1] // 2
    slot = state_ref[1]

    def features_of(at):
        return x_ref.at[0, pl.ds(pl.multiple_of(at * cells, cells), cells), :]

    def first_norm(at, to_ref):
        return norm_first_steps(features_of(at), state_ref[2 + at] == 2, vector(small[0]), vector(small[1]),
                                group_table(x_ref.shape[2]), to_ref)

    def encode_two(with_third):
        found = {}

        def keep_as(name):
            def store(value):
                found[name] = value
            return store

        kind, early_kind = state_ref[2 + slot], state_ref[2 + FIRST]
        third = [first_norm(0, v3_ref)] if with_third else []
        interleave(conv_steps(features_of(FIRST), vector(small[2]), w_ref, v_ref, early_ref),
                   first_norm(slot, v2_ref))
        interleave(conv_steps(features_of(slot), vector(small[2]), w_ref, v2_ref, y_ref),
                   chain(second_norm(early_ref, early_kind, small), *third))
        interleave(chain(second_norm(y_ref, kind, small), patches(keep_as("second"), y_ref, kind, small, perm_ref)),
                   patches(keep_as("first"), early_ref, early_kind, small, perm_ref))
        first_is_last = state_ref[0] == 2
        last = jnp.where(first_is_last, found["first"], found["second"])
        before = jnp.where(first_is_last, found["second"], found["first"])
        message_ref[0:tokens, :] = jnp.concatenate([last, before], axis=1)

    pl.when(state_ref[0] > 2)(lambda: encode_two(True))
    pl.when(state_ref[0] <= 2)(lambda: encode_two(False))
    for c in copies:
        c.wait()
    position = lax.axis_index("seq")
    mine = state_ref[0] - 2
    below, above = jnp.int32(0), mine
    for offset, kind_ref in zip(offsets, kinds):
        other = count_live(kind_ref)
        lower = (position ^ offset) < position
        below = below + jnp.where(lower, other, 0)
        above = above + jnp.where(lower, 0, other)
    first_half = position < lax.axis_size("seq") // 2
    passed = jnp.where(position % 2 == 0, mine, 0)
    sums_ref[0] = jnp.where(first_half, below, -above)
    told = jnp.where(first_half, below + passed, passed - above)
    message_ref[tokens:, :] = jnp.full((message_ref.shape[0] - tokens, 2 * feats), told.astype(F32)).astype(BF16)


def final_kernel(parts, state_ref, x_ref, w_ref, perm_ref, v_ref, *rest):
    pieces, small, rest = rest[:parts], rest[parts:parts + 7], rest[parts + 7:]
    out_ref, embed_ref, y_ref = rest
    group = lax.axis_index("dp")
    width = pieces[0].shape[1]

    def lay_out():
        for j in range(parts):
            value = pieces[0][...]
            for k in range(1, parts):
                value = jnp.where((group ^ j) == k, pieces[k][...], value)
            embed_ref[:, j * width:(j + 1) * width] = value
            yield

    @pl.when(state_ref[0] > 2)
    def _():
        def store(value):
            out_ref[...] = value

        interleave(conv_steps(x_ref.at[0, 0:y_ref.shape[0], :], vector(small[2]), w_ref, v_ref, y_ref),
                   lay_out())
        drain(second_norm(y_ref, state_ref[2], small))
        drain(patches(store, y_ref, state_ref[2], small, perm_ref))

    @pl.when(state_ref[0] <= 2)
    def _():
        drain(lay_out())
        out_ref[...] = jnp.zeros_like(out_ref)


def join_kernel(state_ref, sums_ref, own_ref, third_ref, even_ref, odd_ref, embed_ref, out_ref, source_ref, value_ref, sem):
    live = state_ref[0]
    odd = lax.axis_index("seq") % 2
    tokens, feats = third_ref.shape
    told = even_ref[tokens:, :].astype(F32)[0, 0].astype(jnp.int32)
    carry = sums_ref[0] + told
    for k, ref in enumerate((even_ref, odd_ref, own_ref)):
        source_ref[2 * k] = ref[0:tokens, 0:feats]
        source_ref[2 * k + 1] = ref[0:tokens, feats:]
    source_ref[6] = third_ref[...]
    weight = embed_ref[0:feats, :]
    bias = embed_ref[feats:feats + 1, :].astype(F32)
    copies = []
    for i in range(2):
        incoming = (1 - odd) * 2 + carry - 1 - i
        kept = 4 + live - 1 - (i - carry)
        patch = source_ref[jnp.clip(jnp.where(i < carry, incoming, kept), 0, 6)]
        value = jnp.dot(patch, weight, preferred_element_type=F32) + bias
        rows = pl.ds(i * tokens, tokens)
        value_ref[rows, :] = value.astype(BF16)
        copies.append(pltpu.make_async_copy(value_ref.at[rows, :], out_ref.at[0, rows, :], sem.at[i]))
        copies[i].start()
    for c in copies:
        c.wait()


def exchange(value, axis, offset):
    count = lax.axis_size(axis)
    return lax.ppermute(value, axis, [(i, i ^ offset) for i in range(count)])


def swap_odd_pairs(value):
    groups, count = lax.axis_size("dp"), lax.axis_size("seq")
    pairs = []
    for g in range(groups):
        pairs += [(g * count + end, (g ^ 1) * count + end) for end in (0, count - 1)]
        for i in range(1, count - 1, 2):
            pairs += [(g * count + i, g * count + i + 1), (g * count + i + 1, g * count + i)]
    return lax.ppermute(value, ("dp", "seq"), pairs)


VMEM_SPEC = pl.BlockSpec(memory_space=pltpu.VMEM)
SMEM_SPEC = pl.BlockSpec(memory_space=pltpu.SMEM)
ANY_SPEC = pl.BlockSpec(memory_space=pl.ANY)
MIB = 1024 * 1024


def cost(flops, moved):
    return pl.CostEstimate(flops=flops, bytes_accessed=moved, transcendentals=0)


def encode_flops(cells, channels, lat):
    return cells * channels * 2 * 9 * (channels + lat)


def load(features, slot_kind, embed_weight, embed_bias, small):
    channels = features.shape[2]
    cells = SLOT_ROWS * SLOT_COLS
    feats, width = embed_weight.shape
    return pl.pallas_call(
        load_kernel,
        out_shape=[
            pltpu.SMEM((8,), jnp.int32),
            pltpu.VMEM((cells, channels), BF16),
            pltpu.VMEM((feats + 16, width), BF16),
        ] + [pltpu.VMEM(v.shape, v.dtype) for v in small],
        in_specs=[ANY_SPEC] * (4 + len(small)),
        out_specs=[SMEM_SPEC] + [VMEM_SPEC] * (2 + len(small)),
        scratch_shapes=[
            pltpu.SMEM(slot_kind.shape, jnp.int32),
            pltpu.VMEM(embed_weight.shape, BF16),
            pltpu.VMEM(embed_bias.shape, BF16),
            pltpu.SemaphoreType.DMA,
            pltpu.SemaphoreType.DMA,
            pltpu.SemaphoreType.DMA((len(small) + 2,)),
        ],
        compiler_params=pltpu.CompilerParams(vmem_limit_bytes=63 * MIB),
        cost_estimate=cost(0, features.size),
        name="load",
    )(slot_kind, features, embed_weight, embed_bias, *small)


def local(features, slot_kind, block_gain, block_shift, block_weight, block_bias, final_gain, final_shift,
          latent_weight, latent_bias, embed_weight, embed_bias):
    seq, dp = lax.axis_size("seq"), lax.axis_size("dp")
    channels = features.shape[2]
    cells = SLOT_ROWS * SLOT_COLS
    tokens = cells // 4
    feats, width = embed_weight.shape
    small = (block_gain, block_shift, block_bias, final_gain, final_shift, latent_weight.T, latent_bias)
    offsets = tuple(range(2, seq // 2, 2))
    others = [exchange(slot_kind, "seq", offset) for offset in offsets]
    slot_buffer = pltpu.VMEM((cells, channels), BF16)
    flops = encode_flops(cells, channels, latent_bias.shape[0])
    state, x, piece, *small = load(features, slot_kind, embed_weight, embed_bias, small)
    v_buffer = pltpu.VMEM((3, cells + 4 * SLOT_COLS, channels), BF16)
    v, table, bias4, perm, piece = pl.pallas_call(
        begin_kernel,
        out_shape=[v_buffer, pltpu.VMEM((channels, 3 * LANES), BF16), pltpu.VMEM((1, LANES), F32),
                   pltpu.VMEM((tokens, cells), BF16), pltpu.VMEM(piece.shape, BF16)],
        in_specs=[SMEM_SPEC] + [VMEM_SPEC] * 6,
        out_specs=[VMEM_SPEC] * 5,
        compiler_params=pltpu.CompilerParams(vmem_limit_bytes=16 * MIB),
        cost_estimate=cost(2 * flops, features.size),
        name="begin",
    )(state, x, *small[:2], *small[5:], piece)
    small = (*small[:5], table, bias4)
    message, sums, v3 = pl.pallas_call(
        functools.partial(middle_kernel, offsets),
        out_shape=[jax.ShapeDtypeStruct((tokens + 16, 2 * feats), BF16), pltpu.SMEM((1,), jnp.int32), v_buffer],
        in_specs=[SMEM_SPEC] + [VMEM_SPEC] * (4 + len(small)) + [ANY_SPEC] * len(others),
        out_specs=[VMEM_SPEC, SMEM_SPEC, VMEM_SPEC],
        scratch_shapes=[slot_buffer] * 2 + [v_buffer] + [pltpu.SMEM(slot_kind.shape, jnp.int32) for _ in others]
        + [pltpu.SemaphoreType.DMA((len(others),))],
        compiler_params=pltpu.CompilerParams(vmem_limit_bytes=16 * MIB),
        cost_estimate=cost(flops, block_weight.size * 2),
        name="middle",
    )(state, features, block_weight, perm, v, *small, *others)
    even = exchange(message, "seq", 1)
    odd = swap_odd_pairs(message)
    pieces = [piece] + [exchange(piece, "dp", offset) for offset in range(1, dp)]
    third, embed = pl.pallas_call(
        functools.partial(final_kernel, dp),
        out_shape=[pltpu.VMEM((tokens, feats), BF16), pltpu.VMEM((feats + 16, dp * width), BF16)],
        in_specs=[SMEM_SPEC] + [VMEM_SPEC] * (4 + dp + len(small)),
        out_specs=[VMEM_SPEC] * 2,
        scratch_shapes=[slot_buffer],
        compiler_params=pltpu.CompilerParams(vmem_limit_bytes=16 * MIB),
        cost_estimate=cost(flops, block_weight.size * 2),
        name="final",
    )(state, features, block_weight, perm, v3, *pieces, *small)
    return pl.pallas_call(
        join_kernel,
        out_shape=jax.ShapeDtypeStruct((1, 2 * tokens, dp * width), BF16),
        in_specs=[SMEM_SPEC] * 2 + [VMEM_SPEC] * 5,
        out_specs=ANY_SPEC,
        scratch_shapes=[pltpu.VMEM((7, tokens, feats), BF16), pltpu.VMEM((2 * tokens, dp * width), BF16),
                        pltpu.SemaphoreType.DMA((2,))],
        compiler_params=pltpu.CompilerParams(vmem_limit_bytes=8 * MIB),
        cost_estimate=cost(4 * tokens * feats * dp * width, 4 * tokens * dp * width),
        name="join",
    )(state, sums, message, third, even, odd, embed)


def solution(mesh):
    in_specs = (P("dp", "seq", None), P("dp", "seq")) + (P(),) * 8 + (P(None, "dp"), P("dp"))
    return jax.shard_map(local, mesh=mesh, in_specs=in_specs, out_specs=P("dp", "seq", None), check_vma=False)
```

```python
import functools
import jax
import jax.numpy as jnp
from jax import lax
from jax.sharding import PartitionSpec as P
from jax.sharding import PartitionSpec as P
from jax.experimental import pallas as pl
from jax.experimental.pallas import tpu as pltpu

GROUPS = 32
SLOT_ROWS = 32
SLOT_COLS = 8
LATENT_SHIFT = 0.0609
LATENT_SCALE = 1.5305
NORM_EPSILON = 1e-06
LANES = 128
VMEM_BYTES = 64 * 1024 * 1024
F32 = jnp.float32
BF16 = jnp.bfloat16


def group_total(stats, same_group):
    rows, channels = stats.shape
    chunks = channels // LANES
    packed = jnp.concatenate([stats[:, k * LANES:(k + 1) * LANES] for k in range(chunks)], axis=0)
    high = packed.astype(BF16)
    rest = packed - high.astype(F32)
    middle = rest.astype(BF16)
    low = (rest - middle.astype(F32)).astype(BF16)
    total = sum(jnp.dot(piece, same_group, preferred_element_type=F32) for piece in (high, middle, low))
    return jnp.concatenate([total[k * rows:(k + 1) * rows] for k in range(chunks)], axis=1)


def affine(stats, joined, gain, shift, same_group, count):
    total = group_total(stats, same_group)
    mean, square = total[0:2] * (1.0 / count), total[2:4] * (1.0 / count)
    both_mean = 0.5 * (mean[0:1] + mean[1:2])
    both_square = 0.5 * (square[0:1] + square[1:2])
    mean = jnp.where(joined, both_mean, mean)
    square = jnp.where(joined, both_square, square)
    spread = jnp.maximum(square - mean * mean, 0.0)
    scale = lax.rsqrt(spread + NORM_EPSILON) * (0.5 * gain)
    return scale, 0.5 * shift - mean * scale


def half_stats(half):
    total = jnp.sum(half, axis=0, keepdims=True)
    return total, jnp.sum(half * half, axis=0, keepdims=True)


def halves_together(upper, lower):
    return jnp.stack([upper, lower], axis=1)


def norm_first_steps(x_ref, joined, gain, shift, same_group, v_ref):
    cells, channels = x_ref.shape
    half = cells // 2
    rows = cells // SLOT_COLS
    chunks = channels // LANES
    count = half * (channels // GROUPS)
    keep = jnp.where(joined, 1.0, 0.0).astype(F32)
    column = lax.broadcasted_iota(jnp.int32, (1, SLOT_COLS, 1), 1)
    parts = []
    for k in range(chunks):
        x = x_ref[:, k * LANES:(k + 1) * LANES].astype(F32)
        t0, q0 = half_stats(x[:half])
        t1, q1 = half_stats(x[half:])
        parts.append(jnp.concatenate([t0, t1, q0, q1], axis=0))
        yield
    scale, offset = affine(jnp.concatenate(parts, axis=1), joined, gain, shift, same_group, count)
    zero = jnp.zeros((1, SLOT_COLS, LANES), F32)
    mid = rows // 2
    for k in range(chunks):
        lanes = slice(k * LANES, (k + 1) * LANES)
        x = x_ref[:, lanes].astype(F32)
        v = jnp.concatenate([x[:half] * scale[0:1, lanes] + offset[0:1, lanes],
                             x[half:] * scale[1:2, lanes] + offset[1:2, lanes]], axis=0)
        act = v + v * jnp.tanh(v)
        act3 = act.reshape(rows, SLOT_COLS, LANES)
        left = jnp.where(column == 0, 0.0, pltpu.roll(act3, 1, 1))
        right = jnp.where(column == SLOT_COLS - 1, 0.0, pltpu.roll(act3, SLOT_COLS - 1, 1))
        for b, value in enumerate((left, act3, right)):
            upper, lower = value[:mid], value[mid:]
            top = halves_together(zero, upper[mid - 1:] * keep)
            bottom = halves_together(lower[:1] * keep, zero)
            tiles = jnp.concatenate([top, halves_together(upper, lower), bottom], axis=0)
            v_ref[b, :, lanes] = tiles.reshape(cells + 4 * SLOT_COLS, LANES).astype(BF16)
        yield


def conv_steps(x_ref, bias, w_ref, v_ref, y_ref):
    cells, channels = x_ref.shape
    half = cells // 2
    tile = channels // 2
    totals = []
    for k in range(2):
        lanes = slice(k * tile, (k + 1) * tile)
        x = x_ref[:, lanes].astype(F32).reshape(2, half // SLOT_COLS, SLOT_COLS, tile)
        totals.append(halves_together(x[0], x[1]).reshape(cells, tile) + bias[:, lanes])
    for a in range(3):
        for b in range(3):
            lhs = v_ref[b, 2 * SLOT_COLS * a:2 * SLOT_COLS * a + cells, :]
            base = (3 * a + b) * channels
            for k in range(2):
                totals[k] = totals[k] + jnp.dot(lhs, w_ref[base:base + channels, k * tile:(k + 1) * tile],
                                                preferred_element_type=F32)
                yield
    for k in range(2):
        y_ref[:, k * tile:(k + 1) * tile] = totals[k].astype(BF16)
    yield


def drain(steps):
    for _ in steps:
        pass


def interleave(main, *others):
    for _ in main:
        for steps in others:
            next(steps, None)
    for steps in others:
        drain(steps)


def norm_second_steps(y_ref, joined, gain, shift, same_group):
    cells, channels = y_ref.shape
    half = cells // 2
    rows = half // SLOT_COLS
    chunks = channels // LANES
    count = half * (channels // GROUPS)
    parts = []
    for k in range(chunks):
        inner = y_ref[:, k * LANES:(k + 1) * LANES].astype(F32).reshape(rows, 2, SLOT_COLS, LANES)
        t0, q0 = half_stats(inner[:, 0].reshape(half, LANES))
        t1, q1 = half_stats(inner[:, 1].reshape(half, LANES))
        parts.append(jnp.concatenate([t0, t1, q0, q1], axis=0))
        yield
    scale, offset = affine(jnp.concatenate(parts, axis=1), joined, gain, shift, same_group, count)
    for k in range(chunks):
        lanes = slice(k * LANES, (k + 1) * LANES)
        y = y_ref[:, lanes].astype(F32).reshape(rows, 2, SLOT_COLS, LANES)
        acts = []
        for h in range(2):
            v = y[:, h].reshape(half, LANES) * scale[h:h + 1, lanes] + offset[h:h + 1, lanes]
            acts.append((v + v * jnp.tanh(v)).reshape(rows, SLOT_COLS, LANES))
        y_ref[:, lanes] = halves_together(*acts).reshape(cells, LANES).astype(BF16)
        yield


def to_patches_steps(store, y_ref, joined, table_ref, bias, gather):
    cells, channels = y_ref.shape
    rows = cells // SLOT_COLS
    mid = rows // 2
    tokens = gather.shape[0]
    lat = channels // GROUPS
    keep = jnp.where(joined, 1.0, 0.0).astype(F32)
    column = lax.broadcasted_iota(jnp.int32, (1, SLOT_COLS, 1), 1)
    block = whole(lax.broadcasted_iota(jnp.int32, (1, SLOT_COLS, LANES), 2), lat)
    taps = jnp.dot(y_ref[...], table_ref[...], preferred_element_type=F32)
    yield
    from_left, here, from_right = (taps[:, k * LANES:(k + 1) * LANES].reshape(rows, SLOT_COLS, LANES) for k in range(3))
    moved = here + jnp.where(column == 0, 0.0, pltpu.roll(from_left, 1, 1))
    moved = moved + jnp.where(column == SLOT_COLS - 1, 0.0, pltpu.roll(from_right, SLOT_COLS - 1, 1))
    yield
    moved = moved.reshape(mid, 2, SLOT_COLS, LANES)
    upper, lower = moved[:, 0], moved[:, 1]
    blank = jnp.zeros((1, SLOT_COLS, LANES), F32)
    above = jnp.concatenate([halves_together(blank, upper[mid - 1:] * keep), moved[:mid - 1]], axis=0)
    below = jnp.concatenate([moved[1:], halves_together(lower[:1] * keep, blank)], axis=0)
    step_up = (block == 0) | (block == 3)
    step_none = (block == 1) | (block == 4)
    mixed = jnp.where(step_up, above, jnp.where(step_none, moved, below)).reshape(cells, LANES)
    yield
    latent = mixed + pltpu.roll(mixed, LANES - lat, 1) + pltpu.roll(mixed, LANES - 2 * lat, 1)
    latent = ((latent + bias) - LATENT_SHIFT) * LATENT_SCALE
    corner = block - part(lax.broadcasted_iota(jnp.int32, (1, SLOT_COLS, LANES), 1), 2)
    corner = jnp.stack([corner, corner - 2], axis=0)
    latent = latent.reshape(mid // 2, 2, 2, SLOT_COLS, LANES)
    latent = jnp.where((corner == 0)[None], latent, 0.0).reshape(cells, LANES)
    yield
    store(jnp.dot(gather, latent.astype(BF16), preferred_element_type=F32)[:, :4 * lat].astype(BF16))
    yield


def patch_tables(lw_ref, bias_ref, table_ref, bias4_ref):
    lat = lw_ref.shape[0] // 9
    weight = lw_ref[...].astype(F32)
    blank = jnp.zeros((2 * lat, weight.shape[1]), F32)
    for b in range(3):
        blocks = [weight[(3 * a + b) * lat:(3 * a + b + 1) * lat] for a in range(3)]
        table_ref[:, b * LANES:(b + 1) * LANES] = jnp.concatenate(blocks * 2 + [blank], axis=0).T.astype(BF16)
    bias4_ref[...] = jnp.concatenate([bias_ref[...].reshape(1, lat)] * (LANES // lat), axis=1)
    yield


def whole(value, size):
    return value >> (size.bit_length() - 1)


def part(value, size):
    return value & (size - 1)


def group_table(channels):
    width = channels // GROUPS
    r = whole(lax.broadcasted_iota(jnp.int32, (LANES, LANES), 0), width)
    c = whole(lax.broadcasted_iota(jnp.int32, (LANES, LANES), 1), width)
    return jnp.where(r == c, 1.0, 0.0).astype(BF16)


def patch_table(cells):
    half_cols = SLOT_COLS // 2
    token = lax.broadcasted_iota(jnp.int32, (cells // 4, cells), 0)
    cell = lax.broadcasted_iota(jnp.int32, (cells // 4, cells), 1)
    row_pair = whole(cell, 4 * SLOT_COLS) + part(whole(cell, SLOT_COLS), 2) * (cells // (4 * SLOT_COLS))
    own = row_pair * half_cols + whole(part(cell, SLOT_COLS), 2)
    return jnp.where(own == token, 1.0, 0.0).astype(BF16)


def finish_steps(store, y_ref, joined, gain, shift, same_group, table_ref, bias4, gather):
    yield from norm_second_steps(y_ref, joined, gain, shift, same_group)
    yield from to_patches_steps(store, y_ref, joined, table_ref, bias4, gather)


FIRST = 1


def vector(ref):
    return ref[...].reshape(1, ref.shape[0])


def load_kernel(kind_hbm, feat_hbm, ew_hbm, eb_hbm, *rest):
    names = 7
    small_hbm, rest = rest[:names], rest[names:]
    state_ref, x_ref, piece_ref, *rest = rest
    small, rest = rest[:names], rest[names:]
    kind_ref, ew_ref, eb_ref, ksem, xsem, ssem = rest
    slots = kind_ref.shape[1]
    cells = x_ref.shape[0]
    kcopy = pltpu.make_async_copy(kind_hbm, kind_ref, ksem)
    kcopy.start()
    xcopy = pltpu.make_async_copy(feat_hbm.at[0, pl.ds(FIRST * cells, cells), :], x_ref, xsem)
    scopies = [pltpu.make_async_copy(src, dst, ssem.at[i])
               for i, (src, dst) in enumerate(zip(small_hbm + (ew_hbm, eb_hbm), small + [ew_ref, eb_ref]))]
    for c in [xcopy] + scopies:
        c.start()
    kcopy.wait()
    live = jnp.int32(0)
    for s in range(slots):
        live = live + jnp.where(kind_ref[0, s] > 0, 1, 0).astype(jnp.int32)
        state_ref[2 + s] = kind_ref[0, s]
    state_ref[0] = live
    state_ref[1] = jnp.where(live > 2, 2, 0)
    for c in scopies:
        c.wait()
    feats = ew_ref.shape[0]
    piece_ref[0:feats, :] = ew_ref[...]
    piece_ref[feats:, :] = jnp.broadcast_to(vector(eb_ref), (piece_ref.shape[0] - feats, ew_ref.shape[1]))
    xcopy.wait()


def begin_kernel(state_ref, x_ref, gain_ref, shift_ref, lw_ref, lb_ref, piece_in,
                 v_ref, table_ref, bias4_ref, perm_ref, piece_ref):
    piece_ref[...] = piece_in[...]
    perm_ref[...] = patch_table(x_ref.shape[0])
    interleave(norm_first_steps(x_ref, state_ref[2 + FIRST] == 2, vector(gain_ref), vector(shift_ref),
                                group_table(x_ref.shape[1]), v_ref),
               patch_tables(lw_ref, lb_ref, table_ref, bias4_ref))


def second_norm(y_ref, kind, small):
    return norm_second_steps(y_ref, kind == 2, vector(small[3]), vector(small[4]), group_table(y_ref.shape[1]))


def patches(store, y_ref, kind, small, perm_ref):
    return to_patches_steps(store, y_ref, kind == 2, small[5], small[6][...], perm_ref[...])


def chain(*parts):
    for steps in parts:
        yield from steps


def count_live(kind_ref):
    total = jnp.int32(-2)
    for s in range(kind_ref.shape[1]):
        total = total + jnp.where(kind_ref[0, s] > 0, 1, 0).astype(jnp.int32)
    return total


def middle_kernel(offsets, state_ref, x_ref, w_ref, perm_ref, v_ref, *rest):
    names = 7
    small, rest = rest[:names], rest[names:]
    others, rest = rest[:len(offsets)], rest[len(offsets):]
    message_ref, sums_ref, _, *rest = rest
    early_ref, y_ref, v2_ref, *rest = rest
    kinds, ksem = rest[:-1], rest[-1]
    copies = [pltpu.make_async_copy(src, dst, ksem.at[i]) for i, (src, dst) in enumerate(zip(others, kinds))]
    for c in copies:
        c.start()
    cells = early_ref.shape[0]
    tokens = cells // 4
    feats = message_ref.shape[1] // 2
    slot = state_ref[1]

    def features_of(at):
        return x_ref.at[0, pl.ds(pl.multiple_of(at * cells, cells), cells), :]

    def first_norm(at, to_ref):
        return norm_first_steps(features_of(at), state_ref[2 + at] == 2, vector(small[0]), vector(small[1]),
                                group_table(x_ref.shape[2]), to_ref)

    found = {}

    def keep_as(name):
        def store(value):
            found[name] = value
        return store

    kind, early_kind = state_ref[2 + slot], state_ref[2 + FIRST]
    interleave(conv_steps(features_of(FIRST), vector(small[2]), w_ref, v_ref, early_ref),
               first_norm(slot, v2_ref))
    interleave(conv_steps(features_of(slot), vector(small[2]), w_ref, v2_ref, y_ref),
               second_norm(early_ref, early_kind, small))
    interleave(chain(second_norm(y_ref, kind, small), patches(keep_as("second"), y_ref, kind, small, perm_ref)),
               patches(keep_as("first"), early_ref, early_kind, small, perm_ref))
    first_is_last = state_ref[0] == 2
    last = jnp.where(first_is_last, found["first"], found["second"])
    before = jnp.where(first_is_last, found["second"], found["first"])
    message_ref[0:tokens, :] = jnp.concatenate([last, before], axis=1)

    for c in copies:
        c.wait()
    position = lax.axis_index("seq")
    mine = state_ref[0] - 2
    below, above = jnp.int32(0), mine
    for offset, kind_ref in zip(offsets, kinds):
        other = count_live(kind_ref)
        lower = (position ^ offset) < position
        below = below + jnp.where(lower, other, 0)
        above = above + jnp.where(lower, 0, other)
    first_half = position < lax.axis_size("seq") // 2
    passed = jnp.where(position % 2 == 0, mine, 0)
    sums_ref[0] = jnp.where(first_half, below, -above)
    told = jnp.where(first_half, below + passed, passed - above)
    message_ref[tokens:, :] = jnp.full((message_ref.shape[0] - tokens, 2 * feats), told.astype(F32)).astype(BF16)


def final_kernel(parts, state_ref, x_ref, w_ref, perm_ref, _, *rest):
    pieces, small, rest = rest[:parts], rest[parts:parts + 7], rest[parts + 7:]
    out_ref, embed_ref, y_ref, v_ref = rest
    group = lax.axis_index("dp")
    width = pieces[0].shape[1]

    def lay_out():
        for j in range(parts):
            value = pieces[0][...]
            for k in range(1, parts):
                value = jnp.where((group ^ j) == k, pieces[k][...], value)
            embed_ref[:, j * width:(j + 1) * width] = value
            yield

    @pl.when(state_ref[0] > 2)
    def _():
        def store(value):
            out_ref[...] = value

        x = x_ref.at[0, 0:y_ref.shape[0], :]
        interleave(norm_first_steps(x, state_ref[2] == 2, vector(small[0]), vector(small[1]),
                                    group_table(y_ref.shape[1]), v_ref), lay_out())
        drain(conv_steps(x, vector(small[2]), w_ref, v_ref, y_ref))
        drain(second_norm(y_ref, state_ref[2], small))
        drain(patches(store, y_ref, state_ref[2], small, perm_ref))

    @pl.when(state_ref[0] <= 2)
    def _():
        drain(lay_out())
        out_ref[...] = jnp.zeros_like(out_ref)


def join_kernel(state_ref, sums_ref, own_ref, third_ref, even_ref, odd_ref, embed_ref, out_ref, source_ref, value_ref, sem):
    live = state_ref[0]
    odd = lax.axis_index("seq") % 2
    tokens, feats = third_ref.shape
    told = even_ref[tokens:, :].astype(F32)[0, 0].astype(jnp.int32)
    carry = sums_ref[0] + told
    for k, ref in enumerate((even_ref, odd_ref, own_ref)):
        source_ref[2 * k] = ref[0:tokens, 0:feats]
        source_ref[2 * k + 1] = ref[0:tokens, feats:]
    source_ref[6] = third_ref[...]
    weight = embed_ref[0:feats, :]
    bias = embed_ref[feats:feats + 1, :].astype(F32)
    copies = []
    for i in range(2):
        incoming = (1 - odd) * 2 + carry - 1 - i
        kept = 4 + live - 1 - (i - carry)
        patch = source_ref[jnp.clip(jnp.where(i < carry, incoming, kept), 0, 6)]
        value = jnp.dot(patch, weight, preferred_element_type=F32) + bias
        rows = pl.ds(i * tokens, tokens)
        value_ref[rows, :] = value.astype(BF16)
        copies.append(pltpu.make_async_copy(value_ref.at[rows, :], out_ref.at[0, rows, :], sem.at[i]))
        copies[i].start()
    for c in copies:
        c.wait()


def exchange(value, axis, offset):
    count = lax.axis_size(axis)
    return lax.ppermute(value, axis, [(i, i ^ offset) for i in range(count)])


def swap_odd_pairs(value):
    groups, count = lax.axis_size("dp"), lax.axis_size("seq")
    pairs = []
    for g in range(groups):
        pairs += [(g * count + end, (g ^ 1) * count + end) for end in (0, count - 1)]
        for i in range(1, count - 1, 2):
            pairs += [(g * count + i, g * count + i + 1), (g * count + i + 1, g * count + i)]
    return lax.ppermute(value, ("dp", "seq"), pairs)


VMEM_SPEC = pl.BlockSpec(memory_space=pltpu.VMEM)
SMEM_SPEC = pl.BlockSpec(memory_space=pltpu.SMEM)
ANY_SPEC = pl.BlockSpec(memory_space=pl.ANY)
MIB = 1024 * 1024


def cost(flops, moved):
    return pl.CostEstimate(flops=flops, bytes_accessed=moved, transcendentals=0)


def encode_flops(cells, channels, lat):
    return cells * channels * 2 * 9 * (channels + lat)


def load(features, slot_kind, embed_weight, embed_bias, small):
    channels = features.shape[2]
    cells = SLOT_ROWS * SLOT_COLS
    feats, width = embed_weight.shape
    return pl.pallas_call(
        load_kernel,
        out_shape=[
            pltpu.SMEM((8,), jnp.int32),
            pltpu.VMEM((cells, channels), BF16),
            pltpu.VMEM((feats + 16, width), BF16),
        ] + [pltpu.VMEM(v.shape, v.dtype) for v in small],
        in_specs=[ANY_SPEC] * (4 + len(small)),
        out_specs=[SMEM_SPEC] + [VMEM_SPEC] * (2 + len(small)),
        scratch_shapes=[
            pltpu.SMEM(slot_kind.shape, jnp.int32),
            pltpu.VMEM(embed_weight.shape, BF16),
            pltpu.VMEM(embed_bias.shape, BF16),
            pltpu.SemaphoreType.DMA,
            pltpu.SemaphoreType.DMA,
            pltpu.SemaphoreType.DMA((len(small) + 2,)),
        ],
        compiler_params=pltpu.CompilerParams(vmem_limit_bytes=63 * MIB),
        cost_estimate=cost(0, features.size),
        name="load",
    )(slot_kind, features, embed_weight, embed_bias, *small)


def local(features, slot_kind, block_gain, block_shift, block_weight, block_bias, final_gain, final_shift,
          latent_weight, latent_bias, embed_weight, embed_bias):
    seq, dp = lax.axis_size("seq"), lax.axis_size("dp")
    channels = features.shape[2]
    cells = SLOT_ROWS * SLOT_COLS
    tokens = cells // 4
    feats, width = embed_weight.shape
    small = (block_gain, block_shift, block_bias, final_gain, final_shift, latent_weight.T, latent_bias)
    offsets = tuple(range(2, seq // 2, 2))
    others = [exchange(slot_kind, "seq", offset) for offset in offsets]
    slot_buffer = pltpu.VMEM((cells, channels), BF16)
    flops = encode_flops(cells, channels, latent_bias.shape[0])
    state, x, piece, *small = load(features, slot_kind, embed_weight, embed_bias, small)
    v_buffer = pltpu.VMEM((3, cells + 4 * SLOT_COLS, channels), BF16)
    v, table, bias4, perm, piece = pl.pallas_call(
        begin_kernel,
        out_shape=[v_buffer, pltpu.VMEM((channels, 3 * LANES), BF16), pltpu.VMEM((1, LANES), F32),
                   pltpu.VMEM((tokens, cells), BF16), pltpu.VMEM(piece.shape, BF16)],
        in_specs=[SMEM_SPEC] + [VMEM_SPEC] * 6,
        out_specs=[VMEM_SPEC] * 5,
        compiler_params=pltpu.CompilerParams(vmem_limit_bytes=16 * MIB),
        cost_estimate=cost(2 * flops, features.size),
        name="begin",
    )(state, x, *small[:2], *small[5:], piece)
    small = (*small[:5], table, bias4)
    message, sums, spare = pl.pallas_call(
        functools.partial(middle_kernel, offsets),
        out_shape=[jax.ShapeDtypeStruct((tokens + 16, 2 * feats), BF16), pltpu.SMEM((1,), jnp.int32), v_buffer],
        in_specs=[SMEM_SPEC] + [VMEM_SPEC] * (4 + len(small)) + [ANY_SPEC] * len(others),
        out_specs=[VMEM_SPEC, SMEM_SPEC, VMEM_SPEC],
        scratch_shapes=[slot_buffer] * 2 + [v_buffer] + [pltpu.SMEM(slot_kind.shape, jnp.int32) for _ in others]
        + [pltpu.SemaphoreType.DMA((len(others),))],
        compiler_params=pltpu.CompilerParams(vmem_limit_bytes=16 * MIB),
        cost_estimate=cost(flops, block_weight.size * 2),
        name="middle",
    )(state, features, block_weight, perm, v, *small, *others)
    even = exchange(message, "seq", 1)
    odd = swap_odd_pairs(message)
    pieces = [piece] + [exchange(piece, "dp", offset) for offset in range(1, dp)]
    third, embed = pl.pallas_call(
        functools.partial(final_kernel, dp),
        out_shape=[pltpu.VMEM((tokens, feats), BF16), pltpu.VMEM((feats + 16, dp * width), BF16)],
        in_specs=[SMEM_SPEC] + [VMEM_SPEC] * (4 + dp + len(small)),
        out_specs=[VMEM_SPEC] * 2,
        scratch_shapes=[slot_buffer, v_buffer],
        compiler_params=pltpu.CompilerParams(vmem_limit_bytes=16 * MIB),
        cost_estimate=cost(flops, block_weight.size * 2),
        name="final",
    )(state, features, block_weight, perm, spare, *pieces, *small)
    return pl.pallas_call(
        join_kernel,
        out_shape=jax.ShapeDtypeStruct((1, 2 * tokens, dp * width), BF16),
        in_specs=[SMEM_SPEC] * 2 + [VMEM_SPEC] * 5,
        out_specs=ANY_SPEC,
        scratch_shapes=[pltpu.VMEM((7, tokens, feats), BF16), pltpu.VMEM((2 * tokens, dp * width), BF16),
                        pltpu.SemaphoreType.DMA((2,))],
        compiler_params=pltpu.CompilerParams(vmem_limit_bytes=8 * MIB),
        cost_estimate=cost(4 * tokens * feats * dp * width, 4 * tokens * dp * width),
        name="join",
    )(state, sums, message, third, even, odd, embed)


def solution(mesh):
    in_specs = (P("dp", "seq", None), P("dp", "seq")) + (P(),) * 8 + (P(None, "dp"), P("dp"))
    return jax.shard_map(local, mesh=mesh, in_specs=in_specs, out_specs=P("dp", "seq", None), check_vma=False)
```

```python
import functools
import jax
import jax.numpy as jnp
from jax import lax
from jax.sharding import PartitionSpec as P
from jax.sharding import PartitionSpec as P
from jax.experimental import pallas as pl
from jax.experimental.pallas import tpu as pltpu

GROUPS = 32
SLOT_ROWS = 32
SLOT_COLS = 8
LATENT_SHIFT = 0.0609
LATENT_SCALE = 1.5305
NORM_EPSILON = 1e-06
LANES = 128
VMEM_BYTES = 64 * 1024 * 1024
F32 = jnp.float32
BF16 = jnp.bfloat16


def group_total(stats, same_group):
    rows, channels = stats.shape
    chunks = channels // LANES
    packed = jnp.concatenate([stats[:, k * LANES:(k + 1) * LANES] for k in range(chunks)], axis=0)
    high = packed.astype(BF16)
    rest = packed - high.astype(F32)
    middle = rest.astype(BF16)
    low = (rest - middle.astype(F32)).astype(BF16)
    total = jnp.dot(jnp.concatenate([high, middle, low], axis=0), same_group, preferred_element_type=F32)
    size = rows * chunks
    total = total[:size] + total[size:2 * size] + total[2 * size:]
    return jnp.concatenate([total[k * rows:(k + 1) * rows] for k in range(chunks)], axis=1)


def affine(stats, joined, gain, shift, same_group, count):
    total = group_total(stats, same_group)
    mean, square = total[0:2] * (1.0 / count), total[2:4] * (1.0 / count)
    both_mean = 0.5 * (mean[0:1] + mean[1:2])
    both_square = 0.5 * (square[0:1] + square[1:2])
    mean = jnp.where(joined, both_mean, mean)
    square = jnp.where(joined, both_square, square)
    spread = jnp.maximum(square - mean * mean, 0.0)
    scale = lax.rsqrt(spread + NORM_EPSILON) * (0.5 * gain)
    return scale, 0.5 * shift - mean * scale


def half_stats(half):
    total = jnp.sum(half, axis=0, keepdims=True)
    return total, jnp.sum(half * half, axis=0, keepdims=True)


def halves_together(upper, lower):
    return jnp.stack([upper, lower], axis=1)


def norm_first_steps(x_ref, joined, gain, shift, same_group, v_ref):
    cells, channels = x_ref.shape
    half = cells // 2
    rows = cells // SLOT_COLS
    chunks = channels // LANES
    count = half * (channels // GROUPS)
    keep = jnp.where(joined, 1.0, 0.0).astype(F32)
    column = lax.broadcasted_iota(jnp.int32, (1, SLOT_COLS, 1), 1)
    parts = []
    for k in range(chunks):
        x = x_ref[:, k * LANES:(k + 1) * LANES].astype(F32)
        t0, q0 = half_stats(x[:half])
        t1, q1 = half_stats(x[half:])
        parts.append(jnp.concatenate([t0, t1, q0, q1], axis=0))
        yield
    scale, offset = affine(jnp.concatenate(parts, axis=1), joined, gain, shift, same_group, count)
    zero = jnp.zeros((1, SLOT_COLS, LANES), F32)
    mid = rows // 2
    for k in range(chunks):
        lanes = slice(k * LANES, (k + 1) * LANES)
        x = x_ref[:, lanes].astype(F32)
        v = jnp.concatenate([x[:half] * scale[0:1, lanes] + offset[0:1, lanes],
                             x[half:] * scale[1:2, lanes] + offset[1:2, lanes]], axis=0)
        act = v + v * jnp.tanh(v)
        act3 = act.reshape(rows, SLOT_COLS, LANES)
        left = jnp.where(column == 0, 0.0, pltpu.roll(act3, 1, 1))
        right = jnp.where(column == SLOT_COLS - 1, 0.0, pltpu.roll(act3, SLOT_COLS - 1, 1))
        for b, value in enumerate((left, act3, right)):
            upper, lower = value[:mid], value[mid:]
            top = halves_together(zero, upper[mid - 1:] * keep)
            bottom = halves_together(lower[:1] * keep, zero)
            tiles = jnp.concatenate([top, halves_together(upper, lower), bottom], axis=0)
            v_ref[b, :, lanes] = tiles.reshape(cells + 4 * SLOT_COLS, LANES).astype(BF16)
        yield


def conv_steps(x_ref, bias, w_ref, v_ref, y_ref):
    cells, channels = x_ref.shape
    half = cells // 2
    tile = channels // 2
    totals = []
    for k in range(2):
        lanes = slice(k * tile, (k + 1) * tile)
        x = x_ref[:, lanes].astype(F32).reshape(2, half // SLOT_COLS, SLOT_COLS, tile)
        totals.append(halves_together(x[0], x[1]).reshape(cells, tile) + bias[:, lanes])
    for a in range(3):
        for b in range(3):
            lhs = v_ref[b, 2 * SLOT_COLS * a:2 * SLOT_COLS * a + cells, :]
            base = (3 * a + b) * channels
            for k in range(2):
                totals[k] = totals[k] + jnp.dot(lhs, w_ref[base:base + channels, k * tile:(k + 1) * tile],
                                                preferred_element_type=F32)
                yield
    for k in range(2):
        y_ref[:, k * tile:(k + 1) * tile] = totals[k].astype(BF16)
    yield


def drain(steps):
    for _ in steps:
        pass


def interleave(main, *others):
    for _ in main:
        for steps in others:
            next(steps, None)
    for steps in others:
        drain(steps)


def norm_second_steps(y_ref, joined, gain, shift, same_group):
    cells, channels = y_ref.shape
    half = cells // 2
    rows = half // SLOT_COLS
    chunks = channels // LANES
    count = half * (channels // GROUPS)
    parts = []
    for k in range(chunks):
        inner = y_ref[:, k * LANES:(k + 1) * LANES].astype(F32).reshape(rows, 2, SLOT_COLS, LANES)
        t0, q0 = half_stats(inner[:, 0].reshape(half, LANES))
        t1, q1 = half_stats(inner[:, 1].reshape(half, LANES))
        parts.append(jnp.concatenate([t0, t1, q0, q1], axis=0))
        yield
    scale, offset = affine(jnp.concatenate(parts, axis=1), joined, gain, shift, same_group, count)
    for k in range(chunks):
        lanes = slice(k * LANES, (k + 1) * LANES)
        y = y_ref[:, lanes].astype(F32).reshape(rows, 2, SLOT_COLS, LANES)
        acts = []
        for h in range(2):
            v = y[:, h].reshape(half, LANES) * scale[h:h + 1, lanes] + offset[h:h + 1, lanes]
            acts.append((v + v * jnp.tanh(v)).reshape(rows, SLOT_COLS, LANES))
        y_ref[:, lanes] = halves_together(*acts).reshape(cells, LANES).astype(BF16)
        yield


def to_patches_steps(store, y_ref, joined, table_ref, bias, gather):
    cells, channels = y_ref.shape
    rows = cells // SLOT_COLS
    mid = rows // 2
    tokens = gather.shape[0]
    lat = channels // GROUPS
    keep = jnp.where(joined, 1.0, 0.0).astype(F32)
    column = lax.broadcasted_iota(jnp.int32, (1, SLOT_COLS, 1), 1)
    block = whole(lax.broadcasted_iota(jnp.int32, (1, SLOT_COLS, LANES), 2), lat)
    taps = jnp.dot(y_ref[...], table_ref[...], preferred_element_type=F32)
    yield
    from_left, here, from_right = (taps[:, k * LANES:(k + 1) * LANES].reshape(rows, SLOT_COLS, LANES) for k in range(3))
    moved = here + jnp.where(column == 0, 0.0, pltpu.roll(from_left, 1, 1))
    moved = moved + jnp.where(column == SLOT_COLS - 1, 0.0, pltpu.roll(from_right, SLOT_COLS - 1, 1))
    yield
    moved = moved.reshape(mid, 2, SLOT_COLS, LANES)
    upper, lower = moved[:, 0], moved[:, 1]
    blank = jnp.zeros((1, SLOT_COLS, LANES), F32)
    above = jnp.concatenate([halves_together(blank, upper[mid - 1:] * keep), moved[:mid - 1]], axis=0)
    below = jnp.concatenate([moved[1:], halves_together(lower[:1] * keep, blank)], axis=0)
    step_up = (block == 0) | (block == 3)
    step_none = (block == 1) | (block == 4)
    mixed = jnp.where(step_up, above, jnp.where(step_none, moved, below)).reshape(cells, LANES)
    yield
    latent = mixed + pltpu.roll(mixed, LANES - lat, 1) + pltpu.roll(mixed, LANES - 2 * lat, 1)
    latent = ((latent + bias) - LATENT_SHIFT) * LATENT_SCALE
    corner = block - part(lax.broadcasted_iota(jnp.int32, (1, SLOT_COLS, LANES), 1), 2)
    corner = jnp.stack([corner, corner - 2], axis=0)
    latent = latent.reshape(mid // 2, 2, 2, SLOT_COLS, LANES)
    latent = jnp.where((corner == 0)[None], latent, 0.0).reshape(cells, LANES)
    yield
    store(jnp.dot(gather, latent.astype(BF16), preferred_element_type=F32)[:, :4 * lat].astype(BF16))
    yield


def patch_tables(lw_ref, bias_ref, table_ref, bias4_ref):
    lat = lw_ref.shape[0] // 9
    weight = lw_ref[...].astype(F32)
    blank = jnp.zeros((2 * lat, weight.shape[1]), F32)
    for b in range(3):
        blocks = [weight[(3 * a + b) * lat:(3 * a + b + 1) * lat] for a in range(3)]
        table_ref[:, b * LANES:(b + 1) * LANES] = jnp.concatenate(blocks * 2 + [blank], axis=0).T.astype(BF16)
    bias4_ref[...] = jnp.concatenate([bias_ref[...].reshape(1, lat)] * (LANES // lat), axis=1)
    yield


def whole(value, size):
    return value >> (size.bit_length() - 1)


def part(value, size):
    return value & (size - 1)


def group_table(channels):
    width = channels // GROUPS
    r = whole(lax.broadcasted_iota(jnp.int32, (LANES, LANES), 0), width)
    c = whole(lax.broadcasted_iota(jnp.int32, (LANES, LANES), 1), width)
    return jnp.where(r == c, 1.0, 0.0).astype(BF16)


def patch_table(cells):
    half_cols = SLOT_COLS // 2
    token = lax.broadcasted_iota(jnp.int32, (cells // 4, cells), 0)
    cell = lax.broadcasted_iota(jnp.int32, (cells // 4, cells), 1)
    row_pair = whole(cell, 4 * SLOT_COLS) + part(whole(cell, SLOT_COLS), 2) * (cells // (4 * SLOT_COLS))
    own = row_pair * half_cols + whole(part(cell, SLOT_COLS), 2)
    return jnp.where(own == token, 1.0, 0.0).astype(BF16)


def finish_steps(store, y_ref, joined, gain, shift, same_group, table_ref, bias4, gather):
    yield from norm_second_steps(y_ref, joined, gain, shift, same_group)
    yield from to_patches_steps(store, y_ref, joined, table_ref, bias4, gather)


FIRST = 1


def vector(ref):
    return ref[...].reshape(1, ref.shape[0])


def load_kernel(kind_hbm, feat_hbm, ew_hbm, eb_hbm, *rest):
    names = 7
    small_hbm, rest = rest[:names], rest[names:]
    state_ref, x_ref, piece_ref, *rest = rest
    small, rest = rest[:names], rest[names:]
    kind_ref, ew_ref, eb_ref, ksem, xsem, ssem = rest
    slots = kind_ref.shape[1]
    cells = x_ref.shape[0]
    kcopy = pltpu.make_async_copy(kind_hbm, kind_ref, ksem)
    kcopy.start()
    xcopy = pltpu.make_async_copy(feat_hbm.at[0, pl.ds(FIRST * cells, cells), :], x_ref, xsem)
    scopies = [pltpu.make_async_copy(src, dst, ssem.at[i])
               for i, (src, dst) in enumerate(zip(small_hbm + (ew_hbm, eb_hbm), small + [ew_ref, eb_ref]))]
    for c in [xcopy] + scopies:
        c.start()
    kcopy.wait()
    live = jnp.int32(0)
    for s in range(slots):
        live = live + jnp.where(kind_ref[0, s] > 0, 1, 0).astype(jnp.int32)
        state_ref[2 + s] = kind_ref[0, s]
    state_ref[0] = live
    state_ref[1] = jnp.where(live > 2, 2, 0)
    for c in scopies:
        c.wait()
    feats = ew_ref.shape[0]
    piece_ref[0:feats, :] = ew_ref[...]
    piece_ref[feats:, :] = jnp.broadcast_to(vector(eb_ref), (piece_ref.shape[0] - feats, ew_ref.shape[1]))
    xcopy.wait()


def begin_kernel(state_ref, x_ref, gain_ref, shift_ref, lw_ref, lb_ref, piece_in,
                 v_ref, table_ref, bias4_ref, perm_ref, piece_ref):
    piece_ref[...] = piece_in[...]
    perm_ref[...] = patch_table(x_ref.shape[0])
    interleave(norm_first_steps(x_ref, state_ref[2 + FIRST] == 2, vector(gain_ref), vector(shift_ref),
                                group_table(x_ref.shape[1]), v_ref),
               patch_tables(lw_ref, lb_ref, table_ref, bias4_ref))


def second_norm(y_ref, kind, small):
    return norm_second_steps(y_ref, kind == 2, vector(small[3]), vector(small[4]), group_table(y_ref.shape[1]))


def patches(store, y_ref, kind, small, perm_ref):
    return to_patches_steps(store, y_ref, kind == 2, small[5], small[6][...], perm_ref[...])


def chain(*parts):
    for steps in parts:
        yield from steps


def count_live(kind_ref):
    total = jnp.int32(-2)
    for s in range(kind_ref.shape[1]):
        total = total + jnp.where(kind_ref[0, s] > 0, 1, 0).astype(jnp.int32)
    return total


def middle_kernel(offsets, state_ref, x_ref, w_ref, perm_ref, v_ref, *rest):
    names = 7
    small, rest = rest[:names], rest[names:]
    others, rest = rest[:len(offsets)], rest[len(offsets):]
    message_ref, sums_ref, _, *rest = rest
    early_ref, y_ref, v2_ref, *rest = rest
    kinds, ksem = rest[:-1], rest[-1]
    copies = [pltpu.make_async_copy(src, dst, ksem.at[i]) for i, (src, dst) in enumerate(zip(others, kinds))]
    for c in copies:
        c.start()
    cells = early_ref.shape[0]
    tokens = cells // 4
    feats = message_ref.shape[1] // 2
    slot = state_ref[1]

    def features_of(at):
        return x_ref.at[0, pl.ds(pl.multiple_of(at * cells, cells), cells), :]

    def first_norm(at, to_ref):
        return norm_first_steps(features_of(at), state_ref[2 + at] == 2, vector(small[0]), vector(small[1]),
                                group_table(x_ref.shape[2]), to_ref)

    found = {}

    def keep_as(name):
        def store(value):
            found[name] = value
        return store

    kind, early_kind = state_ref[2 + slot], state_ref[2 + FIRST]
    interleave(conv_steps(features_of(FIRST), vector(small[2]), w_ref, v_ref, early_ref),
               first_norm(slot, v2_ref))
    interleave(conv_steps(features_of(slot), vector(small[2]), w_ref, v2_ref, y_ref),
               second_norm(early_ref, early_kind, small))
    interleave(chain(second_norm(y_ref, kind, small), patches(keep_as("second"), y_ref, kind, small, perm_ref)),
               patches(keep_as("first"), early_ref, early_kind, small, perm_ref))
    first_is_last = state_ref[0] == 2
    last = jnp.where(first_is_last, found["first"], found["second"])
    before = jnp.where(first_is_last, found["second"], found["first"])
    message_ref[0:tokens, :] = jnp.concatenate([last, before], axis=1)

    for c in copies:
        c.wait()
    position = lax.axis_index("seq")
    mine = state_ref[0] - 2
    below, above = jnp.int32(0), mine
    for offset, kind_ref in zip(offsets, kinds):
        other = count_live(kind_ref)
        lower = (position ^ offset) < position
        below = below + jnp.where(lower, other, 0)
        above = above + jnp.where(lower, 0, other)
    first_half = position < lax.axis_size("seq") // 2
    passed = jnp.where(position % 2 == 0, mine, 0)
    sums_ref[0] = jnp.where(first_half, below, -above)
    told = jnp.where(first_half, below + passed, passed - above)
    message_ref[tokens:, :] = jnp.full((message_ref.shape[0] - tokens, 2 * feats), told.astype(F32)).astype(BF16)


def final_kernel(parts, state_ref, x_ref, w_ref, perm_ref, _, *rest):
    pieces, small, rest = rest[:parts], rest[parts:parts + 7], rest[parts + 7:]
    out_ref, embed_ref, y_ref, v_ref = rest
    group = lax.axis_index("dp")
    width = pieces[0].shape[1]

    def lay_out():
        for j in range(parts):
            value = pieces[0][...]
            for k in range(1, parts):
                value = jnp.where((group ^ j) == k, pieces[k][...], value)
            embed_ref[:, j * width:(j + 1) * width] = value
            yield

    @pl.when(state_ref[0] > 2)
    def _():
        def store(value):
            out_ref[...] = value

        x = x_ref.at[0, 0:y_ref.shape[0], :]
        interleave(norm_first_steps(x, state_ref[2] == 2, vector(small[0]), vector(small[1]),
                                    group_table(y_ref.shape[1]), v_ref), lay_out())
        drain(conv_steps(x, vector(small[2]), w_ref, v_ref, y_ref))
        drain(second_norm(y_ref, state_ref[2], small))
        drain(patches(store, y_ref, state_ref[2], small, perm_ref))

    @pl.when(state_ref[0] <= 2)
    def _():
        drain(lay_out())
        out_ref[...] = jnp.zeros_like(out_ref)


def join_kernel(state_ref, sums_ref, own_ref, third_ref, even_ref, odd_ref, embed_ref, out_ref, source_ref, value_ref, sem):
    live = state_ref[0]
    odd = lax.axis_index("seq") % 2
    tokens, feats = third_ref.shape
    told = even_ref[tokens:, :].astype(F32)[0, 0].astype(jnp.int32)
    carry = sums_ref[0] + told
    for k, ref in enumerate((even_ref, odd_ref, own_ref)):
        source_ref[2 * k] = ref[0:tokens, 0:feats]
        source_ref[2 * k + 1] = ref[0:tokens, feats:]
    source_ref[6] = third_ref[...]
    weight = embed_ref[0:feats, :]
    bias = embed_ref[feats:feats + 1, :].astype(F32)
    copies = []
    for i in range(2):
        incoming = (1 - odd) * 2 + carry - 1 - i
        kept = 4 + live - 1 - (i - carry)
        patch = source_ref[jnp.clip(jnp.where(i < carry, incoming, kept), 0, 6)]
        value = jnp.dot(patch, weight, preferred_element_type=F32) + bias
        rows = pl.ds(i * tokens, tokens)
        value_ref[rows, :] = value.astype(BF16)
        copies.append(pltpu.make_async_copy(value_ref.at[rows, :], out_ref.at[0, rows, :], sem.at[i]))
        copies[i].start()
    for c in copies:
        c.wait()


def exchange(value, axis, offset):
    count = lax.axis_size(axis)
    return lax.ppermute(value, axis, [(i, i ^ offset) for i in range(count)])


def swap_odd_pairs(value):
    groups, count = lax.axis_size("dp"), lax.axis_size("seq")
    pairs = []
    for g in range(groups):
        pairs += [(g * count + end, (g ^ 1) * count + end) for end in (0, count - 1)]
        for i in range(1, count - 1, 2):
            pairs += [(g * count + i, g * count + i + 1), (g * count + i + 1, g * count + i)]
    return lax.ppermute(value, ("dp", "seq"), pairs)


VMEM_SPEC = pl.BlockSpec(memory_space=pltpu.VMEM)
SMEM_SPEC = pl.BlockSpec(memory_space=pltpu.SMEM)
ANY_SPEC = pl.BlockSpec(memory_space=pl.ANY)
MIB = 1024 * 1024


def cost(flops, moved):
    return pl.CostEstimate(flops=flops, bytes_accessed=moved, transcendentals=0)


def encode_flops(cells, channels, lat):
    return cells * channels * 2 * 9 * (channels + lat)


def load(features, slot_kind, embed_weight, embed_bias, small):
    channels = features.shape[2]
    cells = SLOT_ROWS * SLOT_COLS
    feats, width = embed_weight.shape
    return pl.pallas_call(
        load_kernel,
        out_shape=[
            pltpu.SMEM((8,), jnp.int32),
            pltpu.VMEM((cells, channels), BF16),
            pltpu.VMEM((feats + 16, width), BF16),
        ] + [pltpu.VMEM(v.shape, v.dtype) for v in small],
        in_specs=[ANY_SPEC] * (4 + len(small)),
        out_specs=[SMEM_SPEC] + [VMEM_SPEC] * (2 + len(small)),
        scratch_shapes=[
            pltpu.SMEM(slot_kind.shape, jnp.int32),
            pltpu.VMEM(embed_weight.shape, BF16),
            pltpu.VMEM(embed_bias.shape, BF16),
            pltpu.SemaphoreType.DMA,
            pltpu.SemaphoreType.DMA,
            pltpu.SemaphoreType.DMA((len(small) + 2,)),
        ],
        compiler_params=pltpu.CompilerParams(vmem_limit_bytes=63 * MIB),
        cost_estimate=cost(0, features.size),
        name="load",
    )(slot_kind, features, embed_weight, embed_bias, *small)


def local(features, slot_kind, block_gain, block_shift, block_weight, block_bias, final_gain, final_shift,
          latent_weight, latent_bias, embed_weight, embed_bias):
    seq, dp = lax.axis_size("seq"), lax.axis_size("dp")
    channels = features.shape[2]
    cells = SLOT_ROWS * SLOT_COLS
    tokens = cells // 4
    feats, width = embed_weight.shape
    small = (block_gain, block_shift, block_bias, final_gain, final_shift, latent_weight.T, latent_bias)
    offsets = tuple(range(2, seq // 2, 2))
    others = [exchange(slot_kind, "seq", offset) for offset in offsets]
    slot_buffer = pltpu.VMEM((cells, channels), BF16)
    flops = encode_flops(cells, channels, latent_bias.shape[0])
    state, x, piece, *small = load(features, slot_kind, embed_weight, embed_bias, small)
    v_buffer = pltpu.VMEM((3, cells + 4 * SLOT_COLS, channels), BF16)
    v, table, bias4, perm, piece = pl.pallas_call(
        begin_kernel,
        out_shape=[v_buffer, pltpu.VMEM((channels, 3 * LANES), BF16), pltpu.VMEM((1, LANES), F32),
                   pltpu.VMEM((tokens, cells), BF16), pltpu.VMEM(piece.shape, BF16)],
        in_specs=[SMEM_SPEC] + [VMEM_SPEC] * 6,
        out_specs=[VMEM_SPEC] * 5,
        compiler_params=pltpu.CompilerParams(vmem_limit_bytes=16 * MIB),
        cost_estimate=cost(2 * flops, features.size),
        name="begin",
    )(state, x, *small[:2], *small[5:], piece)
    small = (*small[:5], table, bias4)
    message, sums, spare = pl.pallas_call(
        functools.partial(middle_kernel, offsets),
        out_shape=[jax.ShapeDtypeStruct((tokens + 16, 2 * feats), BF16), pltpu.SMEM((1,), jnp.int32), v_buffer],
        in_specs=[SMEM_SPEC] + [VMEM_SPEC] * (4 + len(small)) + [ANY_SPEC] * len(others),
        out_specs=[VMEM_SPEC, SMEM_SPEC, VMEM_SPEC],
        scratch_shapes=[slot_buffer] * 2 + [v_buffer] + [pltpu.SMEM(slot_kind.shape, jnp.int32) for _ in others]
        + [pltpu.SemaphoreType.DMA((len(others),))],
        compiler_params=pltpu.CompilerParams(vmem_limit_bytes=16 * MIB),
        cost_estimate=cost(flops, block_weight.size * 2),
        name="middle",
    )(state, features, block_weight, perm, v, *small, *others)
    even = exchange(message, "seq", 1)
    odd = swap_odd_pairs(message)
    pieces = [piece] + [exchange(piece, "dp", offset) for offset in range(1, dp)]
    third, embed = pl.pallas_call(
        functools.partial(final_kernel, dp),
        out_shape=[pltpu.VMEM((tokens, feats), BF16), pltpu.VMEM((feats + 16, dp * width), BF16)],
        in_specs=[SMEM_SPEC] + [VMEM_SPEC] * (4 + dp + len(small)),
        out_specs=[VMEM_SPEC] * 2,
        scratch_shapes=[slot_buffer, v_buffer],
        compiler_params=pltpu.CompilerParams(vmem_limit_bytes=16 * MIB),
        cost_estimate=cost(flops, block_weight.size * 2),
        name="final",
    )(state, features, block_weight, perm, spare, *pieces, *small)
    return pl.pallas_call(
        join_kernel,
        out_shape=jax.ShapeDtypeStruct((1, 2 * tokens, dp * width), BF16),
        in_specs=[SMEM_SPEC] * 2 + [VMEM_SPEC] * 5,
        out_specs=ANY_SPEC,
        scratch_shapes=[pltpu.VMEM((7, tokens, feats), BF16), pltpu.VMEM((2 * tokens, dp * width), BF16),
                        pltpu.SemaphoreType.DMA((2,))],
        compiler_params=pltpu.CompilerParams(vmem_limit_bytes=8 * MIB),
        cost_estimate=cost(4 * tokens * feats * dp * width, 4 * tokens * dp * width),
        name="join",
    )(state, sums, message, third, even, odd, embed)


def solution(mesh):
    in_specs = (P("dp", "seq", None), P("dp", "seq")) + (P(),) * 8 + (P(None, "dp"), P("dp"))
    return jax.shard_map(local, mesh=mesh, in_specs=in_specs, out_specs=P("dp", "seq", None), check_vma=False)
```

```python
import functools
import jax
import jax.numpy as jnp
from jax import lax
from jax.sharding import PartitionSpec as P
from jax.sharding import PartitionSpec as P
from jax.experimental import pallas as pl
from jax.experimental.pallas import tpu as pltpu

GROUPS = 32
SLOT_ROWS = 32
SLOT_COLS = 8
LATENT_SHIFT = 0.0609
LATENT_SCALE = 1.5305
NORM_EPSILON = 1e-06
LANES = 128
VMEM_BYTES = 64 * 1024 * 1024
F32 = jnp.float32
BF16 = jnp.bfloat16


def group_total(stats, same_group):
    rows, channels = stats.shape
    chunks = channels // LANES
    packed = jnp.concatenate([stats[:, k * LANES:(k + 1) * LANES] for k in range(chunks)], axis=0)
    high = packed.astype(BF16)
    rest = packed - high.astype(F32)
    middle = rest.astype(BF16)
    low = (rest - middle.astype(F32)).astype(BF16)
    total = jnp.dot(jnp.concatenate([high, middle, low], axis=0), same_group, preferred_element_type=F32)
    size = rows * chunks
    total = total[:size] + total[size:2 * size] + total[2 * size:]
    return jnp.concatenate([total[k * rows:(k + 1) * rows] for k in range(chunks)], axis=1)


def affine(stats, joined, gain, shift, same_group, count):
    total = group_total(stats, same_group)
    mean, square = total[0:2] * (1.0 / count), total[2:4] * (1.0 / count)
    both_mean = 0.5 * (mean[0:1] + mean[1:2])
    both_square = 0.5 * (square[0:1] + square[1:2])
    mean = jnp.where(joined, both_mean, mean)
    square = jnp.where(joined, both_square, square)
    spread = jnp.maximum(square - mean * mean, 0.0)
    scale = lax.rsqrt(spread + NORM_EPSILON) * (0.5 * gain)
    return scale, 0.5 * shift - mean * scale


def half_stats(half):
    total = jnp.sum(half, axis=0, keepdims=True)
    return total, jnp.sum(half * half, axis=0, keepdims=True)


def halves_together(upper, lower):
    return jnp.stack([upper, lower], axis=1)


def norm_first_steps(x_ref, joined, gain, shift, same_group, v_ref):
    cells, channels = x_ref.shape
    half = cells // 2
    rows = cells // SLOT_COLS
    chunks = channels // LANES
    count = half * (channels // GROUPS)
    keep = jnp.where(joined, 1.0, 0.0).astype(F32)
    column = lax.broadcasted_iota(jnp.int32, (1, SLOT_COLS, 1), 1)
    parts = []
    for k in range(chunks):
        x = x_ref[:, k * LANES:(k + 1) * LANES].astype(F32)
        t0, q0 = half_stats(x[:half])
        t1, q1 = half_stats(x[half:])
        parts.append(jnp.concatenate([t0, t1, q0, q1], axis=0))
        yield
    scale, offset = affine(jnp.concatenate(parts, axis=1), joined, gain, shift, same_group, count)
    zero = jnp.zeros((1, SLOT_COLS, LANES), F32)
    mid = rows // 2
    for k in range(chunks):
        lanes = slice(k * LANES, (k + 1) * LANES)
        x = x_ref[:, lanes].astype(F32)
        v = jnp.concatenate([x[:half] * scale[0:1, lanes] + offset[0:1, lanes],
                             x[half:] * scale[1:2, lanes] + offset[1:2, lanes]], axis=0)
        act = v + v * jnp.tanh(v)
        act3 = act.reshape(rows, SLOT_COLS, LANES)
        left = jnp.where(column == 0, 0.0, pltpu.roll(act3, 1, 1))
        right = jnp.where(column == SLOT_COLS - 1, 0.0, pltpu.roll(act3, SLOT_COLS - 1, 1))
        for b, value in enumerate((left, act3, right)):
            upper, lower = value[:mid], value[mid:]
            top = halves_together(zero, upper[mid - 1:] * keep)
            bottom = halves_together(lower[:1] * keep, zero)
            tiles = jnp.concatenate([top, halves_together(upper, lower), bottom], axis=0)
            v_ref[b, :, lanes] = tiles.reshape(cells + 4 * SLOT_COLS, LANES).astype(BF16)
        yield


def conv_steps(x_ref, bias, w_ref, v_ref, y_ref, by_half=False):
    cells, channels = x_ref.shape
    half = cells // 2
    tile = channels // 2
    totals = []
    for k in range(2):
        lanes = slice(k * tile, (k + 1) * tile)
        x = x_ref[:, lanes].astype(F32).reshape(2, half // SLOT_COLS, SLOT_COLS, tile)
        totals.append(halves_together(x[0], x[1]).reshape(cells, tile) + bias[:, lanes])
    for deep in [slice(h * tile, (h + 1) * tile) for h in range(2)] if by_half else []:
        for a in range(3):
            rows = slice(2 * SLOT_COLS * a, 2 * SLOT_COLS * a + cells)
            lhs = jnp.concatenate([v_ref[b, rows, deep] for b in range(3)], axis=1)
            for k in range(2):
                weight = jnp.concatenate([w_ref[(3 * a + b) * channels + deep.start:(3 * a + b) * channels + deep.stop,
                                                k * tile:(k + 1) * tile] for b in range(3)], axis=0)
                totals[k] = totals[k] + jnp.dot(lhs, weight, preferred_element_type=F32)
                yield
    for a in range(0 if by_half else 3):
        for b in range(3):
            lhs = v_ref[b, 2 * SLOT_COLS * a:2 * SLOT_COLS * a + cells, :]
            base = (3 * a + b) * channels
            for k in range(2):
                totals[k] = totals[k] + jnp.dot(lhs, w_ref[base:base + channels, k * tile:(k + 1) * tile],
                                                preferred_element_type=F32)
                yield
    for k in range(2):
        y_ref[:, k * tile:(k + 1) * tile] = totals[k].astype(BF16)
    yield


def drain(steps):
    for _ in steps:
        pass


def interleave(main, *others):
    for _ in main:
        for steps in others:
            next(steps, None)
    for steps in others:
        drain(steps)


def norm_second_steps(y_ref, joined, gain, shift, same_group):
    cells, channels = y_ref.shape
    half = cells // 2
    rows = half // SLOT_COLS
    chunks = channels // LANES
    count = half * (channels // GROUPS)
    parts = []
    for k in range(chunks):
        inner = y_ref[:, k * LANES:(k + 1) * LANES].astype(F32).reshape(rows, 2, SLOT_COLS, LANES)
        t0, q0 = half_stats(inner[:, 0].reshape(half, LANES))
        t1, q1 = half_stats(inner[:, 1].reshape(half, LANES))
        parts.append(jnp.concatenate([t0, t1, q0, q1], axis=0))
        yield
    scale, offset = affine(jnp.concatenate(parts, axis=1), joined, gain, shift, same_group, count)
    for k in range(chunks):
        lanes = slice(k * LANES, (k + 1) * LANES)
        y = y_ref[:, lanes].astype(F32).reshape(rows, 2, SLOT_COLS, LANES)
        acts = []
        for h in range(2):
            v = y[:, h].reshape(half, LANES) * scale[h:h + 1, lanes] + offset[h:h + 1, lanes]
            acts.append((v + v * jnp.tanh(v)).reshape(rows, SLOT_COLS, LANES))
        y_ref[:, lanes] = halves_together(*acts).reshape(cells, LANES).astype(BF16)
        yield


def to_patches_steps(store, y_ref, joined, table_ref, bias, gather):
    cells, channels = y_ref.shape
    rows = cells // SLOT_COLS
    mid = rows // 2
    tokens = gather.shape[0]
    lat = channels // GROUPS
    keep = jnp.where(joined, 1.0, 0.0).astype(F32)
    column = lax.broadcasted_iota(jnp.int32, (1, SLOT_COLS, 1), 1)
    block = whole(lax.broadcasted_iota(jnp.int32, (1, SLOT_COLS, LANES), 2), lat)
    taps = jnp.dot(y_ref[...], table_ref[...], preferred_element_type=F32)
    yield
    from_left, here, from_right = (taps[:, k * LANES:(k + 1) * LANES].reshape(rows, SLOT_COLS, LANES) for k in range(3))
    moved = here + jnp.where(column == 0, 0.0, pltpu.roll(from_left, 1, 1))
    moved = moved + jnp.where(column == SLOT_COLS - 1, 0.0, pltpu.roll(from_right, SLOT_COLS - 1, 1))
    yield
    moved = moved.reshape(mid, 2, SLOT_COLS, LANES)
    upper, lower = moved[:, 0], moved[:, 1]
    blank = jnp.zeros((1, SLOT_COLS, LANES), F32)
    above = jnp.concatenate([halves_together(blank, upper[mid - 1:] * keep), moved[:mid - 1]], axis=0)
    below = jnp.concatenate([moved[1:], halves_together(lower[:1] * keep, blank)], axis=0)
    step_up = (block == 0) | (block == 3)
    step_none = (block == 1) | (block == 4)
    mixed = jnp.where(step_up, above, jnp.where(step_none, moved, below)).reshape(cells, LANES)
    yield
    latent = mixed + pltpu.roll(mixed, LANES - lat, 1) + pltpu.roll(mixed, LANES - 2 * lat, 1)
    latent = ((latent + bias) - LATENT_SHIFT) * LATENT_SCALE
    corner = block - part(lax.broadcasted_iota(jnp.int32, (1, SLOT_COLS, LANES), 1), 2)
    corner = jnp.stack([corner, corner - 2], axis=0)
    latent = latent.reshape(mid // 2, 2, 2, SLOT_COLS, LANES)
    latent = jnp.where((corner == 0)[None], latent, 0.0).reshape(cells, LANES)
    yield
    store(jnp.dot(gather, latent.astype(BF16), preferred_element_type=F32)[:, :4 * lat].astype(BF16))
    yield


def patch_tables(lw_ref, bias_ref, table_ref, bias4_ref):
    lat = lw_ref.shape[0] // 9
    weight = lw_ref[...].astype(F32)
    blank = jnp.zeros((2 * lat, weight.shape[1]), F32)
    for b in range(3):
        blocks = [weight[(3 * a + b) * lat:(3 * a + b + 1) * lat] for a in range(3)]
        table_ref[:, b * LANES:(b + 1) * LANES] = jnp.concatenate(blocks * 2 + [blank], axis=0).T.astype(BF16)
    bias4_ref[...] = jnp.concatenate([bias_ref[...].reshape(1, lat)] * (LANES // lat), axis=1)
    yield


def whole(value, size):
    return value >> (size.bit_length() - 1)


def part(value, size):
    return value & (size - 1)


def group_table(channels):
    width = channels // GROUPS
    r = whole(lax.broadcasted_iota(jnp.int32, (LANES, LANES), 0), width)
    c = whole(lax.broadcasted_iota(jnp.int32, (LANES, LANES), 1), width)
    return jnp.where(r == c, 1.0, 0.0).astype(BF16)


def patch_table(cells):
    half_cols = SLOT_COLS // 2
    token = lax.broadcasted_iota(jnp.int32, (cells // 4, cells), 0)
    cell = lax.broadcasted_iota(jnp.int32, (cells // 4, cells), 1)
    row_pair = whole(cell, 4 * SLOT_COLS) + part(whole(cell, SLOT_COLS), 2) * (cells // (4 * SLOT_COLS))
    own = row_pair * half_cols + whole(part(cell, SLOT_COLS), 2)
    return jnp.where(own == token, 1.0, 0.0).astype(BF16)


def finish_steps(store, y_ref, joined, gain, shift, same_group, table_ref, bias4, gather):
    yield from norm_second_steps(y_ref, joined, gain, shift, same_group)
    yield from to_patches_steps(store, y_ref, joined, table_ref, bias4, gather)


FIRST = 1


def vector(ref):
    return ref[...].reshape(1, ref.shape[0])


def load_kernel(kind_hbm, feat_hbm, ew_hbm, eb_hbm, *rest):
    names = 7
    small_hbm, rest = rest[:names], rest[names:]
    state_ref, x_ref, piece_ref, *rest = rest
    small, rest = rest[:names], rest[names:]
    kind_ref, ew_ref, eb_ref, ksem, xsem, ssem = rest
    slots = kind_ref.shape[1]
    cells = x_ref.shape[0]
    kcopy = pltpu.make_async_copy(kind_hbm, kind_ref, ksem)
    kcopy.start()
    xcopy = pltpu.make_async_copy(feat_hbm.at[0, pl.ds(FIRST * cells, cells), :], x_ref, xsem)
    scopies = [pltpu.make_async_copy(src, dst, ssem.at[i])
               for i, (src, dst) in enumerate(zip(small_hbm + (ew_hbm, eb_hbm), small + [ew_ref, eb_ref]))]
    for c in [xcopy] + scopies:
        c.start()
    kcopy.wait()
    live = jnp.int32(0)
    for s in range(slots):
        live = live + jnp.where(kind_ref[0, s] > 0, 1, 0).astype(jnp.int32)
        state_ref[2 + s] = kind_ref[0, s]
    state_ref[0] = live
    state_ref[1] = jnp.where(live > 2, 2, 0)
    for c in scopies:
        c.wait()
    feats = ew_ref.shape[0]
    piece_ref[0:feats, :] = ew_ref[...]
    piece_ref[feats:, :] = jnp.broadcast_to(vector(eb_ref), (piece_ref.shape[0] - feats, ew_ref.shape[1]))
    xcopy.wait()


def begin_kernel(state_ref, x_ref, gain_ref, shift_ref, lw_ref, lb_ref, piece_in,
                 v_ref, table_ref, bias4_ref, perm_ref, piece_ref):
    piece_ref[...] = piece_in[...]
    perm_ref[...] = patch_table(x_ref.shape[0])
    interleave(norm_first_steps(x_ref, state_ref[2 + FIRST] == 2, vector(gain_ref), vector(shift_ref),
                                group_table(x_ref.shape[1]), v_ref),
               patch_tables(lw_ref, lb_ref, table_ref, bias4_ref))


def second_norm(y_ref, kind, small):
    return norm_second_steps(y_ref, kind == 2, vector(small[3]), vector(small[4]), group_table(y_ref.shape[1]))


def patches(store, y_ref, kind, small, perm_ref):
    return to_patches_steps(store, y_ref, kind == 2, small[5], small[6][...], perm_ref[...])


def chain(*parts):
    for steps in parts:
        yield from steps


def count_live(kind_ref):
    total = jnp.int32(-2)
    for s in range(kind_ref.shape[1]):
        total = total + jnp.where(kind_ref[0, s] > 0, 1, 0).astype(jnp.int32)
    return total


def middle_kernel(offsets, state_ref, x_ref, w_ref, perm_ref, v_ref, *rest):
    names = 7
    small, rest = rest[:names], rest[names:]
    others, rest = rest[:len(offsets)], rest[len(offsets):]
    message_ref, sums_ref, _, *rest = rest
    early_ref, y_ref, v2_ref, *rest = rest
    kinds, ksem = rest[:-1], rest[-1]
    copies = [pltpu.make_async_copy(src, dst, ksem.at[i]) for i, (src, dst) in enumerate(zip(others, kinds))]
    for c in copies:
        c.start()
    cells = early_ref.shape[0]
    tokens = cells // 4
    feats = message_ref.shape[1] // 2
    slot = state_ref[1]

    def features_of(at):
        return x_ref.at[0, pl.ds(pl.multiple_of(at * cells, cells), cells), :]

    def first_norm(at, to_ref):
        return norm_first_steps(features_of(at), state_ref[2 + at] == 2, vector(small[0]), vector(small[1]),
                                group_table(x_ref.shape[2]), to_ref)

    found = {}

    def keep_as(name):
        def store(value):
            found[name] = value
        return store

    kind, early_kind = state_ref[2 + slot], state_ref[2 + FIRST]
    interleave(conv_steps(features_of(FIRST), vector(small[2]), w_ref, v_ref, early_ref),
               first_norm(slot, v2_ref))
    interleave(conv_steps(features_of(slot), vector(small[2]), w_ref, v2_ref, y_ref),
               second_norm(early_ref, early_kind, small))
    interleave(chain(second_norm(y_ref, kind, small), patches(keep_as("second"), y_ref, kind, small, perm_ref)),
               patches(keep_as("first"), early_ref, early_kind, small, perm_ref))
    first_is_last = state_ref[0] == 2
    last = jnp.where(first_is_last, found["first"], found["second"])
    before = jnp.where(first_is_last, found["second"], found["first"])
    message_ref[0:tokens, :] = jnp.concatenate([last, before], axis=1)

    for c in copies:
        c.wait()
    position = lax.axis_index("seq")
    mine = state_ref[0] - 2
    below, above = jnp.int32(0), mine
    for offset, kind_ref in zip(offsets, kinds):
        other = count_live(kind_ref)
        lower = (position ^ offset) < position
        below = below + jnp.where(lower, other, 0)
        above = above + jnp.where(lower, 0, other)
    first_half = position < lax.axis_size("seq") // 2
    passed = jnp.where(position % 2 == 0, mine, 0)
    sums_ref[0] = jnp.where(first_half, below, -above)
    told = jnp.where(first_half, below + passed, passed - above)
    message_ref[tokens:, :] = jnp.full((message_ref.shape[0] - tokens, 2 * feats), told.astype(F32)).astype(BF16)


def final_kernel(parts, state_ref, x_ref, w_ref, perm_ref, _, *rest):
    pieces, small, rest = rest[:parts], rest[parts:parts + 7], rest[parts + 7:]
    out_ref, embed_ref, y_ref, v_ref = rest
    group = lax.axis_index("dp")
    width = pieces[0].shape[1]

    def lay_out():
        for j in range(parts):
            value = pieces[0][...]
            for k in range(1, parts):
                value = jnp.where((group ^ j) == k, pieces[k][...], value)
            embed_ref[:, j * width:(j + 1) * width] = value
            yield

    @pl.when(state_ref[0] > 2)
    def _():
        def store(value):
            out_ref[...] = value

        x = x_ref.at[0, 0:y_ref.shape[0], :]
        norm = norm_first_steps(x, state_ref[2] == 2, vector(small[0]), vector(small[1]), group_table(y_ref.shape[1]), v_ref)
        for _ in range(6):
            next(norm)
        interleave(conv_steps(x, vector(small[2]), w_ref, v_ref, y_ref, by_half=True), norm, lay_out())
        drain(second_norm(y_ref, state_ref[2], small))
        drain(patches(store, y_ref, state_ref[2], small, perm_ref))

    @pl.when(state_ref[0] <= 2)
    def _():
        drain(lay_out())
        out_ref[...] = jnp.zeros_like(out_ref)


def join_kernel(state_ref, sums_ref, own_ref, third_ref, even_ref, odd_ref, embed_ref, out_ref, source_ref, value_ref, sem):
    live = state_ref[0]
    odd = lax.axis_index("seq") % 2
    tokens, feats = third_ref.shape
    told = even_ref[tokens:, :].astype(F32)[0, 0].astype(jnp.int32)
    carry = sums_ref[0] + told
    for k, ref in enumerate((even_ref, odd_ref, own_ref)):
        source_ref[2 * k] = ref[0:tokens, 0:feats]
        source_ref[2 * k + 1] = ref[0:tokens, feats:]
    source_ref[6] = third_ref[...]
    weight = embed_ref[0:feats, :]
    bias = embed_ref[feats:feats + 1, :].astype(F32)
    copies = []
    for i in range(2):
        incoming = (1 - odd) * 2 + carry - 1 - i
        kept = 4 + live - 1 - (i - carry)
        patch = source_ref[jnp.clip(jnp.where(i < carry, incoming, kept), 0, 6)]
        value = jnp.dot(patch, weight, preferred_element_type=F32) + bias
        rows = pl.ds(i * tokens, tokens)
        value_ref[rows, :] = value.astype(BF16)
        copies.append(pltpu.make_async_copy(value_ref.at[rows, :], out_ref.at[0, rows, :], sem.at[i]))
        copies[i].start()
    for c in copies:
        c.wait()


def exchange(value, axis, offset):
    count = lax.axis_size(axis)
    return lax.ppermute(value, axis, [(i, i ^ offset) for i in range(count)])


def swap_odd_pairs(value):
    groups, count = lax.axis_size("dp"), lax.axis_size("seq")
    pairs = []
    for g in range(groups):
        pairs += [(g * count + end, (g ^ 1) * count + end) for end in (0, count - 1)]
        for i in range(1, count - 1, 2):
            pairs += [(g * count + i, g * count + i + 1), (g * count + i + 1, g * count + i)]
    return lax.ppermute(value, ("dp", "seq"), pairs)


VMEM_SPEC = pl.BlockSpec(memory_space=pltpu.VMEM)
SMEM_SPEC = pl.BlockSpec(memory_space=pltpu.SMEM)
ANY_SPEC = pl.BlockSpec(memory_space=pl.ANY)
MIB = 1024 * 1024


def cost(flops, moved):
    return pl.CostEstimate(flops=flops, bytes_accessed=moved, transcendentals=0)


def encode_flops(cells, channels, lat):
    return cells * channels * 2 * 9 * (channels + lat)


def load(features, slot_kind, embed_weight, embed_bias, small):
    channels = features.shape[2]
    cells = SLOT_ROWS * SLOT_COLS
    feats, width = embed_weight.shape
    return pl.pallas_call(
        load_kernel,
        out_shape=[
            pltpu.SMEM((8,), jnp.int32),
            pltpu.VMEM((cells, channels), BF16),
            pltpu.VMEM((feats + 16, width), BF16),
        ] + [pltpu.VMEM(v.shape, v.dtype) for v in small],
        in_specs=[ANY_SPEC] * (4 + len(small)),
        out_specs=[SMEM_SPEC] + [VMEM_SPEC] * (2 + len(small)),
        scratch_shapes=[
            pltpu.SMEM(slot_kind.shape, jnp.int32),
            pltpu.VMEM(embed_weight.shape, BF16),
            pltpu.VMEM(embed_bias.shape, BF16),
            pltpu.SemaphoreType.DMA,
            pltpu.SemaphoreType.DMA,
            pltpu.SemaphoreType.DMA((len(small) + 2,)),
        ],
        compiler_params=pltpu.CompilerParams(vmem_limit_bytes=63 * MIB),
        cost_estimate=cost(0, features.size),
        name="load",
    )(slot_kind, features, embed_weight, embed_bias, *small)


def local(features, slot_kind, block_gain, block_shift, block_weight, block_bias, final_gain, final_shift,
          latent_weight, latent_bias, embed_weight, embed_bias):
    seq, dp = lax.axis_size("seq"), lax.axis_size("dp")
    channels = features.shape[2]
    cells = SLOT_ROWS * SLOT_COLS
    tokens = cells // 4
    feats, width = embed_weight.shape
    small = (block_gain, block_shift, block_bias, final_gain, final_shift, latent_weight.T, latent_bias)
    offsets = tuple(range(2, seq // 2, 2))
    others = [exchange(slot_kind, "seq", offset) for offset in offsets]
    slot_buffer = pltpu.VMEM((cells, channels), BF16)
    flops = encode_flops(cells, channels, latent_bias.shape[0])
    state, x, piece, *small = load(features, slot_kind, embed_weight, embed_bias, small)
    v_buffer = pltpu.VMEM((3, cells + 4 * SLOT_COLS, channels), BF16)
    v, table, bias4, perm, piece = pl.pallas_call(
        begin_kernel,
        out_shape=[v_buffer, pltpu.VMEM((channels, 3 * LANES), BF16), pltpu.VMEM((1, LANES), F32),
                   pltpu.VMEM((tokens, cells), BF16), pltpu.VMEM(piece.shape, BF16)],
        in_specs=[SMEM_SPEC] + [VMEM_SPEC] * 6,
        out_specs=[VMEM_SPEC] * 5,
        compiler_params=pltpu.CompilerParams(vmem_limit_bytes=16 * MIB),
        cost_estimate=cost(2 * flops, features.size),
        name="begin",
    )(state, x, *small[:2], *small[5:], piece)
    small = (*small[:5], table, bias4)
    message, sums, spare = pl.pallas_call(
        functools.partial(middle_kernel, offsets),
        out_shape=[jax.ShapeDtypeStruct((tokens + 16, 2 * feats), BF16), pltpu.SMEM((1,), jnp.int32), v_buffer],
        in_specs=[SMEM_SPEC] + [VMEM_SPEC] * (4 + len(small)) + [ANY_SPEC] * len(others),
        out_specs=[VMEM_SPEC, SMEM_SPEC, VMEM_SPEC],
        scratch_shapes=[slot_buffer] * 2 + [v_buffer] + [pltpu.SMEM(slot_kind.shape, jnp.int32) for _ in others]
        + [pltpu.SemaphoreType.DMA((len(others),))],
        compiler_params=pltpu.CompilerParams(vmem_limit_bytes=16 * MIB),
        cost_estimate=cost(flops, block_weight.size * 2),
        name="middle",
    )(state, features, block_weight, perm, v, *small, *others)
    even = exchange(message, "seq", 1)
    odd = swap_odd_pairs(message)
    pieces = [piece] + [exchange(piece, "dp", offset) for offset in range(1, dp)]
    third, embed = pl.pallas_call(
        functools.partial(final_kernel, dp),
        out_shape=[pltpu.VMEM((tokens, feats), BF16), pltpu.VMEM((feats + 16, dp * width), BF16)],
        in_specs=[SMEM_SPEC] + [VMEM_SPEC] * (4 + dp + len(small)),
        out_specs=[VMEM_SPEC] * 2,
        scratch_shapes=[slot_buffer, v_buffer],
        compiler_params=pltpu.CompilerParams(vmem_limit_bytes=16 * MIB),
        cost_estimate=cost(flops, block_weight.size * 2),
        name="final",
    )(state, features, block_weight, perm, spare, *pieces, *small)
    return pl.pallas_call(
        join_kernel,
        out_shape=jax.ShapeDtypeStruct((1, 2 * tokens, dp * width), BF16),
        in_specs=[SMEM_SPEC] * 2 + [VMEM_SPEC] * 5,
        out_specs=ANY_SPEC,
        scratch_shapes=[pltpu.VMEM((7, tokens, feats), BF16), pltpu.VMEM((2 * tokens, dp * width), BF16),
                        pltpu.SemaphoreType.DMA((2,))],
        compiler_params=pltpu.CompilerParams(vmem_limit_bytes=8 * MIB),
        cost_estimate=cost(4 * tokens * feats * dp * width, 4 * tokens * dp * width),
        name="join",
    )(state, sums, message, third, even, odd, embed)


def solution(mesh):
    in_specs = (P("dp", "seq", None), P("dp", "seq")) + (P(),) * 8 + (P(None, "dp"), P("dp"))
    return jax.shard_map(local, mesh=mesh, in_specs=in_specs, out_specs=P("dp", "seq", None), check_vma=False)
```
